32 devices in a mesh: seq: 8 (over z, x), fsdp: 4 (over y, core).
Axes of the slice: x: 2, y: 2, z: 4, core: 2. Of those that a mesh axis runs over, the one named last changes fastest.
Arguments:
- hidden: bfloat16 [4, 1024, 2048], P('fsdp', 'seq'), may hold values from -6 to 6
- lengths: int32 [4], P('fsdp'), may hold values from 512 to 1024, as said below
- adapter_ids: int32 [4], P('fsdp'), may hold values from 0 to 7
- norm_gain: bfloat16 [2048], replicated, may hold values from 0.5 to 1.5
- in_proj_x: bfloat16 [2048, 4096], P(('seq', 'fsdp')), may hold values from -0.125 to 0.125
- in_proj_z: bfloat16 [2048, 4096], P(('seq', 'fsdp')), may hold values from -0.125 to 0.125
- conv_weight: bfloat16 [4, 4096], P(None, 'seq'), may hold values from -3 to 3
- conv_bias: bfloat16 [4096], P('seq'), may hold values from -3 to 3
- state_proj: bfloat16 [4096, 160], P('seq'), may hold values from -0.09375 to 0.09375
- step_proj: bfloat16 [128, 4096], P(None, 'seq'), may hold values from -0.5 to 0.5
- step_bias: bfloat16 [4096], P('seq'), may hold values from -6.5 to -2.5
- decay_log: bfloat16 [16, 4096], P(None, 'seq'), may hold values from 0 to 2.796875
- skip_gain: bfloat16 [4096], P('seq'), may hold values from 0.5 to 1.5
- out_proj: bfloat16 [4096, 2048], P(('seq', 'fsdp')), may hold values from -0.375 to 0.375
- in_down: bfloat16 [8, 2048, 16], replicated, may hold values from -0.125 to 0.125
- in_up: bfloat16 [8, 16, 8192], replicated, may hold values from -0.75 to 0.75
- state_down: bfloat16 [8, 4096, 16], P(None, 'seq'), may hold values from -0.09375 to 0.09375
- state_up: bfloat16 [8, 16, 160], replicated, may hold values from -0.75 to 0.75
- step_down: bfloat16 [8, 128, 16], replicated, may hold values from -0.5 to 0.5
- step_up: bfloat16 [8, 16, 4096], P(None, None, 'seq'), may hold values from -0.75 to 0.75
- out_down: bfloat16 [8, 4096, 16], replicated, may hold values from -0.09375 to 0.09375
- out_up: bfloat16 [8, 16, 2048], replicated, may hold values from -1.5 to 1.5
- cotangent: bfloat16 [4, 1024, 2048], P('fsdp', 'seq'), may hold values from -6 to 6
Outputs:
- block_out: bfloat16 [4, 1024, 2048], P('fsdp', 'seq')
- input_grad: float32 [4, 1024, 2048], P('fsdp', 'seq')
- in_down_grad: float32 [8, 2048, 16], replicated
- in_up_grad: float32 [8, 16, 8192], replicated
- state_down_grad: float32 [8, 4096, 16], P(None, 'seq')
- state_up_grad: float32 [8, 16, 160], replicated
- step_down_grad: float32 [8, 128, 16], replicated
- step_up_grad: float32 [8, 16, 4096], P(None, None, 'seq')
- out_down_grad: float32 [8, 4096, 16], replicated
- out_up_grad: float32 [8, 16, 2048], replicated
The draws below stay inside these ranges and needn't reach their ends.
Inputs may be any that keep to these rules, and one draw needn't show every extreme that they name: Positions from lengths[b] on are padding; one sequence has all 1024 positions valid and one has 512.
All inputs are finite; a program needn't handle non-finite values.
Results may differ from the reference program's by a relative error of at most 0.015.
The reference program's roundings to bfloat16 on the way count: a program that leaves them out, or rounds other values in their place, can miss the bound.
Values may be sent and summed in bfloat16 or wider, within the bound.
No kernel may reach another device: no remote copies, remote signals or barrier semaphores. Data moves between devices by JAX's collectives and lax.ppermute only.
A program may use at most 256 MiB of HBM per device.

```python
import jax
import jax.numpy as jnp
from jax import lax

D = 2048
DI = 4096
NST = 16
RK = 128
KC = 4
RANK = 16
ADAPTERS = 8
LEN = 1024
SEQS = 4


def draw_lengths(key, part):
    key = jax.random.fold_in(key, 7)
    left_key, right_key = jax.random.split(key)
    spread = jax.random.randint(left_key, (SEQS,), LEN // 2, LEN + 1)
    ranking = jax.random.permutation(right_key, SEQS)
    spread = jnp.where(ranking == 0, LEN, spread)
    spread = jnp.where(ranking == 1, LEN // 2, spread)
    return spread.astype(jnp.int32)


def set_ends(values, stream_key, smallest, largest):
    shape = values.shape
    place = [jax.random.randint(jax.random.fold_in(stream_key, axis), (), 0, shape[axis]) for axis in range(len(shape))]
    values = values.at[tuple(place)].set(smallest)
    longest = shape.index(max(shape))
    place[longest] = (place[longest] + 1) % shape[longest]
    return values.at[tuple(place)].set(largest)


def level_of(rng, dims, cuts, smallest, largest):
    gain = 1.0
    for position, parts in cuts:
        heights = jax.random.uniform(jax.random.fold_in(jax.random.fold_in(rng, 6), position), (parts,), jnp.float32, smallest / len(cuts), largest / len(cuts))
        gain = gain * jnp.repeat(jnp.exp(heights), dims[position] // parts).reshape((-1,) + (1,) * (len(dims) - 1 - position))
    return gain


def noise(stream_key, extent, scale, most, shards=(), kind=jnp.bfloat16):
    level = level_of(stream_key, extent, shards, -0.22, 0.18) if shards else 1.0
    drawn = jax.random.normal(stream_key, extent, jnp.float32) * scale * level
    return jnp.minimum(jnp.maximum(drawn, -most), most).astype(kind)


def setup_inputs(seed: int = 0) -> dict:
    streams_of = jax.random.split(jax.random.key(seed), 24)
    hidden = noise(streams_of[0], (SEQS, LEN, D), 1.0, 6.0, ((0, 4), (1, 8)))
    lengths = draw_lengths(jax.random.fold_in(streams_of[23], 71), 0)
    adapter_ids = set_ends(jax.random.randint(streams_of[2], (SEQS,), 0, ADAPTERS), jax.random.fold_in(streams_of[2], 1), 0, ADAPTERS - 1).astype(jnp.int32)
    norm_gain = jnp.clip(1.0 + 0.1 * jax.random.normal(streams_of[3], (D,), jnp.float32), 0.5, 1.5).astype(jnp.bfloat16)
    in_proj_x = noise(streams_of[4], (D, DI), D ** -0.5, 0.125, ((0, 32),))
    in_proj_z = noise(streams_of[5], (D, DI), D ** -0.5, 0.125, ((0, 32),))
    conv_weight = noise(streams_of[6], (KC, DI), KC ** -0.5, 3.0, ((1, 8),))
    conv_bias = noise(streams_of[7], (DI,), 0.5, 3.0, ((0, 8),))
    state_proj = noise(streams_of[8], (DI, RK + 2 * NST), DI ** -0.5, 0.09375, ((0, 8),))
    step_proj = noise(streams_of[9], (RK, DI), RK ** -0.5, 0.5, ((1, 8),))
    step_bias = jnp.clip(-6.5 + 4.0 * jax.random.uniform(streams_of[10], (DI,), jnp.float32) ** level_of(streams_of[10], (DI,), ((0, 8),), -0.2, 0.2), -6.5, -2.5).astype(jnp.bfloat16)
    decay_log = jnp.clip(2.796875 * jax.random.uniform(streams_of[11], (NST, DI), jnp.float32) ** level_of(streams_of[11], (NST, DI), ((1, 8),), -0.2, 0.2), 0.0, 2.796875).astype(jnp.bfloat16)
    skip_gain = jnp.clip(0.5 + 1.0 * jax.random.uniform(streams_of[12], (DI,), jnp.float32) ** level_of(streams_of[12], (DI,), ((0, 8),), -0.2, 0.2), 0.5, 1.5).astype(jnp.bfloat16)
    out_proj = noise(streams_of[13], (DI, D), (DI // 16) ** -0.5, 0.375, ((0, 32),))
    in_down = noise(streams_of[14], (ADAPTERS, D, RANK), D ** -0.5, 0.125)
    in_up = noise(streams_of[15], (ADAPTERS, RANK, 2 * DI), (4 * RANK) ** -0.5, 0.75)
    state_down = noise(streams_of[16], (ADAPTERS, DI, RANK), DI ** -0.5, 0.09375, ((1, 8),))
    state_up = noise(streams_of[17], (ADAPTERS, RANK, RK + 2 * NST), (4 * RANK) ** -0.5, 0.75)
    step_down = noise(streams_of[18], (ADAPTERS, RK, RANK), RK ** -0.5, 0.5)
    step_up = noise(streams_of[19], (ADAPTERS, RANK, DI), (4 * RANK) ** -0.5, 0.75, ((2, 8),))
    out_down = noise(streams_of[20], (ADAPTERS, DI, RANK), DI ** -0.5, 0.09375)
    out_up = noise(streams_of[21], (ADAPTERS, RANK, D), RANK ** -0.5, 1.5)
    cotangent = noise(streams_of[22], (SEQS, LEN, D), 1.0, 6.0, ((0, 4), (1, 8)))
    return dict(hidden=hidden, lengths=lengths, adapter_ids=adapter_ids, norm_gain=norm_gain, in_proj_x=in_proj_x, in_proj_z=in_proj_z, conv_weight=conv_weight, conv_bias=conv_bias, state_proj=state_proj, step_proj=step_proj, step_bias=step_bias, decay_log=decay_log, skip_gain=skip_gain, out_proj=out_proj, in_down=in_down, in_up=in_up, state_down=state_down, state_up=state_up, step_down=step_down, step_up=step_up, out_down=out_down, out_up=out_up, cotangent=cotangent)


EPS = 1e-05
PRECISE = lax.Precision.HIGHEST

@jax.custom_vjp
def low(v):
    return lax.optimization_barrier(v.astype(jnp.bfloat16)).astype(jnp.float32)

@jax.custom_vjp
def low_back(v):
    return v

def low_keep(v):
    return (low(v), None)

def low_pass(kept, grad):
    return (grad,)

def back_keep(v):
    return (v, None)

def back_low(kept, grad):
    return (low(grad),)
low.defvjp(low_keep, low_pass)
low_back.defvjp(back_keep, back_low)

def product(left, right):
    return jnp.dot(left, right, precision=PRECISE, preferred_element_type=left.dtype)

def selective_scan(delta, inputs, b_rows, c_rows, decay):
    width = min(256, LEN)

    def advance(carry, item):
        step_delta, step_input, step_b, step_c = item
        carry = jnp.exp(step_delta[:, None] * decay) * carry + (step_delta * step_input)[:, None] * step_b[None, :]
        return (carry, jnp.dot(carry, step_c, precision=PRECISE))

    @jax.checkpoint
    def run_block(carry, items):
        return lax.scan(advance, carry, items)
    shaped = tuple((v.reshape((LEN // width, width) + v.shape[1:]) for v in (delta, inputs, b_rows, c_rows)))
    start = jnp.zeros((DI, NST), delta.dtype)
    final, outputs = lax.scan(run_block, start, shaped)
    return outputs.reshape(LEN, DI)

def mixer(rows, length, ident, frozen, adapters):
    norm_gain, in_proj_x, in_proj_z, conv_weight, conv_bias, state_proj, step_proj, step_bias, decay_log, skip_gain, out_proj = frozen
    in_down, in_up, state_down, state_up, step_down, step_up, out_down, out_up = adapters
    onehot = (jnp.arange(ADAPTERS, dtype=jnp.int32) == ident).astype(rows.dtype)

    def choose(table):
        return jnp.tensordot(onehot, table, axes=1, precision=PRECISE)
    inverse = lax.rsqrt(lax.optimization_barrier(jnp.mean(rows * rows, axis=-1, keepdims=True)) + EPS)
    normed = low(rows * inverse * norm_gain)
    up_table = choose(in_up)
    low_in = low(low_back(product(normed, choose(in_down))))
    proj_x = low(low_back(product(normed, in_proj_x) + product(low_in, up_table[:, :DI])))
    proj_z = low(low_back(product(normed, in_proj_z) + product(low_in, up_table[:, DI:])))
    padded = jnp.concatenate([jnp.zeros((KC - 1, DI), rows.dtype), proj_x], axis=0)
    conv_pre = conv_bias + jnp.zeros((LEN, DI), rows.dtype)
    for tap in range(KC):
        conv_pre = conv_pre + conv_weight[tap] * padded[tap:tap + LEN]
    conv_out = low(jax.nn.silu(conv_pre))
    low_state = low(low_back(product(conv_out, choose(state_down))))
    mixed = low_back(product(conv_out, state_proj) + product(low_state, choose(state_up)))
    step_low = low(mixed[:, :RK])
    b_rows = mixed[:, RK:RK + NST]
    c_rows = mixed[:, RK + NST:]
    step_mid = low(product(step_low, choose(step_down)))
    step_pre = low_back(product(step_low, step_proj) + product(step_mid, choose(step_up)) + step_bias)
    delta = jax.nn.softplus(step_pre)
    decay = -jnp.exp(decay_log).T
    scanned = selective_scan(delta, conv_out, b_rows, c_rows, decay) + skip_gain * conv_out
    gated = low(low_back(scanned * jax.nn.silu(proj_z)))
    low_out = low(low_back(product(gated, choose(out_down))))
    branch = product(gated, out_proj) + product(low_out, choose(out_up))
    valid = (jnp.arange(LEN, dtype=jnp.int32) < length).astype(rows.dtype)
    return rows + valid[:, None] * branch

def reference(hidden, lengths, adapter_ids, norm_gain, in_proj_x, in_proj_z, conv_weight, conv_bias, state_proj, step_proj, step_bias, decay_log, skip_gain, out_proj, in_down, in_up, state_down, state_up, step_down, step_up, out_down, out_up, cotangent):
    frozen = tuple((w.astype(jnp.float32) for w in (norm_gain, in_proj_x, in_proj_z, conv_weight, conv_bias, state_proj, step_proj, step_bias, decay_log, skip_gain, out_proj)))
    adapters = tuple((w.astype(jnp.float32) for w in (in_down, in_up, state_down, state_up, step_down, step_up, out_down, out_up)))

    def forward(hidden_f, adapter_set):

        def one_sequence(item):
            rows, length, ident = item
            return mixer(rows, length, ident, frozen, adapter_set)
        return lax.map(jax.checkpoint(one_sequence), (hidden_f, lengths, adapter_ids))
    result, pullback = jax.vjp(forward, hidden.astype(jnp.float32), adapters)
    input_grad, grads = pullback(cotangent.astype(jnp.float32))
    return (result.astype(jnp.bfloat16), input_grad, grads[0], grads[1], grads[2], grads[3], grads[4], grads[5], grads[6], grads[7])
```

```python
import functools
import jax
import jax.numpy as jnp
from jax import lax
from jax.experimental import pallas as pl
from jax.experimental.pallas import tpu as pltpu
from jax.sharding import PartitionSpec as P

F32 = jnp.float32
BF16 = jnp.bfloat16
LOG2E = 1.4426950408889634


def silu_grad(values):
    sigma = jax.nn.sigmoid(values)
    return sigma * (1.0 + values * (1.0 - sigma))


def softplus(v):
    return jnp.maximum(v, 0.0) + jnp.log1p(jnp.exp(-jnp.abs(v)))


def nt(left, right):
    return lax.dot_general(left, right, (((1,), (1,)), ((), ())), preferred_element_type=F32)


def nn(left, right):
    return jnp.dot(left, right, preferred_element_type=F32)


def spread_matrix(states, sub):
    row = lax.broadcasted_iota(jnp.int32, (states, sub * states), 0)
    col = lax.broadcasted_iota(jnp.int32, (states, sub * states), 1)
    return (lax.rem(col, states) == row).astype(BF16)


def own_step_mask(rows, states, sub):
    row = lax.broadcasted_iota(jnp.int32, (rows, sub * states), 0)
    col = lax.broadcasted_iota(jnp.int32, (rows, sub * states), 1)
    return (lax.rem(row, sub) == lax.div(col, states)).astype(F32)


def scan_forward_kernel(
    low_ref, wstep_ref, bias_ref, bt_ref, c_ref, u_ref, z_ref, decay_ref, skip_ref,
    gated_ref, scanned_ref, states_ref,
    carry, delta_s, du_s, cm_s, *, sub,
):
    rows = u_ref.shape[0]
    states = decay_ref.shape[0]

    @pl.when(pl.program_id(0) == 0)
    def _():
        carry[...] = jnp.zeros_like(carry)

    pre = nn(low_ref[...], wstep_ref[...]) + bias_ref[...]
    delta = softplus(pre)
    u = u_ref[...].astype(F32)
    delta_s[...] = delta
    du_s[...] = delta * u
    cm_s[...] = (nn(c_ref[...], spread_matrix(states, sub)) * own_step_mask(rows, states, sub)).astype(BF16)
    rate = decay_ref[...] * LOG2E

    def group(k, s):
        base = pl.multiple_of(k * sub, sub)
        bt = bt_ref[k]
        for t in range(sub):
            dl = delta_s[pl.ds(base + t, 1), :]
            du = du_s[pl.ds(base + t, 1), :]
            s = jnp.exp2(dl * rate) * s + du * bt[:, t : t + 1]
            states_ref[pl.ds(pl.multiple_of((base + t) * states, states), states), :] = s.astype(BF16)
        scanned_ref[pl.ds(base, sub), :] = nn(
            cm_s[pl.ds(base, sub), :],
            states_ref[pl.ds(pl.multiple_of(base * states, sub * states), sub * states), :],
        )
        return s

    carry[...] = lax.fori_loop(0, rows // sub, group, carry[...])
    scanned = scanned_ref[...] + skip_ref[...] * u
    scanned_ref[...] = scanned
    gated_ref[...] = (scanned * jax.nn.silu(z_ref[...].astype(F32))).astype(BF16)


def scan_forward(low, wstep, bias, bt, c, u, z, decay, skip, block=128):
    length, chans = u.shape
    states = decay.shape[0]
    sub = bt.shape[2]
    block = min(block, length)
    seq = lambda cols: pl.BlockSpec((block, cols), lambda i: (i, 0))
    whole = lambda a: pl.BlockSpec(a.shape, lambda i: (0,) * a.ndim)
    return pl.pallas_call(
        functools.partial(scan_forward_kernel, sub=sub),
        grid=(length // block,),
        in_specs=[
            seq(low.shape[1]), whole(wstep), whole(bias),
            pl.BlockSpec((block // sub, states, sub), lambda i: (i, 0, 0)),
            seq(states), seq(chans), seq(chans), whole(decay), whole(skip),
        ],
        out_specs=[seq(chans), seq(chans), pl.BlockSpec((block * states, chans), lambda i: (i, 0))],
        out_shape=[
            jax.ShapeDtypeStruct((length, chans), BF16),
            jax.ShapeDtypeStruct((length, chans), F32),
            jax.ShapeDtypeStruct((length * states, chans), BF16),
        ],
        scratch_shapes=[
            pltpu.VMEM((states, chans), F32),
            pltpu.VMEM((block, chans), F32),
            pltpu.VMEM((block, chans), F32),
            pltpu.VMEM((block, sub * states), BF16),
        ],
        compiler_params=pltpu.CompilerParams(vmem_limit_bytes=40 << 20),
        name="scan_forward",
    )(low, wstep, bias, bt, c, u, z, decay, skip)


def scan_backward_kernel(
    low_ref, wstep_ref, bias_ref, ct_ref, b_ref, u_ref, z_ref, scanned_ref, bg_ref, states_ref, before_ref,
    decay_ref, skip_ref,
    pre_ref, conv_ref, bz_ref, mixed_ref,
    carry, delta_s, du_s, bs_s, bm_s, g_s, q_s, w_s, bd_s, r1_s, r2_s, *, sub,
):
    rows = u_ref.shape[0]
    states = decay_ref.shape[0]
    step = pl.program_id(0)
    first = step == pl.num_programs(0) - 1

    @pl.when(step == 0)
    def _():
        carry[...] = jnp.zeros_like(carry)

    pre = nn(low_ref[...], wstep_ref[...]) + bias_ref[...]
    delta = softplus(pre)
    u = u_ref[...].astype(F32)
    z = z_ref[...].astype(F32)
    bg = bg_ref[...].astype(F32)
    sigma = jax.nn.sigmoid(z)
    bs_s[...] = bg * (z * sigma)
    bz_ref[...] = (bg * scanned_ref[...] * (sigma * (1.0 + z * (1.0 - sigma)))).astype(BF16)
    delta_s[...] = delta
    du_s[...] = delta * u
    mask = own_step_mask(rows, states, sub)
    bm_s[...] = (nn(b_ref[...], spread_matrix(states, sub)) * mask).astype(BF16)
    ones = own_step_mask(sub, states, sub).astype(BF16)
    decay = decay_ref[...]
    rate = decay * LOG2E
    groups = rows // sub

    def group(i, h):
        k = groups - 1 - i
        base = pl.multiple_of(k * sub, sub)
        ct = ct_ref[k]
        for t in range(sub - 1, -1, -1):
            dl = delta_s[pl.ds(base + t, 1), :]
            bs = bs_s[pl.ds(base + t, 1), :]
            g = bs * ct[:, t : t + 1] + h
            h = g * jnp.exp2(dl * rate)
            if t:
                sp = states_ref[pl.ds(pl.multiple_of((base + t - 1) * states, states), states), :].astype(F32)
            else:
                at = pl.multiple_of(jnp.maximum(base - 1, 0) * states, states)
                inside = states_ref[pl.ds(at, states), :].astype(F32)
                sp = jnp.where(k > 0, inside, jnp.where(first, 0.0, before_ref[...].astype(F32)))
            g_s[t * states : (t + 1) * states, :] = g.astype(BF16)
            q_s[t * states : (t + 1) * states, :] = (h * decay * sp).astype(BF16)
        bd_s[pl.ds(base, sub), :] = nn(ones, q_s[...])
        w_s[pl.ds(base, sub), :] = nn(bm_s[pl.ds(base, sub), :], g_s[...])
        r1_s[pl.ds(base, sub), :] = nt(du_s[pl.ds(base, sub), :].astype(BF16), g_s[...])
        r2_s[pl.ds(base, sub), :] = nt(
            bs_s[pl.ds(base, sub), :].astype(BF16),
            states_ref[pl.ds(pl.multiple_of(base * states, sub * states), sub * states), :],
        )
        return h

    carry[...] = lax.fori_loop(0, groups, group, carry[...])
    w = w_s[...]
    conv_ref[...] = w * delta + skip_ref[...] * bs_s[...]
    back_pre = ((bd_s[...] + w * u) * jax.nn.sigmoid(pre)).astype(BF16)
    pre_ref[...] = back_pre
    fold = spread_matrix(states, sub)
    back_low = nt(back_pre, wstep_ref[...])
    ranks = back_low.shape[1] - states
    back_b = nt((r1_s[...] * mask).astype(BF16), fold)
    back_c = nt((r2_s[...] * mask).astype(BF16), fold)
    mixed_ref[...] = jnp.concatenate([back_low, back_b, back_c], axis=1)


def scan_backward(low, wstep, bias, ct, b, u, z, scanned, bg, kept, decay, skip, block=128):
    length, chans = u.shape
    states = decay.shape[0]
    sub = ct.shape[2]
    block = min(block, length)
    last = length // block - 1
    seq = lambda cols: pl.BlockSpec((block, cols), lambda i: (last - i, 0))
    whole = lambda a: pl.BlockSpec(a.shape, lambda i: (0,) * a.ndim)
    cols = low.shape[1] + 2 * states
    return pl.pallas_call(
        functools.partial(scan_backward_kernel, sub=sub),
        grid=(last + 1,),
        in_specs=[
            seq(low.shape[1]), whole(wstep), whole(bias),
            pl.BlockSpec((block // sub, states, sub), lambda i: (last - i, 0, 0)),
            seq(states), seq(chans), seq(chans), seq(chans), seq(chans),
            pl.BlockSpec((block * states, chans), lambda i: (last - i, 0)),
            pl.BlockSpec((states, chans), lambda i: (jnp.maximum((last - i) * block - 1, 0), 0)),
            whole(decay), whole(skip),
        ],
        out_specs=[seq(chans), seq(chans), seq(chans), seq(cols)],
        out_shape=[
            jax.ShapeDtypeStruct((length, chans), BF16),
            jax.ShapeDtypeStruct((length, chans), F32),
            jax.ShapeDtypeStruct((length, chans), BF16),
            jax.ShapeDtypeStruct((length, cols), F32),
        ],
        scratch_shapes=[
            pltpu.VMEM((states, chans), F32),
            pltpu.VMEM((block, chans), F32),
            pltpu.VMEM((block, chans), F32),
            pltpu.VMEM((block, chans), F32),
            pltpu.VMEM((block, sub * states), BF16),
            pltpu.VMEM((sub * states, chans), BF16),
            pltpu.VMEM((sub * states, chans), BF16),
            pltpu.VMEM((block, chans), F32),
            pltpu.VMEM((block, chans), F32),
            pltpu.VMEM((block, sub * states), F32),
            pltpu.VMEM((block, sub * states), F32),
        ],
        compiler_params=pltpu.CompilerParams(vmem_limit_bytes=40 << 20),
        name="scan_backward",
    )(low, wstep, bias, ct, b, u, z, scanned, bg, kept, kept, decay, skip)


EPS = 1e-05


def ring_order(size):
    return list(range(0, size, 2)) + list(range(1, size, 2))[::-1]


def ring_place(size, offset, axis):
    order = ring_order(size)
    position = {place: i for i, place in enumerate(order)}
    table = [order[(position[i] + offset) % size] for i in range(size)]
    return jnp.asarray(table, jnp.int32)[lax.axis_index(axis)]


def ring_send(value, size, hop, axis):
    order = ring_order(size)
    pairs = [(order[i], order[(i + hop) % size]) for i in range(size)]
    return lax.ppermute(value, axis, pairs)


def ring_gather(own, size, axis):
    rows = own.shape[0]
    half = rows // 2
    pieces = [(0, 0, own)]
    ahead = back = own
    for step in range(1, size // 2):
        ahead, back = ring_send(ahead, size, 1, axis), ring_send(back, size, -1, axis)
        pieces += [(-step, 0, ahead), (step, 0, back)]
    far = size // 2
    pieces += [
        (-far, 0, ring_send(ahead[:half], size, 1, axis)),
        (far, half, ring_send(back[half:], size, -1, axis)),
    ]
    out = jnp.zeros((size * rows,) + own.shape[1:], own.dtype)
    for offset, start, piece in pieces:
        at = ring_place(size, offset, axis) * rows + start
        out = lax.dynamic_update_slice_in_dim(out, piece, at, 0)
    return out


def ring_scatter(partial, size, axis):
    rows = partial.shape[0] // size
    half = rows // 2

    def block(offset):
        at = ring_place(size, offset, axis) * rows
        return lax.dynamic_slice_in_dim(partial, at, rows, 0).astype(F32)

    far = size // 2
    ahead = ring_send(block(far)[:half].astype(BF16), size, 1, axis)
    back = ring_send(block(far)[half:].astype(BF16), size, -1, axis)
    for left in range(far - 1, 0, -1):
        mine, other = block(left), block(-left)
        if left == far - 1:
            mine = mine.at[:half].add(ahead.astype(F32))
            other = other.at[half:].add(back.astype(F32))
        else:
            mine, other = mine + ahead.astype(F32), other + back.astype(F32)
        ahead = ring_send(mine.astype(BF16), size, 1, axis)
        back = ring_send(other.astype(BF16), size, -1, axis)
    return block(0) + ahead.astype(F32) + back.astype(F32)


def swap(value, size, bit, axis):
    return lax.ppermute(value, axis, [(i, i ^ bit) for i in range(size)])


def bits_of(size):
    bit = size // 2
    while bit:
        yield bit
        bit //= 2


def swap_gather(own, size, axis):
    place = lax.axis_index(axis)
    held = [(place, own)]
    for bit in bits_of(size):
        held += [(at ^ bit, swap(block, size, bit, axis)) for at, block in held]
    return held


def small_gather(own, size, axis):
    place = lax.axis_index(axis)
    held = own[None]
    for bit in bits_of(size):
        got = swap(held, size, bit, axis)
        low = (place & bit) == 0
        held = jnp.where(low, jnp.stack([held, got]), jnp.stack([got, held]))
        held = held.reshape((-1,) + own.shape)
    count = len(list(bits_of(size)))
    dims = held.reshape((2,) * count + own.shape)
    order = tuple(range(count))[::-1] + tuple(range(count, dims.ndim))
    return dims.transpose(order).reshape((size * own.shape[0],) + own.shape[1:])


def small_scatter(partial, size, axis):
    got = lax.all_to_all(partial, axis, split_axis=0, concat_axis=0, tiled=True)
    return got.reshape((size, -1) + partial.shape[1:]).astype(F32).sum(0)


def shift_down(values, count):
    if not count:
        return values
    return jnp.concatenate([jnp.zeros((count, values.shape[1]), values.dtype), values[:-count]], 0)


def shift_up(values, count):
    if not count:
        return values
    return jnp.concatenate([values[count:], jnp.zeros((count, values.shape[1]), values.dtype)], 0)


def tn(left, right):
    return lax.dot_general(left, right, (((0,), (0,)), ((), ())), preferred_element_type=F32)


def body(
    hidden, lengths, adapter_ids, norm_gain, in_proj_x, in_proj_z, conv_weight, conv_bias, state_proj,
    step_proj, step_bias, decay_log, skip_gain, out_proj, in_down, in_up, state_down, state_up, step_down,
    step_up, out_down, out_up, cotangent,
):
    parts, groups = lax.axis_size("seq"), lax.axis_size("fsdp")
    part, group = lax.axis_index("seq"), lax.axis_index("fsdp")
    tokens, width = hidden.shape[1:]
    taps, chans = conv_weight.shape
    inner = out_down.shape[1]
    ranks = step_proj.shape[0]
    states = decay_log.shape[0]
    rank = in_down.shape[2]
    adapters = in_down.shape[0]
    ident = adapter_ids[0]
    sub = 16

    def pick(table):
        return lax.dynamic_index_in_dim(table, ident, 0, keepdims=False)

    hidden_f = hidden[0].astype(F32)
    gain_f = norm_gain.astype(F32)
    inverse = lax.rsqrt(jnp.mean(hidden_f * hidden_f, axis=-1, keepdims=True) + EPS)
    normed = (hidden_f * inverse * gain_f).astype(BF16)
    positions = part * tokens + lax.broadcasted_iota(jnp.int32, (tokens, 1), 0)
    valid = (positions < lengths[0]).astype(F32)
    cot_f = cotangent[0].astype(F32)
    back_out = (valid * cot_f).astype(BF16)

    def columns(weight):
        rows = weight.shape[0]
        mine = lax.all_to_all(weight, "seq", split_axis=1, concat_axis=0, tiled=True)
        out = jnp.zeros((parts, groups, rows, chans), weight.dtype)
        for at, block in swap_gather(mine.reshape(parts, 1, rows, chans), groups, "fsdp"):
            out = lax.dynamic_update_slice(out, block, (0, at, 0, 0))
        return out.reshape(parts * groups * rows, chans)

    def columns_later(weight):
        rows = weight.shape[0]
        mine = lax.all_to_all(weight, "seq", split_axis=1, concat_axis=0, tiled=True)
        out = lax.all_gather(mine, "fsdp").reshape(groups, parts, rows, chans)
        return out.transpose(1, 0, 2, 3).reshape(parts * groups * rows, chans)

    back_out_all = lax.all_gather(back_out, "seq", axis=0, tiled=True)
    whole_x = columns(in_proj_x)
    normed_all = ring_gather(normed, parts, "seq")
    whole_z = columns_later(in_proj_z)
    whole_out = lax.all_gather(out_proj, "fsdp", axis=0, tiled=True)

    in_down_sel = pick(in_down)
    up_x = lax.dynamic_slice(in_up, (ident, 0, part * chans), (1, rank, chans))[0]
    up_z = lax.dynamic_slice(in_up, (ident, 0, inner + part * chans), (1, rank, chans))[0]
    out_down_sel = lax.dynamic_slice(out_down, (ident, part * chans, 0), (1, chans, rank))[0]
    state_down_sel, state_up_sel = pick(state_down), pick(state_up)
    step_down_sel, step_up_sel = pick(step_down), pick(step_up)
    out_up_sel = pick(out_up)

    low_in = nn(normed_all, in_down_sel).astype(BF16)
    x = (nn(normed_all, whole_x) + nn(low_in, up_x)).astype(BF16)
    z = (nn(normed_all, whole_z) + nn(low_in, up_z)).astype(BF16)
    kernel = conv_weight.astype(F32)
    x_f = x.astype(F32)
    conv_pre = conv_bias.astype(F32)
    for tap in range(taps):
        conv_pre = conv_pre + kernel[tap] * shift_down(x_f, taps - 1 - tap)
    conv_out = jax.nn.silu(conv_pre).astype(BF16)
    state_all = jnp.concatenate([state_proj, state_down_sel], 1)
    sums = small_scatter(nn(conv_out, state_all).astype(BF16), parts, "seq")
    low_state_own = sums[:, ranks + 2 * states :].astype(BF16)
    mixed = sums[:, : ranks + 2 * states] + nn(low_state_own, state_up_sel)
    step_low_own = mixed[:, :ranks].astype(BF16)
    step_mid_own = nn(step_low_own, step_down_sel).astype(BF16)
    shared = jnp.concatenate([step_low_own, step_mid_own, mixed[:, ranks:].astype(BF16), low_state_own], 1)
    shared = small_gather(shared, parts, "seq")
    cuts = (ranks, ranks + rank, ranks + rank + states, ranks + rank + 2 * states)
    low, low_state = shared[:, : cuts[1]], shared[:, cuts[3] :]
    b_rows, c_rows = shared[:, cuts[1] : cuts[2]], shared[:, cuts[2] : cuts[3]]

    def by_group(rows):
        return rows.reshape(-1, sub, states).transpose(0, 2, 1).astype(F32)

    step_all = jnp.concatenate([step_proj, step_up_sel], 0)
    bias_f = step_bias.astype(F32)[None]
    skip_f = skip_gain.astype(F32)[None]
    decay = -jnp.exp(decay_log.astype(F32))
    gated, scanned, kept = scan_forward(
        low, step_all, bias_f, by_group(b_rows), c_rows, conv_out, z, decay, skip_f
    )
    branch = lax.psum_scatter(nn(gated, whole_out).astype(BF16), "seq", scatter_dimension=0, tiled=True).astype(F32)
    low_out_part = nn(gated, out_down_sel)

    back_low_out = nt(back_out_all, out_up_sel).astype(BF16)
    back_gated = (nt(back_out_all, whole_out) + nt(back_low_out, out_down_sel)).astype(BF16)
    back_pre, back_conv, back_z, mixed_part = scan_backward(
        low, step_all, bias_f, by_group(c_rows), b_rows, conv_out, z, scanned, back_gated, kept, decay, skip_f
    )
    sums = small_scatter(jnp.concatenate([mixed_part, low_out_part], 1).astype(BF16), parts, "seq")
    back_mid_own = sums[:, ranks : ranks + rank]
    back_step = sums[:, :ranks] + nt(back_mid_own, step_down_sel.astype(F32))
    low_out_own = sums[:, cuts[3] :].astype(BF16)
    shared = jnp.concatenate(
        [back_step.astype(BF16), sums[:, cuts[1] : cuts[3]].astype(BF16), back_mid_own.astype(BF16), low_out_own], 1
    )
    shared = small_gather(shared, parts, "seq")
    mixes = ranks + 2 * states
    back_mixed, back_mid, low_out = shared[:, :mixes], shared[:, mixes : mixes + rank], shared[:, mixes + rank :]
    block_out = (hidden_f + valid * (branch + nn(low_out_own, out_up_sel))).astype(BF16)

    back_low_state = nt(back_mixed, state_up_sel).astype(BF16)
    back_conv = back_conv + nt(back_mixed, state_proj) + nt(back_low_state, state_down_sel)
    back_conv_pre = back_conv * silu_grad(conv_pre)
    back_x = jnp.zeros_like(back_conv_pre)
    for tap in range(taps):
        back_x = back_x + kernel[tap] * shift_up(back_conv_pre, taps - 1 - tap)
    back_x = back_x.astype(BF16)
    low_parts = (nt(back_x, up_x) + nt(back_z, up_z)).astype(BF16)
    back_in = ring_scatter((nt(back_x, whole_x) + nt(back_z, whole_z)).astype(BF16), parts, "seq")
    back_low_in = lax.all_to_all(
        jnp.broadcast_to(low_parts.reshape(1, tokens, parts * rank), (parts, tokens, parts * rank)),
        "seq", split_axis=0, concat_axis=0, tiled=True,
    ).astype(F32).sum(0).reshape(parts * tokens, rank).astype(BF16)
    back_low_in_own = lax.dynamic_slice_in_dim(back_low_in, part * tokens, tokens, 0)
    back_normed = back_in + nt(back_low_in_own, in_down_sel)
    gained = back_normed * gain_f
    input_grad = (
        cot_f
        + inverse * gained
        - hidden_f * inverse * inverse * inverse * jnp.mean(hidden_f * gained, axis=-1, keepdims=True)
    )

    span = width // parts

    def own_columns(values):
        return lax.dynamic_slice_in_dim(values, part * span, span, 1)

    chosen = (lax.broadcasted_iota(jnp.int32, (rank, 128), 1) == ident).astype(F32)
    sliced = jnp.concatenate(
        [
            tn(low_in, back_x),
            tn(low_in, back_z),
            tn(back_low_out, gated),
            tn(low_out, own_columns(back_out_all)),
            tn(back_low_in, own_columns(normed_all)),
            tn(back_low_state, conv_out),
            tn(low[:, ranks:], back_pre),
            tn(back_mid, low[:, :ranks]),
            tn(low_state, back_mixed),
            chosen,
        ],
        1,
    ).astype(BF16)
    every = lax.all_gather(sliced, ("seq", "fsdp")).reshape((parts, groups) + sliced.shape).astype(F32)
    here = lax.dynamic_index_in_dim(every, part, 0, keepdims=False)
    picked = here[:, 0, -128 : -128 + adapters]

    def by_adapter(values):
        flat = (slice(None),) + (None,) * (values.ndim - 1)
        return sum(picked[g][flat] * values[g][None] for g in range(groups))

    ends = [0]
    for size in (chans, chans, chans, span, span, chans, chans, ranks, mixes):
        ends.append(ends[-1] + size)

    def joined(index):
        values = every[:, :, :, ends[index] : ends[index + 1]]
        return values.transpose(1, 2, 0, 3).reshape(groups, rank, -1)

    def local(index):
        return here[:, :, ends[index] : ends[index + 1]]

    in_up_grad = by_adapter(jnp.concatenate([joined(0), joined(1)], 2))
    out_down_grad = by_adapter(joined(2)).transpose(0, 2, 1)
    out_up_grad = by_adapter(joined(3))
    in_down_grad = by_adapter(joined(4)).transpose(0, 2, 1)
    state_down_grad = by_adapter(local(5)).transpose(0, 2, 1)
    step_up_grad = by_adapter(local(6))
    step_down_grad = by_adapter(local(7)).transpose(0, 2, 1)
    state_up_grad = by_adapter(local(8))
    return (
        block_out[None], input_grad[None], in_down_grad, in_up_grad, state_down_grad, state_up_grad,
        step_down_grad, step_up_grad, out_down_grad, out_up_grad,
    )


def solution(mesh):
    seq, rows = P("fsdp", "seq", None), P(("seq", "fsdp"), None)
    in_specs = (
        seq, P("fsdp"), P("fsdp"), P(), rows, rows, P(None, "seq"), P("seq"), P("seq", None), P(None, "seq"),
        P("seq"), P(None, "seq"), P("seq"), rows, P(), P(), P(None, "seq", None), P(), P(), P(None, None, "seq"),
        P(), P(), seq,
    )
    out_specs = (seq, seq, P(), P(), P(None, "seq", None), P(), P(), P(None, None, "seq"), P(), P())
    return jax.shard_map(body, mesh=mesh, in_specs=in_specs, out_specs=out_specs, check_vma=False)
```

```python
import functools
import jax
import jax.numpy as jnp
from jax import lax
from jax.experimental import pallas as pl
from jax.experimental.pallas import tpu as pltpu
from jax.sharding import PartitionSpec as P

F32 = jnp.float32
BF16 = jnp.bfloat16
LOG2E = 1.4426950408889634


def silu_grad(values):
    sigma = jax.nn.sigmoid(values)
    return sigma * (1.0 + values * (1.0 - sigma))


def softplus(v):
    return jnp.maximum(v, 0.0) + jnp.log1p(jnp.exp(-jnp.abs(v)))


def nt(left, right):
    return lax.dot_general(left, right, (((1,), (1,)), ((), ())), preferred_element_type=F32)


def nn(left, right):
    return jnp.dot(left, right, preferred_element_type=F32)


def tn(left, right):
    return lax.dot_general(left, right, (((0,), (0,)), ((), ())), preferred_element_type=F32)


def spread_matrix(states, sub):
    row = lax.broadcasted_iota(jnp.int32, (states, sub * states), 0)
    col = lax.broadcasted_iota(jnp.int32, (states, sub * states), 1)
    return (lax.rem(col, states) == row).astype(BF16)


def own_step_mask(rows, width, sub):
    row = lax.broadcasted_iota(jnp.int32, (rows, sub * width), 0)
    col = lax.broadcasted_iota(jnp.int32, (rows, sub * width), 1)
    return (lax.rem(row, sub) == lax.div(col, width)).astype(F32)


def ring_place(position, size):
    position = lax.rem(position + size, size)
    return jnp.where(position < size // 2, 2 * position, 2 * (size - 1 - position) + 1)


def ring_position(place, size):
    return jnp.where(lax.rem(place, 2) == 0, lax.div(place, 2), size - 1 - lax.div(place, 2))


def ring_copies(out_ref, pieces, part, sems):
    size, rows = len(pieces) - 1, pieces[0].shape[0]
    far, half, here = size // 2, rows // 2, ring_position(part, size)
    copies = []
    for i, piece in enumerate(pieces):
        hop = (i + 1) // 2
        place = ring_place(here - hop if i % 2 else here + hop, size)
        at = place * rows
        if i == size:
            at = ring_place(here + far, size) * rows + half
        at = pl.multiple_of(at, half)
        copies.append(pltpu.make_async_copy(piece, out_ref.at[pl.ds(at, piece.shape[0]), :], sems.at[i]))
    return copies


def swap_order(size):
    order, bit = [0], size // 2
    while bit:
        order += [at ^ bit for at in order]
        bit //= 2
    return order


def place_of_block(block, part, size):
    apart, out, bit = jnp.bitwise_xor(block, part), 0, size // 2
    weight = 1
    while bit:
        out = out + weight * jnp.bitwise_and(lax.div(apart, bit), 1)
        weight, bit = weight * 2, bit // 2
    return out


def row_copies(out_ref, pieces, group, sems):
    copies = []
    for i, apart in enumerate(swap_order(out_ref.shape[1])):
        at = i if group is None else jnp.bitwise_xor(group, apart)
        piece = pieces.at[i] if group is None else pieces[i]
        copies.append(pltpu.make_async_copy(piece, out_ref.at[:, at], sems.at[i]))
    return copies


def run_all(copies):
    for copy in copies:
        copy.start()
    for copy in copies:
        copy.wait()


def flat(ref):
    return ref[...].reshape(-1, ref.shape[-1])


def conv_before(x, before, weight_ref, bias_ref):
    taps = weight_ref.shape[0]
    padded = jnp.concatenate([before, x], 0)
    out = bias_ref[...]
    for tap in range(taps):
        at = before.shape[0] - (taps - 1 - tap)
        out = out + weight_ref[tap : tap + 1, :] * padded[at : at + x.shape[0]]
    return out


def project_kernel(meta, *refs, parts, groups):
    pieces, refs = refs[: parts + 1], refs[parts + 1 :]
    columns, refs = refs[:groups], refs[groups:]
    (in_down_ref, up_ref, weight_ref, bias_ref, proj_ref, down_ref,
     low_in_ref, x_ref, conv_ref, sums_ref, before, rows_s, whole_s, piece_sems, column_sems) = refs
    step = pl.program_id(0)
    rows = x_ref.shape[0]

    @pl.when(step == 0)
    def _():
        run_all(ring_copies(rows_s, pieces, meta[1], piece_sems) + row_copies(whole_s, columns, meta[2], column_sems))
        before[...] = jnp.zeros_like(before)

    normed = rows_s[pl.ds(pl.multiple_of(step * rows, rows), rows), :]
    low_in = nt(normed, in_down_ref[0]).astype(BF16)
    low_in_ref[...] = low_in
    x = (nn(normed, flat(whole_s)) + nn(low_in, up_ref[0])).astype(BF16)
    x_ref[...] = x
    x_f = x.astype(F32)
    conv_out = jax.nn.silu(conv_before(x_f, before[...], weight_ref, bias_ref)).astype(BF16)
    before[...] = x_f[-8:]
    conv_ref[...] = conv_out
    cut = proj_ref.shape[0]
    sums_ref[:, :cut] = nt(conv_out, proj_ref[...]).astype(BF16)
    sums_ref[:, cut:] = nt(conv_out, down_ref[0]).astype(BF16)


def once(array):
    return pl.BlockSpec(array.shape, lambda i, *_: (0,) * array.ndim, pipeline_mode=pl.Buffered(1))


def chosen(table, which=0, width=None):
    if width is None:
        return pl.BlockSpec((1,) + table.shape[1:], lambda i, meta: (meta[0], 0, 0))
    return pl.BlockSpec((1, table.shape[1], width), lambda i, meta: (meta[0], 0, meta[1] + which))


LIMIT = 58 << 20
AT_ONCE = 4


def gate_kernel(meta, *refs, parts):
    pieces, refs = refs[: parts + 1], refs[parts + 1 :]
    columns, low_in_ref, up_ref, z_ref, rows_s, whole_s, piece_sems, column_sems = refs
    step = pl.program_id(0)

    @pl.when(step == 0)
    def _():
        run_all(ring_copies(rows_s, pieces, meta[1], piece_sems) + row_copies(whole_s, columns, None, column_sems))

    rows = z_ref.shape[0]
    normed = rows_s[pl.ds(pl.multiple_of(step * rows, rows), rows), :]
    z_ref[...] = (nn(normed, flat(whole_s)) + nn(low_in_ref[...], up_ref[0])).astype(BF16)


def gate(meta, pieces, columns, low_in, up, parts, groups):
    tokens, width = pieces[0].shape
    length, chans = tokens * parts, columns.shape[-1]
    block = AT_ONCE * tokens
    seq = lambda size: pl.BlockSpec((block, size), lambda i, meta: (i, 0))
    return pl.pallas_call(
        functools.partial(gate_kernel, parts=parts),
        grid_spec=pltpu.PrefetchScalarGridSpec(
            num_scalar_prefetch=1,
            grid=(length // block,),
            in_specs=[pl.BlockSpec(memory_space=pl.ANY)] * (len(pieces) + 1)
            + [seq(low_in.shape[1]), chosen(up, parts, chans)],
            out_specs=seq(chans),
            scratch_shapes=[
                pltpu.VMEM((length, width), BF16), pltpu.VMEM((parts, groups) + columns.shape[2:], BF16),
                pltpu.SemaphoreType.DMA((len(pieces),)), pltpu.SemaphoreType.DMA((groups,)),
            ],
        ),
        out_shape=jax.ShapeDtypeStruct((length, chans), BF16),
        compiler_params=pltpu.CompilerParams(vmem_limit_bytes=LIMIT),
        name="gate",
    )(meta, *pieces, columns, low_in, up)


def back_gate_kernel(meta, *refs, parts):
    pieces, refs = refs[: parts + 1], refs[parts + 1 :]
    out_proj_ref, out_down_ref, out_up_ref, back_low_ref, cols_ref, grad_ref, rows_s, sems = refs
    step = pl.program_id(0)

    @pl.when(step == 0)
    def _():
        run_all(ring_copies(rows_s, pieces, meta[1], sems))

    block, span = cols_ref.shape
    at = pl.ds(pl.multiple_of(step * block, block), block)
    share_of = max(span * parts // rows_s.shape[1], 1)
    cols_ref[...] = rows_s[at, pl.ds(pl.multiple_of(lax.div(meta[1], share_of) * span, span), span)]
    rows = rows_s[at, :]
    back_low = nt(rows, out_up_ref[0]).astype(BF16)
    back_low_ref[...] = back_low
    grad_ref[...] = (nt(rows, out_proj_ref[...]) + nn(back_low, out_down_ref[0])).astype(BF16)


def back_gate(meta, pieces, out_proj, out_down, out_up, parts):
    tokens, width = pieces[0].shape
    chans, rank, block, length = out_proj.shape[0], out_up.shape[1], AT_ONCE * tokens, tokens * parts
    span = max(width // parts, 128)
    seq = lambda size: pl.BlockSpec((block, size), lambda i, meta: (i, 0))
    return pl.pallas_call(
        functools.partial(back_gate_kernel, parts=parts),
        grid_spec=pltpu.PrefetchScalarGridSpec(
            num_scalar_prefetch=1,
            grid=(length // block,),
            in_specs=[pl.BlockSpec(memory_space=pl.ANY)] * len(pieces)
            + [once(out_proj), chosen(out_down, 0, chans), chosen(out_up)],
            out_specs=[seq(rank), seq(span), seq(chans)],
            scratch_shapes=[pltpu.VMEM((length, width), BF16), pltpu.SemaphoreType.DMA((len(pieces),))],
        ),
        out_shape=[jax.ShapeDtypeStruct((length, size), BF16) for size in (rank, span, chans)],
        compiler_params=pltpu.CompilerParams(vmem_limit_bytes=LIMIT),
        name="back_gate",
    )(meta, *pieces, out_proj, out_down, out_up)


def project(meta, pieces, columns, in_down, up, weight, bias, proj, down, parts, groups):
    tokens, width = pieces[0].shape
    length, chans, rank = tokens * parts, columns[0].shape[-1], in_down.shape[1]
    cols = proj.shape[0] + rank
    seq = lambda size: pl.BlockSpec((AT_ONCE * tokens, size), lambda i, meta: (i, 0))
    rows = columns[0].shape[1]
    whole_shape = (parts, groups, rows, chans)
    return pl.pallas_call(
        functools.partial(project_kernel, parts=parts, groups=groups),
        grid_spec=pltpu.PrefetchScalarGridSpec(
            num_scalar_prefetch=1,
            grid=(parts // AT_ONCE,),
            in_specs=[pl.BlockSpec(memory_space=pl.ANY)] * (len(pieces) + groups)
            + [chosen(in_down), chosen(up, 0, chans), once(weight), once(bias), once(proj), chosen(down)],
            out_specs=[seq(rank), seq(chans), seq(chans), seq(cols)],
            scratch_shapes=[
                pltpu.VMEM((8, chans), F32), pltpu.VMEM((length, width), BF16), pltpu.VMEM(whole_shape, BF16),
                pltpu.SemaphoreType.DMA((len(pieces),)), pltpu.SemaphoreType.DMA((groups,)),
            ],
        ),
        out_shape=[jax.ShapeDtypeStruct((length, size), BF16) for size in (rank, chans, chans, cols)],
        compiler_params=pltpu.CompilerParams(vmem_limit_bytes=LIMIT),
        name="project",
    )(meta, *pieces, *columns, in_down, up, weight, bias, proj, down)


def share_kernel(meta, got_ref, state_up_ref, step_down_ref, out_ref, *, ranks, states):
    sums = got_ref[0].astype(F32)
    for i in range(1, got_ref.shape[0]):
        sums = sums + got_ref[i].astype(F32)
    cut = ranks + 2 * states
    low_state = sums[:, cut:].astype(BF16)
    mixed = sums[:, :cut] + nn(low_state, state_up_ref[0])
    step_low = mixed[:, :ranks].astype(BF16)
    step_mid = nt(step_low, step_down_ref[0]).astype(BF16)
    out_ref[...] = jnp.concatenate([step_low, step_mid, mixed[:, ranks:].astype(BF16), low_state], 1)


def share(meta, got, state_up, step_down, ranks, states):
    tokens, rank = got.shape[1], step_down.shape[1]
    cols = ranks + 2 * rank + 2 * states
    return pl.pallas_call(
        functools.partial(share_kernel, ranks=ranks, states=states),
        grid_spec=pltpu.PrefetchScalarGridSpec(
            num_scalar_prefetch=1,
            grid=(1,),
            in_specs=[once(got), chosen(state_up), chosen(step_down)],
            out_specs=pl.BlockSpec((tokens, cols), lambda i, meta: (0, 0)),
        ),
        out_shape=jax.ShapeDtypeStruct((tokens, cols), BF16),
        name="share",
    )(meta, got, state_up, step_down)


def share_back_kernel(meta, got_ref, step_down_ref, out_ref, *, ranks, states):
    sums = got_ref[0].astype(F32)
    for i in range(1, got_ref.shape[0]):
        sums = sums + got_ref[i].astype(F32)
    rank = step_down_ref.shape[1]
    mid, end = ranks + rank, ranks + rank + 2 * states
    back_mid = sums[:, ranks:mid]
    down = step_down_ref[0].astype(F32)
    back_step = sums[:, :ranks] + jnp.dot(back_mid, down, precision=lax.Precision.HIGHEST, preferred_element_type=F32)
    out_ref[...] = jnp.concatenate([back_step, sums[:, mid:end], back_mid, sums[:, end:]], 1).astype(BF16)


def share_back(meta, got, step_down, ranks, states):
    tokens, cols = got.shape[1:]
    return pl.pallas_call(
        functools.partial(share_back_kernel, ranks=ranks, states=states),
        grid_spec=pltpu.PrefetchScalarGridSpec(
            num_scalar_prefetch=1,
            grid=(1,),
            in_specs=[once(got), chosen(step_down)],
            out_specs=pl.BlockSpec((tokens, cols), lambda i, meta: (0, 0)),
        ),
        out_shape=jax.ShapeDtypeStruct((tokens, cols), BF16),
        name="share_back",
    )(meta, got, step_down)


def columns_of_groups(values, ref, sub):
    turned = values.astype(F32).T
    for k in range(ref.shape[0]):
        ref[k] = turned[:, k * sub : (k + 1) * sub]


def scan_forward_kernel(
    meta, shared_ref, u_ref, z_ref, step_proj_ref, step_up_ref, bias_ref, rate_ref, skip_ref,
    gated_ref, scanned_ref, states_ref,
    carry, delta_s, du_s, cm_s, y_s, bt_s, held_a, held_b, *, sub, ranks,
):
    rows = u_ref.shape[0]
    states = rate_ref.shape[0]
    rank = step_up_ref.shape[1]

    @pl.when(pl.program_id(0) == 0)
    def _():
        carry[...] = jnp.zeros_like(carry)
        held_b[...] = jnp.zeros_like(held_b)
        cm_s[:sub, :] = jnp.zeros((sub, sub * states), BF16)

    shared = shared_ref[0]
    step_mid = shared[:, ranks : ranks + rank]
    pre = nn(shared[:, :ranks], step_proj_ref[...]) + nn(step_mid, step_up_ref[0]) + bias_ref[...]
    delta = softplus(pre)
    delta_s[...] = delta
    du_s[...] = delta * u_ref[...].astype(F32)
    b_rows = shared[:, ranks + rank : ranks + rank + states]
    c_rows = shared[:, ranks + rank + states : ranks + rank + 2 * states]
    columns_of_groups(b_rows, bt_s, sub)
    cm = nn(c_rows, spread_matrix(states, sub)) * own_step_mask(rows, states, sub)
    cm_s[sub:, :] = cm.astype(BF16)
    rate = rate_ref[...]

    def pair(k, s):
        for turn, (mine, other) in enumerate(((held_a, held_b), (held_b, held_a))):
            base = pl.multiple_of(k * (2 * sub) + turn * sub, sub)
            y_s[pl.ds(base, sub), :] = nn(cm_s[pl.ds(base, sub), :], other[...])
            bt = bt_s[k * 2 + turn]
            for t in range(sub):
                dl = delta_s[pl.ds(base + t, 1), :]
                du = du_s[pl.ds(base + t, 1), :]
                s = jnp.exp2(dl * rate) * s + du * bt[:, t : t + 1]
                low = s.astype(BF16)
                mine[t * states : (t + 1) * states, :] = low
                states_ref[pl.ds(pl.multiple_of((base + t) * states, states), states), :] = low
        return s

    carry[...] = lax.fori_loop(0, rows // (2 * sub), pair, carry[...])
    y_s[rows:, :] = nn(cm_s[rows:, :], held_b[...])
    scanned = y_s[sub:, :] + skip_ref[...] * u_ref[...].astype(F32)
    scanned_ref[...] = scanned
    gated_ref[...] = (scanned * jax.nn.silu(z_ref[...].astype(F32))).astype(BF16)


def scan_forward(meta, shared, u, z, step_proj, step_up, bias, rate, skip, parts, sub):
    length, chans = u.shape
    block = length // parts
    states, ranks = rate.shape[0], step_proj.shape[0]
    seq = lambda cols: pl.BlockSpec((block, cols), lambda i, meta: (i, 0))
    out = lambda cols, dtype=BF16, rows=length: jax.ShapeDtypeStruct((rows, cols), dtype)
    return pl.pallas_call(
        functools.partial(scan_forward_kernel, sub=sub, ranks=ranks),
        grid_spec=pltpu.PrefetchScalarGridSpec(
            num_scalar_prefetch=1,
            grid=(parts,),
            in_specs=[
                pl.BlockSpec((1,) + shared.shape[1:], lambda i, meta: (place_of_block(i, meta[1], parts), 0, 0)),
                seq(chans), seq(chans), once(step_proj), chosen(step_up), once(bias), once(rate), once(skip),
            ],
            out_specs=[seq(chans), seq(chans), pl.BlockSpec((block * states, chans), lambda i, meta: (i, 0))],
            scratch_shapes=[
                pltpu.VMEM((states, chans), F32),
                pltpu.VMEM((block, chans), F32),
                pltpu.VMEM((block, chans), F32),
                pltpu.VMEM((block + sub, sub * states), BF16),
                pltpu.VMEM((block + sub, chans), F32),
                pltpu.VMEM((block // sub, states, sub), F32),
                pltpu.VMEM((sub * states, chans), BF16),
                pltpu.VMEM((sub * states, chans), BF16),
            ],
        ),
        out_shape=[out(chans), out(chans, F32), out(chans, rows=length * states)],
        compiler_params=pltpu.CompilerParams(vmem_limit_bytes=LIMIT),
        name="scan_forward",
    )(meta, shared, u, z, step_proj, step_up, bias, rate, skip)


def scan_backward_kernel(meta, *refs, sub, ranks):
    (shared_ref, step_proj_ref, step_up_ref, bias_ref, u_ref, z_ref, scanned_ref, bg_ref, states_ref, before_ref,
     rate_ref, decay_ref, skip_ref, low_out_ref) = refs[:14]
    pre_ref, conv_ref, bz_ref, mixed_ref = refs[14:18]
    carry, delta_s, du_s, bs_s, pre_s, bm_s, w_s, bd_s, bb_s, bc_s, ct_s, g_a, g_b, q_a, q_b = refs[18:]
    rows, chans = u_ref.shape
    states, rank = rate_ref.shape[0], step_up_ref.shape[1]
    step = pl.program_id(0)
    first = step == pl.num_programs(0) - 1

    @pl.when(step == 0)
    def _():
        carry[...] = jnp.zeros_like(carry)
        for ref in (g_a, q_a):
            ref[...] = jnp.zeros_like(ref)
        bm_s[rows:, :] = jnp.zeros((sub, sub * states), BF16)
        du_s[rows:, :] = jnp.zeros((sub, chans), F32)

    shared = shared_ref[0]
    step_mid = shared[:, ranks : ranks + rank]
    pre = nn(shared[:, :ranks], step_proj_ref[...]) + nn(step_mid, step_up_ref[0]) + bias_ref[...]
    delta = softplus(pre)
    z = z_ref[...].astype(F32)
    bg = bg_ref[...].astype(F32)
    sigma = jax.nn.sigmoid(z)
    bs_s[...] = bg * (z * sigma)
    bz_ref[...] = (bg * scanned_ref[...] * (sigma * (1.0 + z * (1.0 - sigma)))).astype(BF16)
    pre_s[...] = pre
    delta_s[...] = delta
    du_s[:rows, :] = delta * u_ref[...].astype(F32)
    b_rows = shared[:, ranks + rank : ranks + rank + states]
    c_rows = shared[:, ranks + rank + states : ranks + rank + 2 * states]
    columns_of_groups(c_rows, ct_s, sub)
    bm = nn(b_rows, spread_matrix(states, sub)) * own_step_mask(rows, states, sub)
    bm_s[:rows, :] = bm.astype(BF16)
    ones = own_step_mask(sub, states, sub).astype(BF16)
    col = lax.broadcasted_iota(jnp.int32, (states, sub), 1)
    rate = rate_ref[...]
    decay = decay_ref[...]
    pairs = rows // (2 * sub)

    def diagonal(wide):
        out = wide[:states]
        for t in range(1, sub):
            out = jnp.where(col == t, wide[t * states : (t + 1) * states], out)
        return out

    def finish(at, k, g_ref, q_ref):
        w_s[at, :] = nn(bm_s[at, :], g_ref[...])
        bd_s[at, :] = nn(ones, q_ref[...])
        bb_s[k] = diagonal(nt(g_ref[...], du_s[at, :].astype(BF16)))

    def pair(i, h):
        for turn, (g_mine, q_mine, g_other, q_other) in enumerate(((g_b, q_b, g_a, q_a), (g_a, q_a, g_b, q_b))):
            k = (pairs - 1 - i) * 2 + 1 - turn
            base = pl.multiple_of(k * sub, sub)
            finish(pl.ds(pl.multiple_of(base + sub, sub), sub), k + 1, g_other, q_other)
            wide = pl.ds(pl.multiple_of(base * states, sub * states), sub * states)
            bc_s[k] = diagonal(nt(states_ref[wide, :], bs_s[pl.ds(base, sub), :].astype(BF16)))
            ct = ct_s[k]
            for t in range(sub - 1, -1, -1):
                dl = delta_s[pl.ds(base + t, 1), :]
                bs = bs_s[pl.ds(base + t, 1), :]
                g = bs * ct[:, t : t + 1] + h
                h = g * jnp.exp2(dl * rate)
                if t:
                    sp = states_ref[pl.ds(pl.multiple_of((base + t - 1) * states, states), states), :]
                else:
                    at = pl.multiple_of(jnp.maximum(base - 1, 0) * states, states)
                    inside = jnp.where(k > 0, 1.0, 0.0)
                    outside = jnp.where(first, 0.0, 1.0 - inside)
                    sp = states_ref[pl.ds(at, states), :] * inside.astype(BF16)
                    sp = sp + before_ref[...] * outside.astype(BF16)
                g_mine[t * states : (t + 1) * states, :] = g.astype(BF16)
                q_mine[t * states : (t + 1) * states, :] = h.astype(BF16) * (decay * sp)
        return h

    carry[...] = lax.fori_loop(0, pairs, pair, carry[...])
    finish(pl.ds(0, sub), 0, g_a, q_a)
    w = w_s[:rows, :]
    conv_ref[...] = w * delta_s[...] + skip_ref[...] * bs_s[...]
    back_delta = bd_s[:rows, :] + w * u_ref[...].astype(F32)
    back_pre = (back_delta * jax.nn.sigmoid(pre_s[...])).astype(BF16)
    pre_ref[...] = back_pre
    turned = [
        jnp.concatenate([ref[k] for k in range(rows // sub)], 1).T for ref in (bb_s, bc_s)
    ]
    mixed_ref[...] = jnp.concatenate(
        [nt(back_pre, step_proj_ref[...]), nt(back_pre, step_up_ref[0])] + turned + [low_out_ref[...]], 1
    ).astype(BF16)


def scan_backward(
    meta, shared, step_proj, step_up, bias, u, z, scanned, bg, kept, rate, decay, skip, low_out, parts, sub,
):
    length, chans = u.shape
    block = length // parts
    states, rank, ranks = rate.shape[0], step_up.shape[1], step_proj.shape[0]
    end = parts
    seq = lambda cols: pl.BlockSpec((block, cols), lambda i, meta: (end - 1 - i, 0))
    cols = ranks + 2 * rank + 2 * states
    out = lambda cols, dtype=BF16: jax.ShapeDtypeStruct((length, cols), dtype)
    args = (shared, step_proj, step_up, bias, u, z, scanned, bg, kept, kept, rate, decay, skip, low_out)
    return pl.pallas_call(
        functools.partial(scan_backward_kernel, sub=sub, ranks=ranks),
        grid_spec=pltpu.PrefetchScalarGridSpec(
            num_scalar_prefetch=1,
            grid=(parts,),
            in_specs=[
                pl.BlockSpec(
                    (1,) + shared.shape[1:], lambda i, meta: (place_of_block(end - 1 - i, meta[1], parts), 0, 0)
                ),
                once(step_proj), chosen(step_up), once(bias), seq(chans), seq(chans), seq(chans), seq(chans),
                pl.BlockSpec((block * states, chans), lambda i, meta: (end - 1 - i, 0)),
                pl.BlockSpec((states, chans), lambda i, meta: (jnp.maximum((end - 1 - i) * block - 1, 0), 0)),
                once(rate), once(decay), once(skip), seq(rank),
            ],
            out_specs=[seq(chans), seq(chans), seq(chans), seq(cols)],
            scratch_shapes=[
                pltpu.VMEM((states, chans), F32),
                pltpu.VMEM((block, chans), F32),
                pltpu.VMEM((block + sub, chans), F32),
                pltpu.VMEM((block, chans), F32),
                pltpu.VMEM((block, chans), F32),
                pltpu.VMEM((block + sub, sub * states), BF16),
                pltpu.VMEM((block + sub, chans), F32),
                pltpu.VMEM((block + sub, chans), F32),
                pltpu.VMEM((block // sub + 1, states, sub), F32),
                pltpu.VMEM((block // sub, states, sub), F32),
                pltpu.VMEM((block // sub, states, sub), F32),
                pltpu.VMEM((sub * states, chans), BF16),
                pltpu.VMEM((sub * states, chans), BF16),
                pltpu.VMEM((sub * states, chans), BF16),
                pltpu.VMEM((sub * states, chans), BF16),
            ],
        ),
        out_shape=[out(chans), out(chans, F32), out(chans), out(cols)],
        compiler_params=pltpu.CompilerParams(vmem_limit_bytes=LIMIT),
        name="scan_backward",
    )(meta, *args)


def finish_kernel(
    meta, *refs, ranks, states, parts, groups,
):
    pieces, refs = refs[: parts + 1], refs[parts + 1 :]
    columns_x, columns_z, refs = refs[:groups], refs[groups], refs[groups + 1 :]
    (back_ref, shared_ref, conv_grad_ref, back_z_ref, back_pre_ref, x_ref, x_before_ref, u_ref, low_in_ref,
     gated_ref, back_low_ref, cols_ref, up_x_ref, up_z_ref, proj_ref, down_ref,
     state_up_ref, in_down_ref, weight_ref, bias_ref,
     parts_ref, wide_ref, down_grad_ref, local_ref,
     after, sums_s, down_s, local_s, rows_s, whole_x, whole_z, piece_sems, x_sems, z_sems) = refs
    copies = (
        ring_copies(rows_s, pieces, meta[1], piece_sems)
        + row_copies(whole_x, columns_x, meta[2], x_sems)
        + row_copies(whole_z, columns_z, None, z_sems)
    )
    step = pl.program_id(0)
    steps = pl.num_programs(0)
    rows, chans = u_ref.shape
    rank = state_up_ref.shape[1]
    taps = weight_ref.shape[0]
    mixes = ranks + 2 * states

    @pl.when(step == 0)
    def _():
        for copy in copies:
            copy.start()
        after[...] = jnp.zeros_like(after)
        sums_s[...] = jnp.zeros_like(sums_s)
        down_s[...] = jnp.zeros_like(down_s)
        local_s[...] = jnp.zeros_like(local_s)

    per = rows // back_ref.shape[1]
    places = [place_of_block((steps - 1 - step) * per + j, meta[1], parts) for j in range(per)]
    back = jnp.concatenate([back_ref[place] for place in places], 0)
    shared = jnp.concatenate([shared_ref[place] for place in places], 0)
    u = u_ref[...]
    mixed = back[:, :mixes]
    back_low_state = nt(mixed, state_up_ref[0]).astype(BF16)
    grad = conv_grad_ref[...] + nn(mixed, proj_ref[...]) + nn(back_low_state, down_ref[0])
    keep = jnp.where(step == steps - 1, 0.0, 1.0)
    conv_pre = conv_before(x_ref[...].astype(F32), x_before_ref[...].astype(F32) * keep, weight_ref, bias_ref)
    grad = grad * silu_grad(conv_pre)
    padded = jnp.concatenate([grad, after[...]], 0)
    back_x = weight_ref[taps - 1 : taps, :] * grad
    for tap in range(taps - 1):
        at = taps - 1 - tap
        back_x = back_x + weight_ref[tap : tap + 1, :] * padded[at : at + rows]
    after[...] = grad[:8]
    back_x, back_z = back_x.astype(BF16), back_z_ref[...]

    @pl.when(step == 0)
    def _():
        for copy in copies:
            copy.wait()

    normed = rows_s[pl.ds(pl.multiple_of((steps - 1 - step) * rows, rows), rows), :]
    back_low_in = (nt(back_x, up_x_ref[0]) + nt(back_z, up_z_ref[0])).astype(BF16)
    parts_ref[...] = (
        nt(back_x, flat(whole_x)) + nt(back_z, flat(whole_z)) + nn(back_low_in, in_down_ref[0])
    ).astype(BF16)
    down_s[...] += tn(back_low_in, normed)
    low_in = low_in_ref[...]
    sums_s[:, :chans] += tn(low_in, back_x)
    sums_s[:, chans : 2 * chans] += tn(low_in, back_z)
    sums_s[:, 2 * chans : 3 * chans] += tn(back_low_ref[...], gated_ref[...])
    sums_s[:, 3 * chans :] += tn(back[:, mixes + rank :], cols_ref[...])
    local_s[:, :chans] += tn(back_low_state, u)
    local_s[:, chans : 2 * chans] += tn(shared[:, ranks : ranks + rank], back_pre_ref[...])
    local_s[:, 2 * chans : 2 * chans + ranks] += tn(back[:, mixes : mixes + rank], shared[:, :ranks])
    at = 2 * chans + ranks
    local_s[:, at : at + mixes] += tn(shared[:, ranks + rank + 2 * states :], mixed)

    @pl.when(step == steps - 1)
    def _():
        wide_ref[...] = sums_s[...].astype(BF16)
        down_grad_ref[...] = down_s[...].astype(BF16)
        lane = lax.broadcasted_iota(jnp.int32, (rank, 128), 1)
        local_ref[:, :-128] = local_s[...].astype(BF16)
        local_ref[:, -128:] = (lane == meta[0]).astype(BF16)


def finish(
    meta, pieces, columns_x, columns_z, back, shared, conv_grad, back_z, back_pre, x, u, low_in, gated, back_low, cols, up,
    proj, down, state_up, in_down, weight, bias, parts, groups, states,
):
    length, chans = u.shape
    block, rank, span = AT_ONCE * length // parts, low_in.shape[1], cols.shape[1]
    mixes = proj.shape[0]
    ranks = mixes - 2 * states
    width = pieces[0].shape[1]
    whole_shape = (parts, groups) + columns_x[0].shape[1:]
    end = length // block - 1
    seq = lambda size: pl.BlockSpec((block, size), lambda i, meta: (end - i, 0))
    wide = 3 * chans + span
    local = 2 * chans + ranks + 2 * 128
    fixed = lambda size: pl.BlockSpec((rank, size), lambda i, meta: (0, 0))
    return pl.pallas_call(
        functools.partial(finish_kernel, ranks=ranks, states=states, parts=parts, groups=groups),
        grid_spec=pltpu.PrefetchScalarGridSpec(
            num_scalar_prefetch=1,
            grid=(length // block,),
            in_specs=[pl.BlockSpec(memory_space=pl.ANY)] * (len(pieces) + groups + 1)
            + [
                once(back), once(shared), seq(chans), seq(chans), seq(chans), seq(chans),
                pl.BlockSpec((16, chans), lambda i, meta: (jnp.maximum((end - i) * (block // 16) - 1, 0), 0)),
                seq(chans), seq(rank), seq(chans), seq(rank), seq(span),
                chosen(up, 0, chans), chosen(up, parts, chans), once(proj), chosen(down), chosen(state_up),
                chosen(in_down), once(weight), once(bias),
            ],
            out_specs=[seq(width), fixed(wide), fixed(width), fixed(local + 128)],
            scratch_shapes=[
                pltpu.VMEM((8, chans), F32), pltpu.VMEM((rank, wide), F32), pltpu.VMEM((rank, width), F32),
                pltpu.VMEM((rank, local), F32), pltpu.VMEM((length, width), BF16),
                pltpu.VMEM(whole_shape, BF16), pltpu.VMEM(whole_shape, BF16),
                pltpu.SemaphoreType.DMA((len(pieces),)), pltpu.SemaphoreType.DMA((groups,)),
                pltpu.SemaphoreType.DMA((groups,)),
            ],
        ),
        out_shape=[
            jax.ShapeDtypeStruct((length, width), BF16),
            jax.ShapeDtypeStruct((rank, wide), BF16),
            jax.ShapeDtypeStruct((rank, width), BF16),
            jax.ShapeDtypeStruct((rank, local + 128), BF16),
        ],
        compiler_params=pltpu.CompilerParams(vmem_limit_bytes=LIMIT),
        name="finish",
    )(
        meta, *pieces, *columns_x, columns_z, back, shared, conv_grad, back_z, back_pre, x, x, u, low_in, gated, back_low,
        cols, up, up, proj, down, state_up, in_down, weight, bias,
    )


def placed(values, idents, e):
    total = None
    for value, ident in zip(values, idents):
        term = jnp.where(ident == e, value, 0.0)
        total = term if total is None else total + term
    return total


def place_kernel(meta, *refs, first, size, every):
    values_refs, out_ref = refs[:-1], refs[-1]
    groups, parts = len(values_refs), values_refs[0].shape[0]
    count = parts // every
    per = out_ref.shape[2] // size
    idents = [meta[3 + groups + g] for g in range(groups)]
    step = pl.program_id(0)
    column = pl.multiple_of((first + lax.div(step * per, count)) * size, size)
    for j in range(per):
        at = place_of_block(lax.rem(step * per + j, count) * every, meta[1], parts)
        values = [ref[at, :, pl.ds(column, size)].astype(F32) for ref in values_refs]
        for e in range(out_ref.shape[0]):
            out_ref[e, :, j * size : (j + 1) * size] = placed(values, idents, e)


def place(meta, values, adapters, first, size, parts, every=1, runs=1):
    rank = values[0].shape[1]
    count = parts // every
    per = count // 2
    return pl.pallas_call(
        functools.partial(place_kernel, first=first, size=size, every=every),
        grid_spec=pltpu.PrefetchScalarGridSpec(
            num_scalar_prefetch=1,
            grid=(runs * count // per,),
            in_specs=[once(value) for value in values],
            out_specs=pl.BlockSpec((adapters, rank, size * per), lambda i, meta: (0, 0, i)),
        ),
        out_shape=jax.ShapeDtypeStruct((adapters, rank, size * count * runs), F32),
        compiler_params=pltpu.CompilerParams(vmem_limit_bytes=16 << 20),
        name="place",
    )(meta, *values)


def place_local_kernel(meta, values_ref, *out_refs):
    groups = values_ref.shape[0]
    idents = [meta[3 + g] for g in range(groups)]
    at = 0
    for ref in out_refs:
        size = ref.shape[2]
        values = [values_ref[g, :, at : at + size].astype(F32) for g in range(groups)]
        for e in range(ref.shape[0]):
            ref[e] = placed(values, idents, e)
        at += size


def place_local(meta, values, adapters, sizes):
    rank = values.shape[1]
    return pl.pallas_call(
        place_local_kernel,
        grid_spec=pltpu.PrefetchScalarGridSpec(
            num_scalar_prefetch=1,
            grid=(1,),
            in_specs=[once(values)],
            out_specs=[pl.BlockSpec((adapters, rank, size), lambda i, meta: (0, 0, 0)) for size in sizes],
        ),
        out_shape=[jax.ShapeDtypeStruct((adapters, rank, size), F32) for size in sizes],
        name="place_local",
    )(meta, values)


EPS = 1e-05


def ring_send(value, size, hop, axis):
    order = list(range(0, size, 2)) + list(range(1, size, 2))[::-1]
    pairs = [(order[i], order[(i + hop) % size]) for i in range(size)]
    return lax.ppermute(value, axis, pairs)


class RingGather:
    def __init__(self, own, size, axis):
        self.size, self.axis, self.rows, self.done = size, axis, own.shape[0], 0
        self.pieces = [own]
        self.ends = (own, own)

    def advance(self, hops):
        far, half = self.size // 2, self.rows // 2
        for _ in range(min(hops, far - self.done)):
            self.done += 1
            ahead, back = self.ends
            if self.done == far:
                ahead, back = ahead[:half], back[half:]
            self.ends = (ring_send(ahead, self.size, 1, self.axis), ring_send(back, self.size, -1, self.axis))
            self.pieces += list(self.ends)

    def all_pieces(self):
        self.advance(self.size)
        return self.pieces


class RingScatter:
    def __init__(self, partial, size, axis):
        self.partial, self.size, self.axis, self.done = partial, size, axis, 0
        self.rows = partial.shape[0] // size
        self.position = ring_position(lax.axis_index(axis), size)
        self.ends = None

    def block(self, offset, start=0, rows=None):
        at = ring_place(self.position + offset, self.size) * self.rows + start
        return lax.dynamic_slice_in_dim(self.partial, at, rows or self.rows, 0)

    def advance(self, hops):
        far, half = self.size // 2, self.rows // 2
        for _ in range(min(hops, far - self.done)):
            left = far - self.done
            if left == far:
                mine, other = self.block(far, 0, half), self.block(far, half, half)
            else:
                mine, other = self.block(left).astype(F32), self.block(-left).astype(F32)
                ahead, back = (end.astype(F32) for end in self.ends)
                if left == far - 1:
                    blank = jnp.zeros_like(ahead)
                    ahead, back = jnp.concatenate([ahead, blank], 0), jnp.concatenate([blank, back], 0)
                mine, other = (mine + ahead).astype(BF16), (other + back).astype(BF16)
            self.ends = (
                ring_send(mine, self.size, 1, self.axis),
                ring_send(other, self.size, -1, self.axis),
            )
            self.done += 1

    def total(self):
        self.advance(self.size)
        return self.block(0).astype(F32) + self.ends[0].astype(F32) + self.ends[1].astype(F32)


def together(*values):
    return lax.optimization_barrier(values)


def swap(value, size, bit, axis):
    return lax.ppermute(value, axis, [(i, i ^ bit) for i in range(size)])


def bits_of(size):
    bit = size // 2
    while bit:
        yield bit
        bit //= 2


def swap_gather(own, size, axis):
    held = [own]
    for bit in bits_of(size):
        held += [swap(block, size, bit, axis) for block in held]
    return held


def small_gather(own, size, axis):
    held = own[None]
    for bit in bits_of(size):
        held = jnp.concatenate([held, swap(held, size, bit, axis)], 0)
    return held


def exchange(values, size, axis):
    got = lax.all_to_all(values, axis, split_axis=0, concat_axis=0, tiled=True)
    return got.reshape((size, -1) + values.shape[1:])


def body(
    hidden, lengths, adapter_ids, norm_gain, in_proj_x, in_proj_z, conv_weight, conv_bias, state_proj,
    step_proj, step_bias, decay_log, skip_gain, out_proj, in_down, in_up, state_down, state_up, step_down,
    step_up, out_down, out_up, cotangent,
):
    parts, groups = lax.axis_size("seq"), lax.axis_size("fsdp")
    part, group = lax.axis_index("seq"), lax.axis_index("fsdp")
    tokens, width = hidden.shape[1:]
    chans = conv_weight.shape[1]
    ranks = step_proj.shape[0]
    states = decay_log.shape[0]
    rank = in_down.shape[2]
    adapters = in_down.shape[0]
    ident = adapter_ids[0]
    sub = 16
    meta = jnp.stack([ident, part, group]).astype(jnp.int32)
    in_down, state_down, step_down, out_down = (
        table.transpose(0, 2, 1) for table in (in_down, state_down, step_down, out_down)
    )
    state_proj = state_proj.T

    hidden_f = hidden[0].astype(F32)
    gain_f = norm_gain.astype(F32)
    inverse = lax.rsqrt(jnp.mean(hidden_f * hidden_f, axis=-1, keepdims=True) + EPS)
    normed = (hidden_f * inverse * gain_f).astype(BF16)
    positions = part * tokens + lax.broadcasted_iota(jnp.int32, (tokens, 1), 0)
    valid = (positions < lengths[0]).astype(F32)
    cot_f = cotangent[0].astype(F32)
    back_out = (valid * cot_f).astype(BF16)
    conv_weight, conv_bias = conv_weight.astype(F32), conv_bias.astype(F32)[None]
    bias, skip = step_bias.astype(F32)[None], skip_gain.astype(F32)[None]
    decay = -jnp.exp(decay_log.astype(F32))
    rate, decay = decay * LOG2E, decay.astype(BF16)
    rows = in_proj_x.shape[0]

    def own_columns_of(weight):
        return lax.all_to_all(weight, "seq", split_axis=1, concat_axis=0, tiled=True).reshape(parts, rows, chans)

    hops = max(parts // 8, 1)
    whole_out = lax.all_gather(out_proj, "fsdp", axis=0, tiled=True)
    pieces = RingGather(normed, parts, "seq").all_pieces()
    columns = swap_gather(own_columns_of(in_proj_x), groups, "fsdp")

    pieces, columns, back_out, in_proj_z = together(pieces, columns, back_out, in_proj_z)
    cot_ring = RingGather(back_out, parts, "seq")
    cot_ring.advance(hops)
    mine_z = own_columns_of(in_proj_z)
    low_in, x, conv_out, sums = project(
        meta, pieces, columns, in_down, in_up, conv_weight, conv_bias, state_proj, state_down, parts, groups
    )
    sums, cot_ring.ends, mine_z = together(sums, cot_ring.ends, mine_z)
    cot_ring.advance(hops)
    columns_z = lax.all_gather(mine_z, "fsdp")
    shared = share(meta, exchange(sums, parts, "seq"), state_up, step_down, ranks, states)
    shared, cot_ring.ends = together(shared, cot_ring.ends)
    shared = small_gather(shared, parts, "seq")
    z = gate(meta, pieces, columns_z, low_in, in_up, parts, groups)
    shared, z, cot_ring.ends = together(shared, z, cot_ring.ends)
    cot_ring.advance(hops)
    gated, scanned, kept = scan_forward(meta, shared, conv_out, z, step_proj, step_up, bias, rate, skip, parts, sub)
    gated, cot_ring.ends = together(gated, cot_ring.ends)
    cot_ring.advance(parts)
    out_down_sel = lax.dynamic_slice(out_down, (ident, 0, part * chans), (1, rank, chans))[0]
    out_parts, low_out = nn(gated, whole_out).astype(BF16), nt(gated, out_down_sel)
    out_parts, low_out, cot_ring.pieces = together(out_parts, low_out, cot_ring.pieces)
    out_ring = RingScatter(out_parts, parts, "seq")
    out_ring.advance(hops)
    back_low, cols, back_gated = back_gate(meta, cot_ring.pieces, whole_out, out_down, out_up, parts)
    back_gated, out_ring.ends = together(back_gated, out_ring.ends)
    out_ring.advance(hops)
    back_pre, conv_grad, back_z, mixed = scan_backward(
        meta, shared, step_proj, step_up, bias, conv_out, z, scanned, back_gated, kept, rate, decay, skip, low_out, parts,
        sub,
    )
    mixed, out_ring.ends = together(mixed, out_ring.ends)
    out_ring.advance(hops)
    back_own = share_back(meta, exchange(mixed, parts, "seq"), step_down, ranks, states)
    back_own, out_ring.ends = together(back_own, out_ring.ends)
    back = small_gather(back_own, parts, "seq")
    back, out_ring.ends = together(back, out_ring.ends)
    out_ring.advance(parts)
    in_parts, wide, down_grad, local = finish(
        meta, pieces, columns, columns_z, back, shared, conv_grad, back_z, back_pre, x, conv_out, low_in, gated, back_low,
        cols, in_up, state_proj, state_down, state_up, in_down, conv_weight, conv_bias, parts, groups, states,
    )
    in_parts, wide, down_grad, local, out_ring.ends = together(in_parts, wide, down_grad, local, out_ring.ends)
    in_ring = RingScatter(in_parts, parts, "seq")
    span = cols.shape[1]
    share_of = max(span * parts // width, 1)
    held = jnp.concatenate([wide, down_grad], 1)[None]
    for bit in bits_of(parts):
        in_ring.advance(hops)
        held = jnp.concatenate([held, swap(held, parts, bit, "seq")], 0)
        held, in_ring.ends = together(held, in_ring.ends)
    in_ring.advance(parts)
    down_grad = held[:, :, wide.shape[1] :].astype(F32).sum(0).astype(BF16)
    held = held[:, :, : wide.shape[1]]
    wide = [held]
    for bit in bits_of(groups):
        wide += [swap(block, groups, bit, "fsdp") for block in wide]
    local = lax.all_gather(jnp.concatenate([down_grad, local], 1), "fsdp")
    out_up_sel = lax.dynamic_index_in_dim(out_up, ident, 0, keepdims=False)
    block_out = (hidden_f + valid * (out_ring.total() + nn(back_own[:, -rank:], out_up_sel))).astype(BF16)
    gained = in_ring.total() * gain_f
    input_grad = (
        cot_f
        + inverse * gained
        - hidden_f * inverse * inverse * inverse * jnp.mean(hidden_f * gained, axis=-1, keepdims=True)
    )

    lane = lax.broadcasted_iota(jnp.int32, (groups, adapters), 1)
    idents = jnp.sum(local[:, 0, -128 : -128 + adapters].astype(F32) * lane.astype(F32), axis=1).astype(jnp.int32)
    apart = jnp.asarray(swap_order(groups), jnp.int32)
    meta = jnp.concatenate([meta, idents, idents[jnp.bitwise_xor(group, apart)]])
    in_up_grad = place(meta, wide, adapters, 0, chans, parts, runs=2)
    out_down_grad = place(meta, wide, adapters, 2, chans, parts)
    first = 3 * chans // span
    out_up_grad = place(meta, wide, adapters, first, span, parts, every=share_of)
    in_down_grad, state_down_grad, step_up_grad, step_down_grad, state_up_grad = place_local(
        meta, local, adapters, (width, chans, chans, ranks, ranks + 2 * states)
    )
    return (
        block_out[None], input_grad[None], in_down_grad.transpose(0, 2, 1), in_up_grad,
        state_down_grad.transpose(0, 2, 1), state_up_grad, step_down_grad.transpose(0, 2, 1), step_up_grad,
        out_down_grad.transpose(0, 2, 1), out_up_grad,
    )


def solution(mesh):
    seq, rows = P("fsdp", "seq", None), P(("seq", "fsdp"), None)
    in_specs = (
        seq, P("fsdp"), P("fsdp"), P(), rows, rows, P(None, "seq"), P("seq"), P("seq", None), P(None, "seq"),
        P("seq"), P(None, "seq"), P("seq"), rows, P(), P(), P(None, "seq", None), P(), P(), P(None, None, "seq"),
        P(), P(), seq,
    )
    out_specs = (seq, seq, P(), P(), P(None, "seq", None), P(), P(), P(None, None, "seq"), P(), P())
    return jax.shard_map(body, mesh=mesh, in_specs=in_specs, out_specs=out_specs, check_vma=False)
```

```python
import functools
import jax
import jax.numpy as jnp
from jax import lax
from jax.experimental import pallas as pl
from jax.experimental.pallas import tpu as pltpu
from jax.sharding import PartitionSpec as P

F32 = jnp.float32
BF16 = jnp.bfloat16
LOG2E = 1.4426950408889634


def silu_grad(values):
    sigma = jax.nn.sigmoid(values)
    return sigma * (1.0 + values * (1.0 - sigma))


def softplus(v):
    return jnp.maximum(v, 0.0) + jnp.log1p(jnp.exp(-jnp.abs(v)))


def nt(left, right):
    return lax.dot_general(left, right, (((1,), (1,)), ((), ())), preferred_element_type=F32)


def nn(left, right):
    return jnp.dot(left, right, preferred_element_type=F32)


def tn(left, right):
    return lax.dot_general(left, right, (((0,), (0,)), ((), ())), preferred_element_type=F32)


def spread_matrix(states, sub):
    row = lax.broadcasted_iota(jnp.int32, (states, sub * states), 0)
    col = lax.broadcasted_iota(jnp.int32, (states, sub * states), 1)
    return (lax.rem(col, states) == row).astype(BF16)


def own_step_mask(rows, width, sub):
    row = lax.broadcasted_iota(jnp.int32, (rows, sub * width), 0)
    col = lax.broadcasted_iota(jnp.int32, (rows, sub * width), 1)
    return (lax.rem(row, sub) == lax.div(col, width)).astype(F32)


def ring_place(position, size):
    position = lax.rem(position + size, size)
    return jnp.where(position < size // 2, 2 * position, 2 * (size - 1 - position) + 1)


def ring_position(place, size):
    return jnp.where(lax.rem(place, 2) == 0, lax.div(place, 2), size - 1 - lax.div(place, 2))


def ring_copies(out_ref, pieces, part, sems):
    size, rows = len(pieces) - 1, pieces[0].shape[0]
    far, half, here = size // 2, rows // 2, ring_position(part, size)
    copies = []
    for i, piece in enumerate(pieces):
        hop = (i + 1) // 2
        place = ring_place(here - hop if i % 2 else here + hop, size)
        at = place * rows
        if i == size:
            at = ring_place(here + far, size) * rows + half
        at = pl.multiple_of(at, half)
        copies.append(pltpu.make_async_copy(piece, out_ref.at[pl.ds(at, piece.shape[0]), :], sems.at[i]))
    return copies


def swap_order(size):
    order, bit = [0], size // 2
    while bit:
        order += [at ^ bit for at in order]
        bit //= 2
    return order


def place_of_block(block, part, size):
    apart, out, bit = jnp.bitwise_xor(block, part), 0, size // 2
    weight = 1
    while bit:
        out = out + weight * jnp.bitwise_and(lax.div(apart, bit), 1)
        weight, bit = weight * 2, bit // 2
    return out


def row_copies(out_ref, pieces, group, sems):
    copies = []
    for i, apart in enumerate(swap_order(out_ref.shape[1])):
        at = i if group is None else jnp.bitwise_xor(group, apart)
        piece = pieces.at[i] if group is None else pieces[i]
        copies.append(pltpu.make_async_copy(piece, out_ref.at[:, at], sems.at[i]))
    return copies


def run_all(copies):
    for copy in copies:
        copy.start()
    for copy in copies:
        copy.wait()


def flat(ref):
    return ref[...].reshape(-1, ref.shape[-1])


def conv_before(x, before, weight_ref, bias_ref):
    taps = weight_ref.shape[0]
    padded = jnp.concatenate([before, x], 0)
    out = bias_ref[...]
    for tap in range(taps):
        at = before.shape[0] - (taps - 1 - tap)
        out = out + weight_ref[tap : tap + 1, :] * padded[at : at + x.shape[0]]
    return out


def project_kernel(meta, *refs, parts, groups):
    pieces, refs = refs[: parts + 1], refs[parts + 1 :]
    columns, refs = refs[:groups], refs[groups:]
    (in_down_ref, up_ref, weight_ref, bias_ref, proj_ref, down_ref,
     low_in_ref, x_ref, conv_ref, sums_ref, before, rows_s, whole_s, piece_sems, column_sems) = refs
    step = pl.program_id(0)
    rows = x_ref.shape[0]

    @pl.when(step == 0)
    def _():
        run_all(ring_copies(rows_s, pieces, meta[1], piece_sems) + row_copies(whole_s, columns, meta[2], column_sems))
        before[...] = jnp.zeros_like(before)

    normed = rows_s[pl.ds(pl.multiple_of(step * rows, rows), rows), :]
    low_in = nt(normed, in_down_ref[0]).astype(BF16)
    low_in_ref[...] = low_in
    x = (nn(normed, flat(whole_s)) + nn(low_in, up_ref[0])).astype(BF16)
    x_ref[...] = x
    x_f = x.astype(F32)
    conv_out = jax.nn.silu(conv_before(x_f, before[...], weight_ref, bias_ref)).astype(BF16)
    before[...] = x_f[-8:]
    conv_ref[...] = conv_out
    sums = jnp.concatenate([nt(proj_ref[...], conv_out), nt(down_ref[0], conv_out)], 0).astype(BF16)
    tokens = sums_ref.shape[2]
    for j in range(sums_ref.shape[0]):
        sums_ref[j] = sums[:, j * tokens : (j + 1) * tokens]


def once(array):
    return pl.BlockSpec(array.shape, lambda i, *_: (0,) * array.ndim, pipeline_mode=pl.Buffered(1))


def chosen(table, which=0, width=None):
    if width is None:
        return pl.BlockSpec((1,) + table.shape[1:], lambda i, meta: (meta[0], 0, 0))
    return pl.BlockSpec((1, table.shape[1], width), lambda i, meta: (meta[0], 0, meta[1] + which))


LIMIT = 58 << 20
AT_ONCE = 4


def gate_kernel(meta, *refs, parts):
    pieces, refs = refs[: parts + 1], refs[parts + 1 :]
    columns, low_in_ref, up_ref, z_ref, rows_s, whole_s, piece_sems, column_sems = refs
    step = pl.program_id(0)

    @pl.when(step == 0)
    def _():
        run_all(ring_copies(rows_s, pieces, meta[1], piece_sems) + row_copies(whole_s, columns, None, column_sems))

    rows = z_ref.shape[0]
    normed = rows_s[pl.ds(pl.multiple_of(step * rows, rows), rows), :]
    z_ref[...] = (nn(normed, flat(whole_s)) + nn(low_in_ref[...], up_ref[0])).astype(BF16)


def gate(meta, pieces, columns, low_in, up, parts, groups):
    tokens, width = pieces[0].shape
    length, chans = tokens * parts, columns.shape[-1]
    block = AT_ONCE * tokens
    seq = lambda size: pl.BlockSpec((block, size), lambda i, meta: (i, 0))
    return pl.pallas_call(
        functools.partial(gate_kernel, parts=parts),
        grid_spec=pltpu.PrefetchScalarGridSpec(
            num_scalar_prefetch=1,
            grid=(length // block,),
            in_specs=[pl.BlockSpec(memory_space=pl.ANY)] * (len(pieces) + 1)
            + [seq(low_in.shape[1]), chosen(up, parts, chans)],
            out_specs=seq(chans),
            scratch_shapes=[
                pltpu.VMEM((length, width), BF16), pltpu.VMEM((parts, groups) + columns.shape[2:], BF16),
                pltpu.SemaphoreType.DMA((len(pieces),)), pltpu.SemaphoreType.DMA((groups,)),
            ],
        ),
        out_shape=jax.ShapeDtypeStruct((length, chans), BF16),
        compiler_params=pltpu.CompilerParams(vmem_limit_bytes=LIMIT),
        name="gate",
    )(meta, *pieces, columns, low_in, up)


def back_gate_kernel(meta, *refs, parts):
    pieces, refs = refs[: parts + 1], refs[parts + 1 :]
    out_proj_ref, out_down_ref, out_up_ref, back_low_ref, cols_ref, grad_ref, rows_s, sems = refs
    step = pl.program_id(0)

    @pl.when(step == 0)
    def _():
        run_all(ring_copies(rows_s, pieces, meta[1], sems))

    block, span = cols_ref.shape
    at = pl.ds(pl.multiple_of(step * block, block), block)
    share_of = max(span * parts // rows_s.shape[1], 1)
    cols_ref[...] = rows_s[at, pl.ds(pl.multiple_of(lax.div(meta[1], share_of) * span, span), span)]
    rows = rows_s[at, :]
    back_low = nt(rows, out_up_ref[0]).astype(BF16)
    back_low_ref[...] = back_low
    grad_ref[...] = (nt(rows, out_proj_ref[...]) + nn(back_low, out_down_ref[0])).astype(BF16)


def back_gate(meta, pieces, out_proj, out_down, out_up, parts):
    tokens, width = pieces[0].shape
    chans, rank, block, length = out_proj.shape[0], out_up.shape[1], AT_ONCE * tokens, tokens * parts
    span = max(width // parts, 128)
    seq = lambda size: pl.BlockSpec((block, size), lambda i, meta: (i, 0))
    return pl.pallas_call(
        functools.partial(back_gate_kernel, parts=parts),
        grid_spec=pltpu.PrefetchScalarGridSpec(
            num_scalar_prefetch=1,
            grid=(length // block,),
            in_specs=[pl.BlockSpec(memory_space=pl.ANY)] * len(pieces)
            + [once(out_proj), chosen(out_down, 0, chans), chosen(out_up)],
            out_specs=[seq(rank), seq(span), seq(chans)],
            scratch_shapes=[pltpu.VMEM((length, width), BF16), pltpu.SemaphoreType.DMA((len(pieces),))],
        ),
        out_shape=[jax.ShapeDtypeStruct((length, size), BF16) for size in (rank, span, chans)],
        compiler_params=pltpu.CompilerParams(vmem_limit_bytes=LIMIT),
        name="back_gate",
    )(meta, *pieces, out_proj, out_down, out_up)


def project(meta, pieces, columns, in_down, up, weight, bias, proj, down, parts, groups):
    tokens, width = pieces[0].shape
    length, chans, rank = tokens * parts, columns[0].shape[-1], in_down.shape[1]
    cols = proj.shape[0] + rank
    once_rows = AT_ONCE // 2
    seq = lambda size: pl.BlockSpec((once_rows * tokens, size), lambda i, meta: (i, 0))
    rows = columns[0].shape[1]
    whole_shape = (parts, groups, rows, chans)
    return pl.pallas_call(
        functools.partial(project_kernel, parts=parts, groups=groups),
        grid_spec=pltpu.PrefetchScalarGridSpec(
            num_scalar_prefetch=1,
            grid=(parts // once_rows,),
            in_specs=[pl.BlockSpec(memory_space=pl.ANY)] * (len(pieces) + groups)
            + [chosen(in_down), chosen(up, 0, chans), once(weight), once(bias), once(proj), chosen(down)],
            out_specs=[
                seq(rank), seq(chans), seq(chans), pl.BlockSpec((once_rows, cols, tokens), lambda i, meta: (i, 0, 0))
            ],
            scratch_shapes=[
                pltpu.VMEM((8, chans), F32), pltpu.VMEM((length, width), BF16), pltpu.VMEM(whole_shape, BF16),
                pltpu.SemaphoreType.DMA((len(pieces),)), pltpu.SemaphoreType.DMA((groups,)),
            ],
        ),
        out_shape=[jax.ShapeDtypeStruct((length, size), BF16) for size in (rank, chans, chans)]
        + [jax.ShapeDtypeStruct((parts, cols, tokens), BF16)],
        compiler_params=pltpu.CompilerParams(vmem_limit_bytes=LIMIT),
        name="project",
    )(meta, *pieces, *columns, in_down, up, weight, bias, proj, down)


def share_kernel(meta, got_ref, state_up_ref, step_down_ref, out_ref, *, ranks, states):
    sums = got_ref[0].astype(F32)
    for i in range(1, got_ref.shape[0]):
        sums = sums + got_ref[i].astype(F32)
    sums = sums.T
    cut = ranks + 2 * states
    low_state = sums[:, cut:].astype(BF16)
    mixed = sums[:, :cut] + nn(low_state, state_up_ref[0])
    step_low = mixed[:, :ranks].astype(BF16)
    step_mid = nt(step_low, step_down_ref[0]).astype(BF16)
    out_ref[...] = jnp.concatenate([step_low, step_mid, mixed[:, ranks:].astype(BF16), low_state], 1)


def share(meta, got, state_up, step_down, ranks, states):
    tokens, rank = got.shape[2], step_down.shape[1]
    cols = ranks + 2 * rank + 2 * states
    return pl.pallas_call(
        functools.partial(share_kernel, ranks=ranks, states=states),
        grid_spec=pltpu.PrefetchScalarGridSpec(
            num_scalar_prefetch=1,
            grid=(1,),
            in_specs=[once(got), chosen(state_up), chosen(step_down)],
            out_specs=pl.BlockSpec((tokens, cols), lambda i, meta: (0, 0)),
        ),
        out_shape=jax.ShapeDtypeStruct((tokens, cols), BF16),
        name="share",
    )(meta, got, state_up, step_down)


def share_back_kernel(meta, got_ref, step_down_ref, out_ref, *, ranks, states):
    sums = got_ref[0].astype(F32)
    for i in range(1, got_ref.shape[0]):
        sums = sums + got_ref[i].astype(F32)
    sums = sums.T
    rank = step_down_ref.shape[1]
    mid, end = ranks + rank, ranks + rank + 2 * states
    back_mid = sums[:, ranks:mid]
    down = step_down_ref[0].astype(F32)
    back_step = sums[:, :ranks] + jnp.dot(back_mid, down, precision=lax.Precision.HIGHEST, preferred_element_type=F32)
    out_ref[...] = jnp.concatenate([back_step, sums[:, mid:end], back_mid, sums[:, end:]], 1).astype(BF16)


def share_back(meta, got, step_down, ranks, states):
    cols, tokens = got.shape[1:]
    return pl.pallas_call(
        functools.partial(share_back_kernel, ranks=ranks, states=states),
        grid_spec=pltpu.PrefetchScalarGridSpec(
            num_scalar_prefetch=1,
            grid=(1,),
            in_specs=[once(got), chosen(step_down)],
            out_specs=pl.BlockSpec((tokens, cols), lambda i, meta: (0, 0)),
        ),
        out_shape=jax.ShapeDtypeStruct((tokens, cols), BF16),
        name="share_back",
    )(meta, got, step_down)


def columns_of_groups(values, ref, sub):
    turned = values.astype(F32).T
    for k in range(ref.shape[0]):
        ref[k] = turned[:, k * sub : (k + 1) * sub]


def scan_kernel(
    meta, shared_ref, u_ref, z_ref, bg_ref, step_proj_ref, step_up_ref, bias_ref, rate_ref, decay_ref, skip_ref, down_ref,
    gated_ref, pre_ref, conv_ref, bz_ref, mixed_ref,
    carry, states_s, pre_s, delta_s, du_s, scanned_s, bs_s, wide_s, w_s, bd_s, bb_s, bc_s, turned_s, held_a, held_b,
    q_a, q_b, *, sub, ranks,
):
    rows, chans = u_ref.shape
    parts, tokens = shared_ref.shape[:2]
    per = rows // tokens
    states, rank = rate_ref.shape[0], step_up_ref.shape[1]
    step = pl.program_id(0)
    blocks = pl.num_programs(0) // 2
    block = jnp.where(step < blocks, step, 2 * blocks - 1 - step)
    origin = pl.multiple_of(block * rows, rows)
    here = pl.ds(origin, rows)
    shared = jnp.concatenate(
        [shared_ref[place_of_block(block * per + j, meta[1], parts)] for j in range(per)], 0
    )
    b_rows = shared[:, ranks + rank : ranks + rank + states]
    c_rows = shared[:, ranks + rank + states : ranks + rank + 2 * states]
    rate = rate_ref[...]
    pairs = rows // (2 * sub)

    @pl.when(step < blocks)
    def _():
        @pl.when(step == 0)
        def _():
            carry[...] = jnp.zeros_like(carry)
            held_b[...] = jnp.zeros_like(held_b)
            states_s[:states, :] = jnp.zeros((states, chans), BF16)
            wide_s[:sub, :] = jnp.zeros((sub, sub * states), BF16)

        pre = nn(shared[:, :ranks], step_proj_ref[...]) + nn(shared[:, ranks : ranks + rank], step_up_ref[0]) + bias_ref[...]
        delta = softplus(pre)
        pre_s[here, :] = pre
        delta_s[here, :] = delta
        du_s[here, :] = delta * u_ref[...].astype(F32)
        columns_of_groups(b_rows, turned_s, sub)
        spread = nn(c_rows, spread_matrix(states, sub)) * own_step_mask(rows, states, sub)
        wide_s[sub:, :] = spread.astype(BF16)

        def pair(k, s):
            for turn, (mine, other) in enumerate(((held_a, held_b), (held_b, held_a))):
                base = pl.multiple_of(k * (2 * sub) + turn * sub, sub)
                w_s[pl.ds(base, sub), :] = nn(wide_s[pl.ds(base, sub), :], other[...])
                bt = turned_s[k * 2 + turn]
                for t in range(sub):
                    dl = delta_s[pl.ds(origin + base + t, 1), :]
                    du = du_s[pl.ds(origin + base + t, 1), :]
                    s = jnp.exp2(dl * rate) * s + du * bt[:, t : t + 1]
                    low = s.astype(BF16)
                    mine[t * states : (t + 1) * states, :] = low
                    states_s[pl.ds(pl.multiple_of((origin + base + t + 1) * states, states), states), :] = low
            return s

        carry[...] = lax.fori_loop(0, pairs, pair, carry[...])
        w_s[rows:, :] = nn(wide_s[rows:, :], held_b[...])
        scanned = w_s[sub:, :] + skip_ref[...] * u_ref[...].astype(F32)
        scanned_s[here, :] = scanned
        gated_ref[...] = (scanned * jax.nn.silu(z_ref[...].astype(F32))).astype(BF16)

    @pl.when(step >= blocks)
    def _():
        @pl.when(step == blocks)
        def _():
            carry[...] = jnp.zeros_like(carry)
            for ref in (held_a, q_a):
                ref[...] = jnp.zeros_like(ref)
            wide_s[rows:, :] = jnp.zeros((sub, sub * states), BF16)
            du_s[pl.ds(blocks * rows, sub), :] = jnp.zeros((sub, chans), F32)

        z = z_ref[...].astype(F32)
        bg = bg_ref[...].astype(F32)
        sigma = jax.nn.sigmoid(z)
        bs_s[...] = bg * (z * sigma)
        bz_ref[...] = (bg * scanned_s[here, :] * (sigma * (1.0 + z * (1.0 - sigma)))).astype(BF16)
        columns_of_groups(c_rows, turned_s, sub)
        spread = nn(b_rows, spread_matrix(states, sub)) * own_step_mask(rows, states, sub)
        wide_s[:rows, :] = spread.astype(BF16)
        ones = own_step_mask(sub, states, sub).astype(BF16)
        col = lax.broadcasted_iota(jnp.int32, (states, sub), 1)
        decay = decay_ref[...]

        def diagonal(wide):
            out = wide[:states]
            for t in range(1, sub):
                out = jnp.where(col == t, wide[t * states : (t + 1) * states], out)
            return out

        def sums(at, k, g_ref, q_ref):
            w_s[pl.ds(at, sub), :] = nn(wide_s[pl.ds(at, sub), :], g_ref[...])
            bd_s[pl.ds(at, sub), :] = nn(ones, q_ref[...])
            bb_s[k] = diagonal(nt(g_ref[...], du_s[pl.ds(pl.multiple_of(origin + at, sub), sub), :].astype(BF16)))

        def pair(i, h):
            for turn, (g_mine, q_mine, g_other, q_other) in enumerate(
                ((held_b, q_b, held_a, q_a), (held_a, q_a, held_b, q_b))
            ):
                k = (pairs - 1 - i) * 2 + 1 - turn
                base = pl.multiple_of(k * sub, sub)
                sums(pl.multiple_of(base + sub, sub), k + 1, g_other, q_other)
                kept = states_s[pl.ds(pl.multiple_of((origin + base + 1) * states, states), sub * states), :]
                bc_s[k] = diagonal(nt(kept, bs_s[pl.ds(base, sub), :].astype(BF16)))
                ct = turned_s[k]
                for t in range(sub - 1, -1, -1):
                    dl = delta_s[pl.ds(origin + base + t, 1), :]
                    bs = bs_s[pl.ds(base + t, 1), :]
                    g = bs * ct[:, t : t + 1] + h
                    h = g * jnp.exp2(dl * rate)
                    before = states_s[pl.ds(pl.multiple_of((origin + base + t) * states, states), states), :]
                    g_mine[t * states : (t + 1) * states, :] = g.astype(BF16)
                    q_mine[t * states : (t + 1) * states, :] = h.astype(BF16) * (decay * before)
            return h

        carry[...] = lax.fori_loop(0, pairs, pair, carry[...])
        sums(0, 0, held_a, q_a)
        w = w_s[:rows, :]
        conv_ref[...] = w * delta_s[here, :] + skip_ref[...] * bs_s[...]
        back_delta = bd_s[:rows, :] + w * u_ref[...].astype(F32)
        back_pre = (back_delta * jax.nn.sigmoid(pre_s[here, :])).astype(BF16)
        pre_ref[...] = back_pre
        gated_low = nt(down_ref[0], gated_block(scanned_s[here, :], z))
        mixed = [nt(step_proj_ref[...], back_pre), nt(step_up_ref[0], back_pre)]
        mixed += [jnp.concatenate([ref[k] for k in range(rows // sub)], 1) for ref in (bb_s, bc_s)]
        mixed = jnp.concatenate(mixed + [gated_low], 0).astype(BF16)
        for j in range(per):
            mixed_ref[j] = mixed[:, j * tokens : (j + 1) * tokens]


def gated_block(scanned, z):
    return (scanned * jax.nn.silu(z)).astype(BF16)


def scan(meta, shared, u, z, bg, step_proj, step_up, bias, rate, decay, skip, out_down, parts, sub):
    length, chans = u.shape
    tokens = length // parts
    block = 2 * tokens
    blocks = length // block
    states, rank, ranks = rate.shape[0], step_up.shape[1], step_proj.shape[0]
    cols = ranks + 2 * rank + 2 * states
    mirrored = lambda i: jnp.where(i < blocks, i, 2 * blocks - 1 - i)
    back = lambda i: jnp.where(i < blocks, blocks - 1, 2 * blocks - 1 - i)
    both = pl.BlockSpec((block, chans), lambda i, meta: (mirrored(i), 0))
    first = pl.BlockSpec((block, chans), lambda i, meta: (jnp.minimum(i, blocks - 1), 0))
    second = pl.BlockSpec((block, chans), lambda i, meta: (back(i), 0))
    return pl.pallas_call(
        functools.partial(scan_kernel, sub=sub, ranks=ranks),
        grid_spec=pltpu.PrefetchScalarGridSpec(
            num_scalar_prefetch=1,
            grid=(2 * blocks,),
            in_specs=[
                once(shared), both, both, second, once(step_proj), chosen(step_up), once(bias), once(rate), once(decay),
                once(skip), chosen(out_down, 0, chans),
            ],
            out_specs=[
                first, second, second, second,
                pl.BlockSpec((2, cols, tokens), lambda i, meta: (back(i), 0, 0)),
            ],
            scratch_shapes=[
                pltpu.VMEM((states, chans), F32),
                pltpu.VMEM(((length + 1) * states, chans), BF16),
                pltpu.VMEM((length, chans), F32),
                pltpu.VMEM((length, chans), F32),
                pltpu.VMEM((length + sub, chans), F32),
                pltpu.VMEM((length, chans), F32),
                pltpu.VMEM((block, chans), F32),
                pltpu.VMEM((block + sub, sub * states), BF16),
                pltpu.VMEM((block + sub, chans), F32),
                pltpu.VMEM((block + sub, chans), F32),
                pltpu.VMEM((block // sub + 1, states, sub), F32),
                pltpu.VMEM((block // sub, states, sub), F32),
                pltpu.VMEM((block // sub, states, sub), F32),
                pltpu.VMEM((sub * states, chans), BF16),
                pltpu.VMEM((sub * states, chans), BF16),
                pltpu.VMEM((sub * states, chans), BF16),
                pltpu.VMEM((sub * states, chans), BF16),
            ],
        ),
        out_shape=[
            jax.ShapeDtypeStruct((length, chans), BF16),
            jax.ShapeDtypeStruct((length, chans), BF16),
            jax.ShapeDtypeStruct((length, chans), F32),
            jax.ShapeDtypeStruct((length, chans), BF16),
            jax.ShapeDtypeStruct((parts, cols, tokens), BF16),
        ],
        compiler_params=pltpu.CompilerParams(vmem_limit_bytes=LIMIT),
        name="scan",
    )(meta, shared, u, z, bg, step_proj, step_up, bias, rate, decay, skip, out_down)


def finish_kernel(
    meta, *refs, ranks, states, parts, groups,
):
    pieces, refs = refs[: parts + 1], refs[parts + 1 :]
    columns_x, columns_z, refs = refs[:groups], refs[groups], refs[groups + 1 :]
    (back_ref, shared_ref, conv_grad_ref, back_z_ref, back_pre_ref, x_ref, x_before_ref, u_ref, low_in_ref,
     gated_ref, back_low_ref, cols_ref, up_x_ref, up_z_ref, proj_ref, down_ref,
     state_up_ref, in_down_ref, weight_ref, bias_ref,
     parts_ref, wide_ref, local_ref,
     after, sums_s, down_s, local_s, rows_s, whole_x, whole_z, piece_sems, x_sems, z_sems) = refs
    copies = (
        ring_copies(rows_s, pieces, meta[1], piece_sems)
        + row_copies(whole_x, columns_x, meta[2], x_sems)
        + row_copies(whole_z, columns_z, None, z_sems)
    )
    step = pl.program_id(0)
    steps = pl.num_programs(0)
    rows, chans = u_ref.shape
    rank = state_up_ref.shape[1]
    taps = weight_ref.shape[0]
    mixes = ranks + 2 * states

    @pl.when(step == 0)
    def _():
        for copy in copies:
            copy.start()
        after[...] = jnp.zeros_like(after)
        sums_s[...] = jnp.zeros_like(sums_s)
        down_s[...] = jnp.zeros_like(down_s)
        local_s[...] = jnp.zeros_like(local_s)

    per = rows // back_ref.shape[1]
    places = [place_of_block((steps - 1 - step) * per + j, meta[1], parts) for j in range(per)]
    back = jnp.concatenate([back_ref[place] for place in places], 0)
    shared = jnp.concatenate([shared_ref[place] for place in places], 0)
    u = u_ref[...]
    mixed = back[:, :mixes]
    back_low_state = nt(mixed, state_up_ref[0]).astype(BF16)
    grad = conv_grad_ref[...] + nn(mixed, proj_ref[...]) + nn(back_low_state, down_ref[0])
    keep = jnp.where(step == steps - 1, 0.0, 1.0)
    conv_pre = conv_before(x_ref[...].astype(F32), x_before_ref[...].astype(F32) * keep, weight_ref, bias_ref)
    grad = grad * silu_grad(conv_pre)
    padded = jnp.concatenate([grad, after[...]], 0)
    back_x = weight_ref[taps - 1 : taps, :] * grad
    for tap in range(taps - 1):
        at = taps - 1 - tap
        back_x = back_x + weight_ref[tap : tap + 1, :] * padded[at : at + rows]
    after[...] = grad[:8]
    back_x, back_z = back_x.astype(BF16), back_z_ref[...]

    @pl.when(step == 0)
    def _():
        for copy in copies:
            copy.wait()

    normed = rows_s[pl.ds(pl.multiple_of((steps - 1 - step) * rows, rows), rows), :]
    back_low_in = (nt(back_x, up_x_ref[0]) + nt(back_z, up_z_ref[0])).astype(BF16)
    parts_ref[...] = (
        nt(back_x, flat(whole_x)) + nt(back_z, flat(whole_z)) + nn(back_low_in, in_down_ref[0])
    ).astype(BF16)
    down_s[...] += tn(back_low_in, normed)
    low_in = low_in_ref[...]
    sums_s[:, :chans] += tn(low_in, back_x)
    sums_s[:, chans : 2 * chans] += tn(low_in, back_z)
    sums_s[:, 2 * chans : 3 * chans] += tn(back_low_ref[...], gated_ref[...])
    sums_s[:, 3 * chans :] += tn(back[:, mixes + rank :], cols_ref[...])
    local_s[:, :chans] += tn(back_low_state, u)
    local_s[:, chans : 2 * chans] += tn(shared[:, ranks : ranks + rank], back_pre_ref[...])
    local_s[:, 2 * chans : 2 * chans + ranks] += tn(back[:, mixes : mixes + rank], shared[:, :ranks])
    at = 2 * chans + ranks
    local_s[:, at : at + mixes] += tn(shared[:, ranks + rank + 2 * states :], mixed)

    @pl.when(step == steps - 1)
    def _():
        for values, ref, first in (
            (sums_s, wide_ref, 0), (down_s, wide_ref, sums_s.shape[1] // 128), (local_s, local_ref, 0)
        ):
            for j in range(values.shape[1] // 128):
                ref[first + j] = values[:, j * 128 : (j + 1) * 128].astype(BF16)
        lane = lax.broadcasted_iota(jnp.int32, (rank, 128), 1)
        local_ref[local_ref.shape[0] - 1] = (lane == meta[0]).astype(BF16)


def finish(
    meta, pieces, columns_x, columns_z, back, shared, conv_grad, back_z, back_pre, x, u, low_in, gated, back_low, cols, up,
    proj, down, state_up, in_down, weight, bias, parts, groups, states,
):
    length, chans = u.shape
    block, rank, span = AT_ONCE * length // parts, low_in.shape[1], cols.shape[1]
    mixes = proj.shape[0]
    ranks = mixes - 2 * states
    width = pieces[0].shape[1]
    whole_shape = (parts, groups) + columns_x[0].shape[1:]
    end = length // block - 1
    seq = lambda size: pl.BlockSpec((block, size), lambda i, meta: (end - i, 0))
    wide = 3 * chans + span
    local = 2 * chans + ranks + 2 * 128
    chunks = ((wide + width) // 128, local // 128 + 1)
    fixed = lambda count: pl.BlockSpec((count, rank, 128), lambda i, meta: (0, 0, 0))
    return pl.pallas_call(
        functools.partial(finish_kernel, ranks=ranks, states=states, parts=parts, groups=groups),
        grid_spec=pltpu.PrefetchScalarGridSpec(
            num_scalar_prefetch=1,
            grid=(length // block,),
            in_specs=[pl.BlockSpec(memory_space=pl.ANY)] * (len(pieces) + groups + 1)
            + [
                once(back), once(shared), seq(chans), seq(chans), seq(chans), seq(chans),
                pl.BlockSpec((16, chans), lambda i, meta: (jnp.maximum((end - i) * (block // 16) - 1, 0), 0)),
                seq(chans), seq(rank), seq(chans), seq(rank), seq(span),
                chosen(up, 0, chans), chosen(up, parts, chans), once(proj), chosen(down), chosen(state_up),
                chosen(in_down), once(weight), once(bias),
            ],
            out_specs=[seq(width)] + [fixed(count) for count in chunks],
            scratch_shapes=[
                pltpu.VMEM((8, chans), F32), pltpu.VMEM((rank, wide), F32), pltpu.VMEM((rank, width), F32),
                pltpu.VMEM((rank, local), F32), pltpu.VMEM((length, width), BF16),
                pltpu.VMEM(whole_shape, BF16), pltpu.VMEM(whole_shape, BF16),
                pltpu.SemaphoreType.DMA((len(pieces),)), pltpu.SemaphoreType.DMA((groups,)),
                pltpu.SemaphoreType.DMA((groups,)),
            ],
        ),
        out_shape=[
            jax.ShapeDtypeStruct((length, width), BF16),
        ]
        + [jax.ShapeDtypeStruct((count, rank, 128), BF16) for count in chunks],
        compiler_params=pltpu.CompilerParams(vmem_limit_bytes=LIMIT),
        name="finish",
    )(
        meta, *pieces, *columns_x, columns_z, back, shared, conv_grad, back_z, back_pre, x, x, u, low_in, gated, back_low,
        cols, up, up, proj, down, state_up, in_down, weight, bias,
    )


def place_kernel(meta, *refs, groups, parts, chans, span, every, wide):
    values, outs = refs[:groups], refs[groups:]
    in_up_ref, out_down_ref, out_up_ref, in_down_ref, state_down_ref, step_up_ref, step_down_ref, state_up_ref = outs
    adapter = pl.program_id(0)
    uses = [meta[3 + g] == adapter for g in range(groups)]

    def put(ref, column, at, size=128):
        total = None
        for use, value in zip(uses, values):
            term = jnp.where(use, value[at].astype(F32), 0.0)
            total = term if total is None else total + term
        ref[0, :, column : column + size] = total[:, :size]

    inner = parts * chans
    for p in range(parts):
        at = place_of_block(p, meta[1], parts) * wide
        for j in range(chans // 128):
            put(in_up_ref, p * chans + j * 128, at + j)
            put(in_up_ref, inner + p * chans + j * 128, at + chans // 128 + j)
            put(out_down_ref, p * chans + j * 128, at + 2 * (chans // 128) + j)
        if p % every == 0:
            for j in range(span // 128):
                put(out_up_ref, p // every * span + j * 128, at + 3 * (chans // 128) + j)
    at = parts * wide
    for ref in (in_down_ref, state_down_ref, step_up_ref, step_down_ref, state_up_ref):
        for j in range(pl.cdiv(ref.shape[2], 128)):
            put(ref, j * 128, at, min(128, ref.shape[2] - j * 128))
            at += 1


def place(meta, values, adapters, parts, chans, span, width, wide, ranks, mixes):
    groups, rank = len(values), values[0].shape[1]
    every = max(span * parts // width, 1)
    sizes = (2 * parts * chans, parts * chans, width, width, chans, chans, ranks, mixes)
    return pl.pallas_call(
        functools.partial(place_kernel, groups=groups, parts=parts, chans=chans, span=span, every=every, wide=wide),
        grid_spec=pltpu.PrefetchScalarGridSpec(
            num_scalar_prefetch=1,
            grid=(adapters,),
            in_specs=[once(value) for value in values],
            out_specs=[pl.BlockSpec((1, rank, size), lambda i, meta: (i, 0, 0)) for size in sizes],
        ),
        out_shape=[jax.ShapeDtypeStruct((adapters, rank, size), F32) for size in sizes],
        compiler_params=pltpu.CompilerParams(vmem_limit_bytes=16 << 20),
        name="place",
    )(meta, *values)


def split_kernel(values_ref, out_ref):
    chans = out_ref.shape[2]
    for i in range(out_ref.shape[0]):
        out_ref[i] = values_ref[:, i * chans : (i + 1) * chans]


def split_columns(values, parts):
    rows, cols = values.shape
    return pl.pallas_call(
        split_kernel, out_shape=jax.ShapeDtypeStruct((parts, rows, cols // parts), values.dtype), name="split_columns"
    )(values)


EPS = 1e-05


def ring_send(value, size, hop, axis):
    order = list(range(0, size, 2)) + list(range(1, size, 2))[::-1]
    pairs = [(order[i], order[(i + hop) % size]) for i in range(size)]
    return lax.ppermute(value, axis, pairs)


class RingGather:
    def __init__(self, own, size, axis):
        self.size, self.axis, self.rows, self.done = size, axis, own.shape[0], 0
        self.pieces = [own]
        self.ends = (own, own)

    def advance(self, hops):
        far, half = self.size // 2, self.rows // 2
        for _ in range(min(hops, far - self.done)):
            self.done += 1
            ahead, back = self.ends
            if self.done == far:
                ahead, back = ahead[:half], back[half:]
            self.ends = (ring_send(ahead, self.size, 1, self.axis), ring_send(back, self.size, -1, self.axis))
            self.pieces += list(self.ends)

    def all_pieces(self):
        self.advance(self.size)
        return self.pieces


class RingScatter:
    def __init__(self, partial, size, axis):
        self.partial, self.size, self.axis, self.done = partial, size, axis, 0
        self.rows = partial.shape[0] // size
        self.position = ring_position(lax.axis_index(axis), size)
        self.ends = None

    def block(self, offset, start=0, rows=None):
        at = ring_place(self.position + offset, self.size) * self.rows + start
        return lax.dynamic_slice_in_dim(self.partial, at, rows or self.rows, 0)

    def advance(self, hops):
        far, half = self.size // 2, self.rows // 2
        for _ in range(min(hops, far - self.done)):
            left = far - self.done
            if left == far:
                mine, other = self.block(far, 0, half), self.block(far, half, half)
            else:
                mine, other = self.block(left).astype(F32), self.block(-left).astype(F32)
                ahead, back = (end.astype(F32) for end in self.ends)
                if left == far - 1:
                    blank = jnp.zeros_like(ahead)
                    ahead, back = jnp.concatenate([ahead, blank], 0), jnp.concatenate([blank, back], 0)
                mine, other = (mine + ahead).astype(BF16), (other + back).astype(BF16)
            self.ends = (
                ring_send(mine, self.size, 1, self.axis),
                ring_send(other, self.size, -1, self.axis),
            )
            self.done += 1

    def total(self):
        self.advance(self.size)
        return self.block(0).astype(F32) + self.ends[0].astype(F32) + self.ends[1].astype(F32)


def together(*values):
    return lax.optimization_barrier(values)


def swap(value, size, bit, axis):
    return lax.ppermute(value, axis, [(i, i ^ bit) for i in range(size)])


def bits_of(size):
    bit = size // 2
    while bit:
        yield bit
        bit //= 2


def swap_gather(own, size, axis):
    held = [own]
    for bit in bits_of(size):
        held += [swap(block, size, bit, axis) for block in held]
    return held


def small_gather(own, size, axis):
    held = own[None]
    for bit in bits_of(size):
        held = jnp.concatenate([held, swap(held, size, bit, axis)], 0)
    return held


def exchange(values, axis):
    return lax.all_to_all(values, axis, split_axis=0, concat_axis=0, tiled=True)


def body(
    hidden, lengths, adapter_ids, norm_gain, in_proj_x, in_proj_z, conv_weight, conv_bias, state_proj,
    step_proj, step_bias, decay_log, skip_gain, out_proj, in_down, in_up, state_down, state_up, step_down,
    step_up, out_down, out_up, cotangent,
):
    parts, groups = lax.axis_size("seq"), lax.axis_size("fsdp")
    part, group = lax.axis_index("seq"), lax.axis_index("fsdp")
    tokens, width = hidden.shape[1:]
    chans = conv_weight.shape[1]
    ranks = step_proj.shape[0]
    states = decay_log.shape[0]
    rank = in_down.shape[2]
    adapters = in_down.shape[0]
    ident = adapter_ids[0]
    sub = 16
    meta = jnp.stack([ident, part, group]).astype(jnp.int32)
    in_down, state_down, step_down, out_down = (
        table.transpose(0, 2, 1) for table in (in_down, state_down, step_down, out_down)
    )
    state_proj = state_proj.T

    hidden_f = hidden[0].astype(F32)
    gain_f = norm_gain.astype(F32)
    inverse = lax.rsqrt(jnp.mean(hidden_f * hidden_f, axis=-1, keepdims=True) + EPS)
    normed = (hidden_f * inverse * gain_f).astype(BF16)
    positions = part * tokens + lax.broadcasted_iota(jnp.int32, (tokens, 1), 0)
    valid = (positions < lengths[0]).astype(F32)
    cot_f = cotangent[0].astype(F32)
    back_out = (valid * cot_f).astype(BF16)
    conv_weight, conv_bias = conv_weight.astype(F32), conv_bias.astype(F32)[None]
    bias, skip = step_bias.astype(F32)[None], skip_gain.astype(F32)[None]
    decay = -jnp.exp(decay_log.astype(F32))
    rate, decay = decay * LOG2E, decay.astype(BF16)
    rows = in_proj_x.shape[0]

    def own_columns_of(weight):
        return lax.all_to_all(weight, "seq", split_axis=0, concat_axis=0, tiled=True)

    hops = max(parts // 8, 1)
    whole_out = lax.all_gather(out_proj, "fsdp", axis=0, tiled=True)
    ring = RingGather(normed, parts, "seq")
    ring.advance(hops)
    mine_x = own_columns_of(split_columns(in_proj_x, parts))
    small = (conv_weight, conv_bias, bias, skip, rate, decay, meta, split_columns(in_proj_z, parts))
    ring.ends, small = together(ring.ends, small)
    conv_weight, conv_bias, bias, skip, rate, decay, meta, in_proj_z = small
    pieces = ring.all_pieces()
    columns = swap_gather(mine_x, groups, "fsdp")

    pieces, columns, back_out, in_proj_z = together(pieces, columns, back_out, in_proj_z)
    cot_ring = RingGather(back_out, parts, "seq")
    cot_ring.advance(hops)
    mine_z = own_columns_of(in_proj_z)
    low_in, x, conv_out, sums = project(
        meta, pieces, columns, in_down, in_up, conv_weight, conv_bias, state_proj, state_down, parts, groups
    )
    sums, cot_ring.ends, mine_z = together(sums, cot_ring.ends, mine_z)
    cot_ring.advance(hops)
    columns_z = lax.all_gather(mine_z, "fsdp")
    sums = exchange(sums, "seq")
    sums, cot_ring.ends = together(sums, cot_ring.ends)
    cot_ring.advance(hops)
    shared = share(meta, sums, state_up, step_down, ranks, states)[None]
    z = back = None
    for i, bit in enumerate(bits_of(parts)):
        shared = jnp.concatenate([shared, swap(shared, parts, bit, "seq")], 0)
        if i == 0:
            shared, cot_ring.ends, columns_z = together(shared, cot_ring.ends, columns_z)
            cot_ring.advance(parts)
            z = gate(meta, pieces, columns_z, low_in, in_up, parts, groups)
        elif i == 1:
            shared, cot_ring.pieces, z = together(shared, cot_ring.pieces, z)
            back = back_gate(meta, cot_ring.pieces, whole_out, out_down, out_up, parts)
    back_low, cols, back_gated = back
    gated, back_pre, conv_grad, back_z, mixed = scan(
        meta, shared, conv_out, z, back_gated, step_proj, step_up, bias, rate, decay, skip, out_down, parts, sub
    )
    out_ring = RingScatter(nn(gated, whole_out).astype(BF16), parts, "seq")
    out_ring.advance(hops)
    back_own = share_back(meta, exchange(mixed, "seq"), step_down, ranks, states)
    back = back_own[None]
    for i, bit in enumerate(bits_of(parts)):
        back = jnp.concatenate([back, swap(back, parts, bit, "seq")], 0)
        if i % 2 == 0:
            back, out_ring.ends = together(back, out_ring.ends)
            out_ring.advance(hops)
    in_parts, wide, local = finish(
        meta, pieces, columns, columns_z, back, shared, conv_grad, back_z, back_pre, x, conv_out, low_in, gated, back_low,
        cols, in_up, state_proj, state_down, state_up, in_down, conv_weight, conv_bias, parts, groups, states,
    )
    in_parts, wide, local, out_ring.ends = together(in_parts, wide, local, out_ring.ends)
    out_ring.advance(parts)
    in_ring = RingScatter(in_parts, parts, "seq")
    held = wide[None]
    for bit in bits_of(parts):
        in_ring.advance(hops)
        held = jnp.concatenate([held, swap(held, parts, bit, "seq")], 0)
        held, in_ring.ends = together(held, in_ring.ends)
    in_ring.advance(parts)
    span = cols.shape[1]
    own = (3 * chans + span) // 128
    down_grad = held[:, own:].astype(F32).sum(0).astype(BF16)
    chunks = [jnp.concatenate([held[:, :own].reshape(parts * own, rank, 128), down_grad, local], 0)]
    first, *others = bits_of(groups)
    chunks += [swap(chunks[0], groups, first, "fsdp")]
    branch = out_ring.total()
    chunks, in_ring.ends, branch = together(chunks, in_ring.ends, branch)
    for bit in others:
        chunks += [swap(block, groups, bit, "fsdp") for block in chunks]
    out_up_sel = lax.dynamic_index_in_dim(out_up, ident, 0, keepdims=False)
    block_out = (hidden_f + valid * (branch + nn(back_own[:, -rank:], out_up_sel))).astype(BF16)
    gained = in_ring.total() * gain_f
    input_grad = (
        cot_f
        + inverse * gained
        - hidden_f * inverse * inverse * inverse * jnp.mean(hidden_f * gained, axis=-1, keepdims=True)
    )

    lane = lax.broadcasted_iota(jnp.int32, (groups, adapters), 1)
    picks = jnp.stack([block[-1, 0, :adapters] for block in chunks]).astype(F32)
    idents = jnp.sum(picks * lane.astype(F32), axis=1).astype(jnp.int32)
    (in_up_grad, out_down_grad, out_up_grad, in_down_grad, state_down_grad, step_up_grad, step_down_grad,
     state_up_grad) = place(
        jnp.concatenate([meta, idents]), chunks, adapters, parts, chans, span, width, own, ranks, ranks + 2 * states
    )
    return (
        block_out[None], input_grad[None], in_down_grad.transpose(0, 2, 1), in_up_grad,
        state_down_grad.transpose(0, 2, 1), state_up_grad, step_down_grad.transpose(0, 2, 1), step_up_grad,
        out_down_grad.transpose(0, 2, 1), out_up_grad,
    )


def solution(mesh):
    seq, rows = P("fsdp", "seq", None), P(("seq", "fsdp"), None)
    in_specs = (
        seq, P("fsdp"), P("fsdp"), P(), rows, rows, P(None, "seq"), P("seq"), P("seq", None), P(None, "seq"),
        P("seq"), P(None, "seq"), P("seq"), rows, P(), P(), P(None, "seq", None), P(), P(), P(None, None, "seq"),
        P(), P(), seq,
    )
    out_specs = (seq, seq, P(), P(), P(None, "seq", None), P(), P(), P(None, None, "seq"), P(), P())
    return jax.shard_map(body, mesh=mesh, in_specs=in_specs, out_specs=out_specs, check_vma=False)
```

```python
import functools
import jax
import jax.numpy as jnp
from jax import lax
from jax.experimental import pallas as pl
from jax.experimental.pallas import tpu as pltpu
from jax.sharding import PartitionSpec as P

F32 = jnp.float32
BF16 = jnp.bfloat16
LOG2E = 1.4426950408889634


def silu_grad(values):
    sigma = jax.nn.sigmoid(values)
    return sigma * (1.0 + values * (1.0 - sigma))


def softplus(v):
    return jnp.maximum(v, 0.0) + jnp.log1p(jnp.exp(-jnp.abs(v)))


def nt(left, right):
    return lax.dot_general(left, right, (((1,), (1,)), ((), ())), preferred_element_type=F32)


def nn(left, right):
    return jnp.dot(left, right, preferred_element_type=F32)


def tn(left, right):
    return lax.dot_general(left, right, (((0,), (0,)), ((), ())), preferred_element_type=F32)


def spread_matrix(states, sub):
    row = lax.broadcasted_iota(jnp.int32, (states, sub * states), 0)
    col = lax.broadcasted_iota(jnp.int32, (states, sub * states), 1)
    return (lax.rem(col, states) == row).astype(BF16)


def own_step_mask(rows, width, sub):
    row = lax.broadcasted_iota(jnp.int32, (rows, sub * width), 0)
    col = lax.broadcasted_iota(jnp.int32, (rows, sub * width), 1)
    return (lax.rem(row, sub) == lax.div(col, width)).astype(F32)


def ring_place(position, size):
    position = lax.rem(position + size, size)
    return jnp.where(position < size // 2, 2 * position, 2 * (size - 1 - position) + 1)


def ring_position(place, size):
    return jnp.where(lax.rem(place, 2) == 0, lax.div(place, 2), size - 1 - lax.div(place, 2))


def ring_copies(out_ref, pieces, part, sems):
    size, rows = len(pieces) - 1, pieces[0].shape[0]
    far, half, here = size // 2, rows // 2, ring_position(part, size)
    copies = []
    for i, piece in enumerate(pieces):
        hop = (i + 1) // 2
        place = ring_place(here - hop if i % 2 else here + hop, size)
        at = place * rows
        if i == size:
            at = ring_place(here + far, size) * rows + half
        at = pl.multiple_of(at, half)
        copies.append(pltpu.make_async_copy(piece, out_ref.at[pl.ds(at, piece.shape[0]), :], sems.at[i]))
    return copies


def swap_order(size):
    order, bit = [0], size // 2
    while bit:
        order += [at ^ bit for at in order]
        bit //= 2
    return order


def place_of_block(block, part, size):
    apart, out, bit = jnp.bitwise_xor(block, part), 0, size // 2
    weight = 1
    while bit:
        out = out + weight * jnp.bitwise_and(lax.div(apart, bit), 1)
        weight, bit = weight * 2, bit // 2
    return out


def row_copies(out_ref, pieces, group, sems):
    copies = []
    for i, apart in enumerate(swap_order(out_ref.shape[1])):
        at = i if group is None else jnp.bitwise_xor(group, apart)
        piece = pieces.at[i] if group is None else pieces[i]
        copies.append(pltpu.make_async_copy(piece, out_ref.at[:, at], sems.at[i]))
    return copies


def run_all(copies):
    for copy in copies:
        copy.start()
    for copy in copies:
        copy.wait()


def flat(ref):
    return ref[...].reshape(-1, ref.shape[-1])


def conv_before(x, before, weight_ref, bias_ref):
    taps = weight_ref.shape[0]
    padded = jnp.concatenate([before, x], 0)
    out = bias_ref[...]
    for tap in range(taps):
        at = before.shape[0] - (taps - 1 - tap)
        out = out + weight_ref[tap : tap + 1, :] * padded[at : at + x.shape[0]]
    return out


def project_kernel(meta, *refs, parts, groups):
    pieces, refs = refs[: parts + 1], refs[parts + 1 :]
    columns, refs = refs[:groups], refs[groups:]
    (in_down_ref, up_ref, weight_ref, bias_ref, proj_ref, down_ref,
     low_in_ref, x_ref, conv_ref, sums_ref, before, rows_s, whole_s, piece_sems, column_sems) = refs
    step = pl.program_id(0)
    rows = x_ref.shape[0]

    @pl.when(step == 0)
    def _():
        run_all(ring_copies(rows_s, pieces, meta[1], piece_sems) + row_copies(whole_s, columns, meta[2], column_sems))
        before[...] = jnp.zeros_like(before)

    normed = rows_s[pl.ds(pl.multiple_of(step * rows, rows), rows), :]
    low_in = nt(normed, in_down_ref[0]).astype(BF16)
    low_in_ref[...] = low_in
    x = (nn(normed, flat(whole_s)) + nn(low_in, up_ref[0])).astype(BF16)
    x_ref[...] = x
    x_f = x.astype(F32)
    conv_out = jax.nn.silu(conv_before(x_f, before[...], weight_ref, bias_ref)).astype(BF16)
    before[...] = x_f[-8:]
    conv_ref[...] = conv_out
    sums = jnp.concatenate([nt(proj_ref[...], conv_out), nt(down_ref[0], conv_out)], 0).astype(BF16)
    tokens = sums_ref.shape[2]
    for j in range(sums_ref.shape[0]):
        sums_ref[j] = sums[:, j * tokens : (j + 1) * tokens]


def once(array):
    return pl.BlockSpec(array.shape, lambda i, *_: (0,) * array.ndim, pipeline_mode=pl.Buffered(1))


def chosen(table, which=0, width=None):
    if width is None:
        return pl.BlockSpec((1,) + table.shape[1:], lambda i, meta: (meta[0], 0, 0))
    return pl.BlockSpec((1, table.shape[1], width), lambda i, meta: (meta[0], 0, meta[1] + which))


LIMIT = 58 << 20
AT_ONCE = 4


def gate_kernel(meta, *refs, parts):
    pieces, refs = refs[: parts + 1], refs[parts + 1 :]
    columns, low_in_ref, up_ref, z_ref, rows_s, whole_s, piece_sems, column_sems = refs
    step = pl.program_id(0)

    @pl.when(step == 0)
    def _():
        run_all(ring_copies(rows_s, pieces, meta[1], piece_sems) + row_copies(whole_s, columns, None, column_sems))

    rows = z_ref.shape[0]
    normed = rows_s[pl.ds(pl.multiple_of(step * rows, rows), rows), :]
    z_ref[...] = (nn(normed, flat(whole_s)) + nn(low_in_ref[...], up_ref[0])).astype(BF16)


def gate(meta, pieces, columns, low_in, up, parts, groups):
    tokens, width = pieces[0].shape
    length, chans = tokens * parts, columns.shape[-1]
    block = AT_ONCE * tokens
    seq = lambda size: pl.BlockSpec((block, size), lambda i, meta: (i, 0))
    return pl.pallas_call(
        functools.partial(gate_kernel, parts=parts),
        grid_spec=pltpu.PrefetchScalarGridSpec(
            num_scalar_prefetch=1,
            grid=(length // block,),
            in_specs=[pl.BlockSpec(memory_space=pl.ANY)] * (len(pieces) + 1)
            + [seq(low_in.shape[1]), chosen(up, parts, chans)],
            out_specs=seq(chans),
            scratch_shapes=[
                pltpu.VMEM((length, width), BF16), pltpu.VMEM((parts, groups) + columns.shape[2:], BF16),
                pltpu.SemaphoreType.DMA((len(pieces),)), pltpu.SemaphoreType.DMA((groups,)),
            ],
        ),
        out_shape=jax.ShapeDtypeStruct((length, chans), BF16),
        compiler_params=pltpu.CompilerParams(vmem_limit_bytes=LIMIT),
        name="gate",
    )(meta, *pieces, columns, low_in, up)


def back_gate_kernel(meta, *refs, parts):
    pieces, refs = refs[: parts + 1], refs[parts + 1 :]
    out_proj_ref, out_down_ref, out_up_ref, back_low_ref, cols_ref, grad_ref, rows_s, sems = refs
    step = pl.program_id(0)

    @pl.when(step == 0)
    def _():
        run_all(ring_copies(rows_s, pieces, meta[1], sems))

    block, span = cols_ref.shape
    at = pl.ds(pl.multiple_of(step * block, block), block)
    share_of = max(span * parts // rows_s.shape[1], 1)
    cols_ref[...] = rows_s[at, pl.ds(pl.multiple_of(lax.div(meta[1], share_of) * span, span), span)]
    rows = rows_s[at, :]
    back_low = nt(rows, out_up_ref[0]).astype(BF16)
    back_low_ref[...] = back_low
    grad_ref[...] = (nt(rows, out_proj_ref[...]) + nn(back_low, out_down_ref[0])).astype(BF16)


def back_gate(meta, pieces, out_proj, out_down, out_up, parts):
    tokens, width = pieces[0].shape
    chans, rank, block, length = out_proj.shape[0], out_up.shape[1], AT_ONCE * tokens, tokens * parts
    span = max(width // parts, 128)
    seq = lambda size: pl.BlockSpec((block, size), lambda i, meta: (i, 0))
    return pl.pallas_call(
        functools.partial(back_gate_kernel, parts=parts),
        grid_spec=pltpu.PrefetchScalarGridSpec(
            num_scalar_prefetch=1,
            grid=(length // block,),
            in_specs=[pl.BlockSpec(memory_space=pl.ANY)] * len(pieces)
            + [once(out_proj), chosen(out_down, 0, chans), chosen(out_up)],
            out_specs=[seq(rank), seq(span), seq(chans)],
            scratch_shapes=[pltpu.VMEM((length, width), BF16), pltpu.SemaphoreType.DMA((len(pieces),))],
        ),
        out_shape=[jax.ShapeDtypeStruct((length, size), BF16) for size in (rank, span, chans)],
        compiler_params=pltpu.CompilerParams(vmem_limit_bytes=LIMIT),
        name="back_gate",
    )(meta, *pieces, out_proj, out_down, out_up)


def project(meta, pieces, columns, in_down, up, weight, bias, proj, down, parts, groups):
    tokens, width = pieces[0].shape
    length, chans, rank = tokens * parts, columns[0].shape[-1], in_down.shape[1]
    cols = proj.shape[0] + rank
    once_rows = AT_ONCE // 2
    seq = lambda size: pl.BlockSpec((once_rows * tokens, size), lambda i, meta: (i, 0))
    rows = columns[0].shape[1]
    whole_shape = (parts, groups, rows, chans)
    return pl.pallas_call(
        functools.partial(project_kernel, parts=parts, groups=groups),
        grid_spec=pltpu.PrefetchScalarGridSpec(
            num_scalar_prefetch=1,
            grid=(parts // once_rows,),
            in_specs=[pl.BlockSpec(memory_space=pl.ANY)] * (len(pieces) + groups)
            + [chosen(in_down), chosen(up, 0, chans), once(weight), once(bias), once(proj), chosen(down)],
            out_specs=[
                seq(rank), seq(chans), seq(chans), pl.BlockSpec((once_rows, cols, tokens), lambda i, meta: (i, 0, 0))
            ],
            scratch_shapes=[
                pltpu.VMEM((8, chans), F32), pltpu.VMEM((length, width), BF16), pltpu.VMEM(whole_shape, BF16),
                pltpu.SemaphoreType.DMA((len(pieces),)), pltpu.SemaphoreType.DMA((groups,)),
            ],
        ),
        out_shape=[jax.ShapeDtypeStruct((length, size), BF16) for size in (rank, chans, chans)]
        + [jax.ShapeDtypeStruct((parts, cols, tokens), BF16)],
        compiler_params=pltpu.CompilerParams(vmem_limit_bytes=LIMIT),
        name="project",
    )(meta, *pieces, *columns, in_down, up, weight, bias, proj, down)


def share_kernel(meta, got_ref, state_up_ref, step_down_ref, out_ref, *, ranks, states):
    sums = got_ref[0].astype(F32)
    for i in range(1, got_ref.shape[0]):
        sums = sums + got_ref[i].astype(F32)
    sums = sums.T
    cut = ranks + 2 * states
    low_state = sums[:, cut:].astype(BF16)
    mixed = sums[:, :cut] + nn(low_state, state_up_ref[0])
    step_low = mixed[:, :ranks].astype(BF16)
    step_mid = nt(step_low, step_down_ref[0]).astype(BF16)
    out_ref[...] = jnp.concatenate([step_low, step_mid, mixed[:, ranks:].astype(BF16), low_state], 1)


def share(meta, got, state_up, step_down, ranks, states):
    tokens, rank = got.shape[2], step_down.shape[1]
    cols = ranks + 2 * rank + 2 * states
    return pl.pallas_call(
        functools.partial(share_kernel, ranks=ranks, states=states),
        grid_spec=pltpu.PrefetchScalarGridSpec(
            num_scalar_prefetch=1,
            grid=(1,),
            in_specs=[once(got), chosen(state_up), chosen(step_down)],
            out_specs=pl.BlockSpec((tokens, cols), lambda i, meta: (0, 0)),
        ),
        out_shape=jax.ShapeDtypeStruct((tokens, cols), BF16),
        name="share",
    )(meta, got, state_up, step_down)


def share_back_kernel(meta, got_ref, step_down_ref, out_ref, *, ranks, states):
    sums = got_ref[0].astype(F32)
    for i in range(1, got_ref.shape[0]):
        sums = sums + got_ref[i].astype(F32)
    sums = sums.T
    rank = step_down_ref.shape[1]
    mid, end = ranks + rank, ranks + rank + 2 * states
    back_mid = sums[:, ranks:mid]
    down = step_down_ref[0].astype(F32)
    back_step = sums[:, :ranks] + jnp.dot(back_mid, down, precision=lax.Precision.HIGHEST, preferred_element_type=F32)
    out_ref[...] = jnp.concatenate([back_step, sums[:, mid:end], back_mid, sums[:, end:]], 1).astype(BF16)


def share_back(meta, got, step_down, ranks, states):
    cols, tokens = got.shape[1:]
    return pl.pallas_call(
        functools.partial(share_back_kernel, ranks=ranks, states=states),
        grid_spec=pltpu.PrefetchScalarGridSpec(
            num_scalar_prefetch=1,
            grid=(1,),
            in_specs=[once(got), chosen(step_down)],
            out_specs=pl.BlockSpec((tokens, cols), lambda i, meta: (0, 0)),
        ),
        out_shape=jax.ShapeDtypeStruct((tokens, cols), BF16),
        name="share_back",
    )(meta, got, step_down)


def columns_of_groups(values, ref, sub):
    turned = values.astype(F32).T
    for k in range(ref.shape[0]):
        ref[k] = turned[:, k * sub : (k + 1) * sub]


def scan_kernel(
    meta, shared_ref, u_ref, z_ref, bg_ref, step_proj_ref, step_up_ref, bias_ref, rate_ref, decay_ref, skip_ref, down_ref,
    gated_ref, pre_ref, conv_ref, bz_ref, mixed_ref,
    carry, states_s, pre_s, delta_s, du_s, scanned_s, bs_s, wide_s, w_s, bd_s, bb_s, bc_s, turned_s, held_a, held_b,
    q_a, q_b, *, sub, ranks,
):
    rows, chans = u_ref.shape
    parts, tokens = shared_ref.shape[:2]
    per = rows // tokens
    states, rank = rate_ref.shape[0], step_up_ref.shape[1]
    step = pl.program_id(0)
    blocks = pl.num_programs(0) // 2
    block = jnp.where(step < blocks, step, 2 * blocks - 1 - step)
    origin = pl.multiple_of(block * rows, rows)
    here = pl.ds(origin, rows)
    shared = jnp.concatenate(
        [shared_ref[place_of_block(block * per + j, meta[1], parts)] for j in range(per)], 0
    )
    b_rows = shared[:, ranks + rank : ranks + rank + states]
    c_rows = shared[:, ranks + rank + states : ranks + rank + 2 * states]
    rate = rate_ref[...]
    pairs = rows // (2 * sub)

    @pl.when(step < blocks)
    def _():
        @pl.when(step == 0)
        def _():
            carry[...] = jnp.zeros_like(carry)
            held_b[...] = jnp.zeros_like(held_b)
            states_s[:states, :] = jnp.zeros((states, chans), BF16)
            wide_s[:sub, :] = jnp.zeros((sub, sub * states), BF16)

        pre = nn(shared[:, :ranks], step_proj_ref[...]) + nn(shared[:, ranks : ranks + rank], step_up_ref[0]) + bias_ref[...]
        delta = softplus(pre)
        pre_s[here, :] = pre
        delta_s[here, :] = delta
        du_s[here, :] = delta * u_ref[...].astype(F32)
        columns_of_groups(b_rows, turned_s, sub)
        spread = nn(c_rows, spread_matrix(states, sub)) * own_step_mask(rows, states, sub)
        wide_s[sub:, :] = spread.astype(BF16)

        def pair(k, s):
            for turn, (mine, other) in enumerate(((held_a, held_b), (held_b, held_a))):
                base = pl.multiple_of(k * (2 * sub) + turn * sub, sub)
                w_s[pl.ds(base, sub), :] = nn(wide_s[pl.ds(base, sub), :], other[...])
                bt = turned_s[k * 2 + turn]
                for t in range(sub):
                    dl = delta_s[pl.ds(origin + base + t, 1), :]
                    du = du_s[pl.ds(origin + base + t, 1), :]
                    s = jnp.exp2(dl * rate) * s + du * bt[:, t : t + 1]
                    low = s.astype(BF16)
                    mine[t * states : (t + 1) * states, :] = low
                    states_s[pl.ds(pl.multiple_of((origin + base + t + 1) * states, states), states), :] = low
            return s

        carry[...] = lax.fori_loop(0, pairs, pair, carry[...])
        w_s[rows:, :] = nn(wide_s[rows:, :], held_b[...])
        scanned = w_s[sub:, :] + skip_ref[...] * u_ref[...].astype(F32)
        scanned_s[here, :] = scanned
        gated_ref[...] = (scanned * jax.nn.silu(z_ref[...].astype(F32))).astype(BF16)

    @pl.when(step >= blocks)
    def _():
        @pl.when(step == blocks)
        def _():
            carry[...] = jnp.zeros_like(carry)
            for ref in (held_a, q_a):
                ref[...] = jnp.zeros_like(ref)
            wide_s[rows:, :] = jnp.zeros((sub, sub * states), BF16)
            du_s[pl.ds(blocks * rows, sub), :] = jnp.zeros((sub, chans), F32)

        z = z_ref[...].astype(F32)
        bg = bg_ref[...].astype(F32)
        sigma = jax.nn.sigmoid(z)
        bs_s[...] = bg * (z * sigma)
        bz_ref[...] = (bg * scanned_s[here, :] * (sigma * (1.0 + z * (1.0 - sigma)))).astype(BF16)
        columns_of_groups(c_rows, turned_s, sub)
        spread = nn(b_rows, spread_matrix(states, sub)) * own_step_mask(rows, states, sub)
        wide_s[:rows, :] = spread.astype(BF16)
        ones = own_step_mask(sub, states, sub).astype(BF16)
        col = lax.broadcasted_iota(jnp.int32, (states, sub), 1)
        decay = decay_ref[...]

        def diagonal(wide):
            out = wide[:states]
            for t in range(1, sub):
                out = jnp.where(col == t, wide[t * states : (t + 1) * states], out)
            return out

        def sums(at, k, g_ref, q_ref):
            w_s[pl.ds(at, sub), :] = nn(wide_s[pl.ds(at, sub), :], g_ref[...])
            bd_s[pl.ds(at, sub), :] = nn(ones, q_ref[...])
            bb_s[k] = diagonal(nt(g_ref[...], du_s[pl.ds(pl.multiple_of(origin + at, sub), sub), :].astype(BF16)))

        def pair(i, h):
            for turn, (g_mine, q_mine, g_other, q_other) in enumerate(
                ((held_b, q_b, held_a, q_a), (held_a, q_a, held_b, q_b))
            ):
                k = (pairs - 1 - i) * 2 + 1 - turn
                base = pl.multiple_of(k * sub, sub)
                sums(pl.multiple_of(base + sub, sub), k + 1, g_other, q_other)
                kept = states_s[pl.ds(pl.multiple_of((origin + base + 1) * states, states), sub * states), :]
                bc_s[k] = diagonal(nt(kept, bs_s[pl.ds(base, sub), :].astype(BF16)))
                ct = turned_s[k]
                for t in range(sub - 1, -1, -1):
                    dl = delta_s[pl.ds(origin + base + t, 1), :]
                    bs = bs_s[pl.ds(base + t, 1), :]
                    g = bs * ct[:, t : t + 1] + h
                    h = g * jnp.exp2(dl * rate)
                    before = states_s[pl.ds(pl.multiple_of((origin + base + t) * states, states), states), :]
                    g_mine[t * states : (t + 1) * states, :] = g.astype(BF16)
                    q_mine[t * states : (t + 1) * states, :] = h.astype(BF16) * (decay * before)
            return h

        carry[...] = lax.fori_loop(0, pairs, pair, carry[...])
        sums(0, 0, held_a, q_a)
        w = w_s[:rows, :]
        conv_ref[...] = w * delta_s[here, :] + skip_ref[...] * bs_s[...]
        back_delta = bd_s[:rows, :] + w * u_ref[...].astype(F32)
        back_pre = (back_delta * jax.nn.sigmoid(pre_s[here, :])).astype(BF16)
        pre_ref[...] = back_pre
        gated_low = nt(down_ref[0], gated_block(scanned_s[here, :], z))
        mixed = [nt(step_proj_ref[...], back_pre), nt(step_up_ref[0], back_pre)]
        mixed += [jnp.concatenate([ref[k] for k in range(rows // sub)], 1) for ref in (bb_s, bc_s)]
        mixed = jnp.concatenate(mixed + [gated_low], 0).astype(BF16)
        for j in range(per):
            mixed_ref[j] = mixed[:, j * tokens : (j + 1) * tokens]


def gated_block(scanned, z):
    return (scanned * jax.nn.silu(z)).astype(BF16)


def scan(meta, shared, u, z, bg, step_proj, step_up, bias, rate, decay, skip, out_down, parts, sub):
    length, chans = u.shape
    tokens = length // parts
    block = 2 * tokens
    blocks = length // block
    states, rank, ranks = rate.shape[0], step_up.shape[1], step_proj.shape[0]
    cols = ranks + 2 * rank + 2 * states
    mirrored = lambda i: jnp.where(i < blocks, i, 2 * blocks - 1 - i)
    back = lambda i: jnp.where(i < blocks, blocks - 1, 2 * blocks - 1 - i)
    both = pl.BlockSpec((block, chans), lambda i, meta: (mirrored(i), 0))
    first = pl.BlockSpec((block, chans), lambda i, meta: (jnp.minimum(i, blocks - 1), 0))
    second = pl.BlockSpec((block, chans), lambda i, meta: (back(i), 0))
    return pl.pallas_call(
        functools.partial(scan_kernel, sub=sub, ranks=ranks),
        grid_spec=pltpu.PrefetchScalarGridSpec(
            num_scalar_prefetch=1,
            grid=(2 * blocks,),
            in_specs=[
                once(shared), both, both, second, once(step_proj), chosen(step_up), once(bias), once(rate), once(decay),
                once(skip), chosen(out_down, 0, chans),
            ],
            out_specs=[
                first, second, second, second,
                pl.BlockSpec((2, cols, tokens), lambda i, meta: (back(i), 0, 0)),
            ],
            scratch_shapes=[
                pltpu.VMEM((states, chans), F32),
                pltpu.VMEM(((length + 1) * states, chans), BF16),
                pltpu.VMEM((length, chans), F32),
                pltpu.VMEM((length, chans), F32),
                pltpu.VMEM((length + sub, chans), F32),
                pltpu.VMEM((length, chans), F32),
                pltpu.VMEM((block, chans), F32),
                pltpu.VMEM((block + sub, sub * states), BF16),
                pltpu.VMEM((block + sub, chans), F32),
                pltpu.VMEM((block + sub, chans), F32),
                pltpu.VMEM((block // sub + 1, states, sub), F32),
                pltpu.VMEM((block // sub, states, sub), F32),
                pltpu.VMEM((block // sub, states, sub), F32),
                pltpu.VMEM((sub * states, chans), BF16),
                pltpu.VMEM((sub * states, chans), BF16),
                pltpu.VMEM((sub * states, chans), BF16),
                pltpu.VMEM((sub * states, chans), BF16),
            ],
        ),
        out_shape=[
            jax.ShapeDtypeStruct((length, chans), BF16),
            jax.ShapeDtypeStruct((length, chans), BF16),
            jax.ShapeDtypeStruct((length, chans), F32),
            jax.ShapeDtypeStruct((length, chans), BF16),
            jax.ShapeDtypeStruct((parts, cols, tokens), BF16),
        ],
        compiler_params=pltpu.CompilerParams(vmem_limit_bytes=LIMIT),
        name="scan",
    )(meta, shared, u, z, bg, step_proj, step_up, bias, rate, decay, skip, out_down)


def finish_kernel(
    meta, *refs, ranks, states, parts, groups,
):
    pieces, refs = refs[: parts + 1], refs[parts + 1 :]
    columns_x, columns_z, refs = refs[:groups], refs[groups], refs[groups + 1 :]
    (back_ref, shared_ref, conv_grad_ref, back_z_ref, back_pre_ref, x_ref, x_before_ref, u_ref, low_in_ref,
     gated_ref, back_low_ref, cols_ref, up_x_ref, up_z_ref, proj_ref, down_ref,
     state_up_ref, in_down_ref, weight_ref, bias_ref,
     parts_ref, wide_ref, local_ref,
     after, sums_s, down_s, local_s, rows_s, whole_x, whole_z, piece_sems, x_sems, z_sems) = refs
    copies = (
        ring_copies(rows_s, pieces, meta[1], piece_sems)
        + row_copies(whole_x, columns_x, meta[2], x_sems)
        + row_copies(whole_z, columns_z, None, z_sems)
    )
    step = pl.program_id(0)
    steps = pl.num_programs(0)
    rows, chans = u_ref.shape
    rank = state_up_ref.shape[1]
    taps = weight_ref.shape[0]
    mixes = ranks + 2 * states

    @pl.when(step == 0)
    def _():
        for copy in copies:
            copy.start()
        after[...] = jnp.zeros_like(after)
        sums_s[...] = jnp.zeros_like(sums_s)
        down_s[...] = jnp.zeros_like(down_s)
        local_s[...] = jnp.zeros_like(local_s)

    per = rows // back_ref.shape[1]
    places = [place_of_block((steps - 1 - step) * per + j, meta[1], parts) for j in range(per)]
    back = jnp.concatenate([back_ref[place] for place in places], 0)
    shared = jnp.concatenate([shared_ref[place] for place in places], 0)
    u = u_ref[...]
    mixed = back[:, :mixes]
    back_low_state = nt(mixed, state_up_ref[0]).astype(BF16)
    grad = conv_grad_ref[...] + nn(mixed, proj_ref[...]) + nn(back_low_state, down_ref[0])
    keep = jnp.where(step == steps - 1, 0.0, 1.0)
    conv_pre = conv_before(x_ref[...].astype(F32), x_before_ref[...].astype(F32) * keep, weight_ref, bias_ref)
    grad = grad * silu_grad(conv_pre)
    padded = jnp.concatenate([grad, after[...]], 0)
    back_x = weight_ref[taps - 1 : taps, :] * grad
    for tap in range(taps - 1):
        at = taps - 1 - tap
        back_x = back_x + weight_ref[tap : tap + 1, :] * padded[at : at + rows]
    after[...] = grad[:8]
    back_x, back_z = back_x.astype(BF16), back_z_ref[...]

    @pl.when(step == 0)
    def _():
        for copy in copies:
            copy.wait()

    normed = rows_s[pl.ds(pl.multiple_of((steps - 1 - step) * rows, rows), rows), :]
    back_low_in = (nt(back_x, up_x_ref[0]) + nt(back_z, up_z_ref[0])).astype(BF16)
    parts_ref[...] = (
        nt(back_x, flat(whole_x)) + nt(back_z, flat(whole_z)) + nn(back_low_in, in_down_ref[0])
    ).astype(BF16)
    down_s[...] += tn(back_low_in, normed)
    low_in = low_in_ref[...]
    sums_s[:, :chans] += tn(low_in, back_x)
    sums_s[:, chans : 2 * chans] += tn(low_in, back_z)
    sums_s[:, 2 * chans : 3 * chans] += tn(back_low_ref[...], gated_ref[...])
    sums_s[:, 3 * chans :] += tn(back[:, mixes + rank :], cols_ref[...])
    local_s[:, :chans] += tn(back_low_state, u)
    local_s[:, chans : 2 * chans] += tn(shared[:, ranks : ranks + rank], back_pre_ref[...])
    local_s[:, 2 * chans : 2 * chans + ranks] += tn(back[:, mixes : mixes + rank], shared[:, :ranks])
    at = 2 * chans + ranks
    local_s[:, at : at + mixes] += tn(shared[:, ranks + rank + 2 * states :], mixed)

    @pl.when(step == steps - 1)
    def _():
        for values, ref, first in (
            (sums_s, wide_ref, 0), (down_s, wide_ref, sums_s.shape[1] // 128), (local_s, local_ref, 0)
        ):
            for j in range(values.shape[1] // 128):
                ref[first + j] = values[:, j * 128 : (j + 1) * 128].astype(BF16)
        lane = lax.broadcasted_iota(jnp.int32, (rank, 128), 1)
        local_ref[local_ref.shape[0] - 1] = (lane == meta[0]).astype(BF16)


def finish(
    meta, pieces, columns_x, columns_z, back, shared, conv_grad, back_z, back_pre, x, u, low_in, gated, back_low, cols, up,
    proj, down, state_up, in_down, weight, bias, parts, groups, states,
):
    length, chans = u.shape
    block, rank, span = AT_ONCE * length // parts, low_in.shape[1], cols.shape[1]
    mixes = proj.shape[0]
    ranks = mixes - 2 * states
    width = pieces[0].shape[1]
    whole_shape = (parts, groups) + columns_x[0].shape[1:]
    end = length // block - 1
    seq = lambda size: pl.BlockSpec((block, size), lambda i, meta: (end - i, 0))
    wide = 3 * chans + span
    local = 2 * chans + ranks + 2 * 128
    chunks = ((wide + width) // 128, local // 128 + 1)
    fixed = lambda count: pl.BlockSpec((count, rank, 128), lambda i, meta: (0, 0, 0))
    return pl.pallas_call(
        functools.partial(finish_kernel, ranks=ranks, states=states, parts=parts, groups=groups),
        grid_spec=pltpu.PrefetchScalarGridSpec(
            num_scalar_prefetch=1,
            grid=(length // block,),
            in_specs=[pl.BlockSpec(memory_space=pl.ANY)] * (len(pieces) + groups + 1)
            + [
                once(back), once(shared), seq(chans), seq(chans), seq(chans), seq(chans),
                pl.BlockSpec((16, chans), lambda i, meta: (jnp.maximum((end - i) * (block // 16) - 1, 0), 0)),
                seq(chans), seq(rank), seq(chans), seq(rank), seq(span),
                chosen(up, 0, chans), chosen(up, parts, chans), once(proj), chosen(down), chosen(state_up),
                chosen(in_down), once(weight), once(bias),
            ],
            out_specs=[seq(width)] + [fixed(count) for count in chunks],
            scratch_shapes=[
                pltpu.VMEM((8, chans), F32), pltpu.VMEM((rank, wide), F32), pltpu.VMEM((rank, width), F32),
                pltpu.VMEM((rank, local), F32), pltpu.VMEM((length, width), BF16),
                pltpu.VMEM(whole_shape, BF16), pltpu.VMEM(whole_shape, BF16),
                pltpu.SemaphoreType.DMA((len(pieces),)), pltpu.SemaphoreType.DMA((groups,)),
                pltpu.SemaphoreType.DMA((groups,)),
            ],
        ),
        out_shape=[
            jax.ShapeDtypeStruct((length, width), BF16),
        ]
        + [jax.ShapeDtypeStruct((count, rank, 128), BF16) for count in chunks],
        compiler_params=pltpu.CompilerParams(vmem_limit_bytes=LIMIT),
        name="finish",
    )(
        meta, *pieces, *columns_x, columns_z, back, shared, conv_grad, back_z, back_pre, x, x, u, low_in, gated, back_low,
        cols, up, up, proj, down, state_up, in_down, weight, bias,
    )


def place_kernel(meta, *refs, groups, parts, chans, span, every, wide):
    values, outs = refs[:groups], refs[groups:]
    in_up_ref, out_down_ref, out_up_ref, in_down_ref, state_down_ref, step_up_ref, step_down_ref, state_up_ref = outs
    adapter = pl.program_id(0)
    uses = [meta[3 + g] == adapter for g in range(groups)]

    def put(ref, column, at, size=128):
        total = None
        for use, value in zip(uses, values):
            term = jnp.where(use, value[at].astype(F32), 0.0)
            total = term if total is None else total + term
        ref[0, :, column : column + size] = total[:, :size]

    inner = parts * chans
    for p in range(parts):
        at = place_of_block(p, meta[1], parts) * wide
        for j in range(chans // 128):
            put(in_up_ref, p * chans + j * 128, at + j)
            put(in_up_ref, inner + p * chans + j * 128, at + chans // 128 + j)
            put(out_down_ref, p * chans + j * 128, at + 2 * (chans // 128) + j)
        if p % every == 0:
            for j in range(span // 128):
                put(out_up_ref, p // every * span + j * 128, at + 3 * (chans // 128) + j)
    at = parts * wide
    for ref in (in_down_ref, state_down_ref, step_up_ref, step_down_ref, state_up_ref):
        for j in range(pl.cdiv(ref.shape[2], 128)):
            put(ref, j * 128, at, min(128, ref.shape[2] - j * 128))
            at += 1


def place(meta, values, adapters, parts, chans, span, width, wide, ranks, mixes):
    groups, rank = len(values), values[0].shape[1]
    every = max(span * parts // width, 1)
    sizes = (2 * parts * chans, parts * chans, width, width, chans, chans, ranks, mixes)
    return pl.pallas_call(
        functools.partial(place_kernel, groups=groups, parts=parts, chans=chans, span=span, every=every, wide=wide),
        grid_spec=pltpu.PrefetchScalarGridSpec(
            num_scalar_prefetch=1,
            grid=(adapters,),
            in_specs=[once(value) for value in values],
            out_specs=[pl.BlockSpec((1, rank, size), lambda i, meta: (i, 0, 0)) for size in sizes],
        ),
        out_shape=[jax.ShapeDtypeStruct((adapters, rank, size), F32) for size in sizes],
        compiler_params=pltpu.CompilerParams(vmem_limit_bytes=16 << 20),
        name="place",
    )(meta, *values)


def split_kernel(values_ref, out_ref):
    chans = out_ref.shape[2]
    for i in range(out_ref.shape[0]):
        out_ref[i] = values_ref[:, i * chans : (i + 1) * chans]


def split_columns(values, parts):
    rows, cols = values.shape
    return pl.pallas_call(
        split_kernel, out_shape=jax.ShapeDtypeStruct((parts, rows, cols // parts), values.dtype), name="split_columns"
    )(values)


EPS = 1e-05


def ring_send(value, size, hop, axis):
    order = list(range(0, size, 2)) + list(range(1, size, 2))[::-1]
    pairs = [(order[i], order[(i + hop) % size]) for i in range(size)]
    return lax.ppermute(value, axis, pairs)


class RingGather:
    def __init__(self, own, size, axis):
        self.size, self.axis, self.rows, self.done = size, axis, own.shape[0], 0
        self.pieces = [own]
        self.ends = (own, own)

    def advance(self, hops):
        far, half = self.size // 2, self.rows // 2
        for _ in range(min(hops, far - self.done)):
            self.done += 1
            ahead, back = self.ends
            if self.done == far:
                ahead, back = ahead[:half], back[half:]
            self.ends = (ring_send(ahead, self.size, 1, self.axis), ring_send(back, self.size, -1, self.axis))
            self.pieces += list(self.ends)

    def all_pieces(self):
        self.advance(self.size)
        return self.pieces


class RingScatter:
    def __init__(self, partial, size, axis):
        self.partial, self.size, self.axis, self.done = partial, size, axis, 0
        self.rows = partial.shape[0] // size
        self.position = ring_position(lax.axis_index(axis), size)
        self.ends = None

    def block(self, offset, start=0, rows=None):
        at = ring_place(self.position + offset, self.size) * self.rows + start
        return lax.dynamic_slice_in_dim(self.partial, at, rows or self.rows, 0)

    def advance(self, hops):
        far, half = self.size // 2, self.rows // 2
        for _ in range(min(hops, far - self.done)):
            left = far - self.done
            if left == far:
                mine, other = self.block(far, 0, half), self.block(far, half, half)
            else:
                mine, other = self.block(left).astype(F32), self.block(-left).astype(F32)
                ahead, back = (end.astype(F32) for end in self.ends)
                if left == far - 1:
                    blank = jnp.zeros_like(ahead)
                    ahead, back = jnp.concatenate([ahead, blank], 0), jnp.concatenate([blank, back], 0)
                mine, other = (mine + ahead).astype(BF16), (other + back).astype(BF16)
            self.ends = (
                ring_send(mine, self.size, 1, self.axis),
                ring_send(other, self.size, -1, self.axis),
            )
            self.done += 1

    def total(self):
        self.advance(self.size)
        return self.block(0).astype(F32) + self.ends[0].astype(F32) + self.ends[1].astype(F32)


def together(*values):
    return lax.optimization_barrier(values)


def swap(value, size, bit, axis):
    return lax.ppermute(value, axis, [(i, i ^ bit) for i in range(size)])


def bits_of(size):
    bit = size // 2
    while bit:
        yield bit
        bit //= 2


def swap_gather(own, size, axis):
    held = [own]
    for bit in bits_of(size):
        held += [swap(block, size, bit, axis) for block in held]
    return held


def small_gather(own, size, axis):
    held = own[None]
    for bit in bits_of(size):
        held = jnp.concatenate([held, swap(held, size, bit, axis)], 0)
    return held


def exchange(values, axis):
    return lax.all_to_all(values, axis, split_axis=0, concat_axis=0, tiled=True)


def body(
    hidden, lengths, adapter_ids, norm_gain, in_proj_x, in_proj_z, conv_weight, conv_bias, state_proj,
    step_proj, step_bias, decay_log, skip_gain, out_proj, in_down, in_up, state_down, state_up, step_down,
    step_up, out_down, out_up, cotangent,
):
    parts, groups = lax.axis_size("seq"), lax.axis_size("fsdp")
    part, group = lax.axis_index("seq"), lax.axis_index("fsdp")
    tokens, width = hidden.shape[1:]
    chans = conv_weight.shape[1]
    ranks = step_proj.shape[0]
    states = decay_log.shape[0]
    rank = in_down.shape[2]
    adapters = in_down.shape[0]
    ident = adapter_ids[0]
    sub = 16
    meta = jnp.stack([ident, part, group]).astype(jnp.int32)
    in_down, state_down, step_down, out_down = (
        table.transpose(0, 2, 1) for table in (in_down, state_down, step_down, out_down)
    )
    state_proj = state_proj.T

    hidden_f = hidden[0].astype(F32)
    gain_f = norm_gain.astype(F32)
    inverse = lax.rsqrt(jnp.mean(hidden_f * hidden_f, axis=-1, keepdims=True) + EPS)
    normed = (hidden_f * inverse * gain_f).astype(BF16)
    positions = part * tokens + lax.broadcasted_iota(jnp.int32, (tokens, 1), 0)
    valid = (positions < lengths[0]).astype(F32)
    cot_f = cotangent[0].astype(F32)
    back_out = (valid * cot_f).astype(BF16)
    conv_weight, conv_bias = conv_weight.astype(F32), conv_bias.astype(F32)[None]
    bias, skip = step_bias.astype(F32)[None], skip_gain.astype(F32)[None]
    decay = -jnp.exp(decay_log.astype(F32))
    rate, decay = decay * LOG2E, decay.astype(BF16)
    rows = in_proj_x.shape[0]

    def own_columns_of(weight):
        return lax.all_to_all(weight, "seq", split_axis=0, concat_axis=0, tiled=True)

    hops = max(parts // 8, 1)
    whole_out = lax.all_gather(out_proj, "fsdp", axis=0, tiled=True)
    ring = RingGather(normed, parts, "seq")
    ring.advance(hops)
    mine_x = own_columns_of(split_columns(in_proj_x, parts))
    small = (conv_weight, conv_bias, bias, skip, rate, decay, meta, split_columns(in_proj_z, parts))
    ring.ends, small = together(ring.ends, small)
    conv_weight, conv_bias, bias, skip, rate, decay, meta, in_proj_z = small
    pieces = ring.all_pieces()
    columns = swap_gather(mine_x, groups, "fsdp")

    pieces, columns, back_out, in_proj_z = together(pieces, columns, back_out, in_proj_z)
    cot_ring = RingGather(back_out, parts, "seq")
    cot_ring.advance(hops)
    mine_z = own_columns_of(in_proj_z)
    low_in, x, conv_out, sums = project(
        meta, pieces, columns, in_down, in_up, conv_weight, conv_bias, state_proj, state_down, parts, groups
    )
    sums, mine_z = together(sums, mine_z)
    cot_ring.advance(hops)
    columns_z = lax.all_gather(mine_z, "fsdp")
    sums = exchange(sums, "seq")
    sums, cot_ring.ends = together(sums, cot_ring.ends)
    cot_ring.advance(hops)
    shared = share(meta, sums, state_up, step_down, ranks, states)[None]
    z = back = None
    for i, bit in enumerate(bits_of(parts)):
        shared = jnp.concatenate([shared, swap(shared, parts, bit, "seq")], 0)
        if i == 0:
            shared, cot_ring.ends, columns_z = together(shared, cot_ring.ends, columns_z)
            cot_ring.advance(parts)
            z = gate(meta, pieces, columns_z, low_in, in_up, parts, groups)
        elif i == 1:
            shared, cot_ring.pieces, z = together(shared, cot_ring.pieces, z)
            back = back_gate(meta, cot_ring.pieces, whole_out, out_down, out_up, parts)
    back_low, cols, back_gated = back
    gated, back_pre, conv_grad, back_z, mixed = scan(
        meta, shared, conv_out, z, back_gated, step_proj, step_up, bias, rate, decay, skip, out_down, parts, sub
    )
    out_ring = RingScatter(nn(gated, whole_out).astype(BF16), parts, "seq")
    out_ring.advance(hops)
    back_own = share_back(meta, exchange(mixed, "seq"), step_down, ranks, states)
    back = back_own[None]
    for i, bit in enumerate(bits_of(parts)):
        back = jnp.concatenate([back, swap(back, parts, bit, "seq")], 0)
        if i % 2 == 0:
            back, out_ring.ends = together(back, out_ring.ends)
            out_ring.advance(hops)
    in_parts, wide, local = finish(
        meta, pieces, columns, columns_z, back, shared, conv_grad, back_z, back_pre, x, conv_out, low_in, gated, back_low,
        cols, in_up, state_proj, state_down, state_up, in_down, conv_weight, conv_bias, parts, groups, states,
    )
    in_parts, wide, local, out_ring.ends = together(in_parts, wide, local, out_ring.ends)
    out_ring.advance(parts)
    in_ring = RingScatter(in_parts, parts, "seq")
    span = cols.shape[1]
    own = (3 * chans + span) // 128
    held, down_grad = wide[:own], wide[own:]
    for bit in bits_of(parts):
        in_ring.advance(hops)
        got = swap(jnp.concatenate([held, down_grad], 0), parts, bit, "seq")
        count = held.shape[0]
        held = jnp.concatenate([held, got[:count]], 0)
        down_grad = (down_grad.astype(F32) + got[count:].astype(F32)).astype(BF16)
        held, down_grad, in_ring.ends = together(held, down_grad, in_ring.ends)
    in_ring.advance(parts)
    chunks = [jnp.concatenate([held, down_grad, local], 0)]
    first, *others = bits_of(groups)
    chunks += [swap(chunks[0], groups, first, "fsdp")]
    branch = out_ring.total()
    chunks, in_ring.ends, branch = together(chunks, in_ring.ends, branch)
    for bit in others:
        chunks += [swap(block, groups, bit, "fsdp") for block in chunks]
    out_up_sel = lax.dynamic_index_in_dim(out_up, ident, 0, keepdims=False)
    block_out = (hidden_f + valid * (branch + nn(back_own[:, -rank:], out_up_sel))).astype(BF16)
    gained = in_ring.total() * gain_f
    input_grad = (
        cot_f
        + inverse * gained
        - hidden_f * inverse * inverse * inverse * jnp.mean(hidden_f * gained, axis=-1, keepdims=True)
    )

    lane = lax.broadcasted_iota(jnp.int32, (groups, adapters), 1)
    picks = jnp.stack([block[-1, 0, :adapters] for block in chunks]).astype(F32)
    idents = jnp.sum(picks * lane.astype(F32), axis=1).astype(jnp.int32)
    (in_up_grad, out_down_grad, out_up_grad, in_down_grad, state_down_grad, step_up_grad, step_down_grad,
     state_up_grad) = place(
        jnp.concatenate([meta, idents]), chunks, adapters, parts, chans, span, width, own, ranks, ranks + 2 * states
    )
    return (
        block_out[None], input_grad[None], in_down_grad.transpose(0, 2, 1), in_up_grad,
        state_down_grad.transpose(0, 2, 1), state_up_grad, step_down_grad.transpose(0, 2, 1), step_up_grad,
        out_down_grad.transpose(0, 2, 1), out_up_grad,
    )


def solution(mesh):
    seq, rows = P("fsdp", "seq", None), P(("seq", "fsdp"), None)
    in_specs = (
        seq, P("fsdp"), P("fsdp"), P(), rows, rows, P(None, "seq"), P("seq"), P("seq", None), P(None, "seq"),
        P("seq"), P(None, "seq"), P("seq"), rows, P(), P(), P(None, "seq", None), P(), P(), P(None, None, "seq"),
        P(), P(), seq,
    )
    out_specs = (seq, seq, P(), P(), P(None, "seq", None), P(), P(), P(None, None, "seq"), P(), P())
    return jax.shard_map(body, mesh=mesh, in_specs=in_specs, out_specs=out_specs, check_vma=False)
```

```python
import functools
import jax
import jax.numpy as jnp
from jax import lax
from jax.experimental import pallas as pl
from jax.experimental.pallas import tpu as pltpu
from jax.sharding import PartitionSpec as P

F32 = jnp.float32
BF16 = jnp.bfloat16
LOG2E = 1.4426950408889634


def silu_grad(values):
    sigma = jax.nn.sigmoid(values)
    return sigma * (1.0 + values * (1.0 - sigma))


def softplus(v):
    return jnp.maximum(v, 0.0) + jnp.log1p(jnp.exp(-jnp.abs(v)))


def nt(left, right):
    return lax.dot_general(left, right, (((1,), (1,)), ((), ())), preferred_element_type=F32)


def nn(left, right):
    return jnp.dot(left, right, preferred_element_type=F32)


def tn(left, right):
    return lax.dot_general(left, right, (((0,), (0,)), ((), ())), preferred_element_type=F32)


def spread_matrix(states, sub):
    row = lax.broadcasted_iota(jnp.int32, (states, sub * states), 0)
    col = lax.broadcasted_iota(jnp.int32, (states, sub * states), 1)
    return (lax.rem(col, states) == row).astype(BF16)


def own_step_mask(rows, width, sub):
    row = lax.broadcasted_iota(jnp.int32, (rows, sub * width), 0)
    col = lax.broadcasted_iota(jnp.int32, (rows, sub * width), 1)
    return (lax.rem(row, sub) == lax.div(col, width)).astype(F32)


def ring_place(position, size):
    position = lax.rem(position + size, size)
    return jnp.where(position < size // 2, 2 * position, 2 * (size - 1 - position) + 1)


def ring_position(place, size):
    return jnp.where(lax.rem(place, 2) == 0, lax.div(place, 2), size - 1 - lax.div(place, 2))


def ring_copies(out_ref, pieces, part, sems):
    size, rows = len(pieces) - 1, pieces[0].shape[0]
    far, half, here = size // 2, rows // 2, ring_position(part, size)
    copies = []
    for i, piece in enumerate(pieces):
        hop = (i + 1) // 2
        place = ring_place(here - hop if i % 2 else here + hop, size)
        at = place * rows
        if i == size:
            at = ring_place(here + far, size) * rows + half
        at = pl.multiple_of(at, half)
        copies.append(pltpu.make_async_copy(piece, out_ref.at[pl.ds(at, piece.shape[0]), :], sems.at[i]))
    return copies


def swap_order(size):
    order, bit = [0], size // 2
    while bit:
        order += [at ^ bit for at in order]
        bit //= 2
    return order


def place_of_block(block, part, size):
    apart, out, bit = jnp.bitwise_xor(block, part), 0, size // 2
    weight = 1
    while bit:
        out = out + weight * jnp.bitwise_and(lax.div(apart, bit), 1)
        weight, bit = weight * 2, bit // 2
    return out


def row_copies(out_ref, pieces, group, sems):
    copies = []
    for i, apart in enumerate(swap_order(out_ref.shape[1])):
        at = i if group is None else jnp.bitwise_xor(group, apart)
        piece = pieces.at[i] if group is None else pieces[i]
        copies.append(pltpu.make_async_copy(piece, out_ref.at[:, at], sems.at[i]))
    return copies


def run_all(copies):
    for copy in copies:
        copy.start()
    for copy in copies:
        copy.wait()


def flat(ref):
    return ref[...].reshape(-1, ref.shape[-1])


def conv_before(x, before, weight_ref, bias_ref):
    taps = weight_ref.shape[0]
    padded = jnp.concatenate([before, x], 0)
    out = bias_ref[...]
    for tap in range(taps):
        at = before.shape[0] - (taps - 1 - tap)
        out = out + weight_ref[tap : tap + 1, :] * padded[at : at + x.shape[0]]
    return out


def project_kernel(meta, *refs, parts, groups):
    pieces, refs = refs[: parts + 1], refs[parts + 1 :]
    columns, refs = refs[:groups], refs[groups:]
    (in_down_ref, up_ref, weight_ref, bias_ref, proj_ref, down_ref,
     low_in_ref, x_ref, conv_ref, sums_ref, before, rows_s, whole_s, piece_sems, column_sems) = refs
    step = pl.program_id(0)
    rows = x_ref.shape[0]

    @pl.when(step == 0)
    def _():
        run_all(ring_copies(rows_s, pieces, meta[1], piece_sems) + row_copies(whole_s, columns, meta[2], column_sems))
        before[...] = jnp.zeros_like(before)

    normed = rows_s[pl.ds(pl.multiple_of(step * rows, rows), rows), :]
    low_in = nt(normed, in_down_ref[0]).astype(BF16)
    low_in_ref[...] = low_in
    x = (nn(normed, flat(whole_s)) + nn(low_in, up_ref[0])).astype(BF16)
    x_ref[...] = x
    x_f = x.astype(F32)
    conv_out = jax.nn.silu(conv_before(x_f, before[...], weight_ref, bias_ref)).astype(BF16)
    before[...] = x_f[-8:]
    conv_ref[...] = conv_out
    sums = jnp.concatenate([nt(proj_ref[...], conv_out), nt(down_ref[0], conv_out)], 0).astype(BF16)
    tokens = sums_ref.shape[2]
    for j in range(sums_ref.shape[0]):
        sums_ref[j] = sums[:, j * tokens : (j + 1) * tokens]


def once(array):
    return pl.BlockSpec(array.shape, lambda i, *_: (0,) * array.ndim, pipeline_mode=pl.Buffered(1))


def chosen(table, which=0, width=None):
    if width is None:
        return pl.BlockSpec((1,) + table.shape[1:], lambda i, meta: (meta[0], 0, 0))
    return pl.BlockSpec((1, table.shape[1], width), lambda i, meta: (meta[0], 0, meta[1] + which))


LIMIT = 58 << 20
AT_ONCE = 4


def gate_kernel(meta, *refs, parts):
    pieces, refs = refs[: parts + 1], refs[parts + 1 :]
    columns, low_in_ref, up_ref, z_ref, rows_s, whole_s, piece_sems, column_sems = refs
    step = pl.program_id(0)

    @pl.when(step == 0)
    def _():
        run_all(ring_copies(rows_s, pieces, meta[1], piece_sems) + row_copies(whole_s, columns, None, column_sems))

    rows = z_ref.shape[0]
    normed = rows_s[pl.ds(pl.multiple_of(step * rows, rows), rows), :]
    z_ref[...] = (nn(normed, flat(whole_s)) + nn(low_in_ref[...], up_ref[0])).astype(BF16)


def gate(meta, pieces, columns, low_in, up, parts, groups):
    tokens, width = pieces[0].shape
    length, chans = tokens * parts, columns.shape[-1]
    block = AT_ONCE * tokens
    seq = lambda size: pl.BlockSpec((block, size), lambda i, meta: (i, 0))
    return pl.pallas_call(
        functools.partial(gate_kernel, parts=parts),
        grid_spec=pltpu.PrefetchScalarGridSpec(
            num_scalar_prefetch=1,
            grid=(length // block,),
            in_specs=[pl.BlockSpec(memory_space=pl.ANY)] * (len(pieces) + 1)
            + [seq(low_in.shape[1]), chosen(up, parts, chans)],
            out_specs=seq(chans),
            scratch_shapes=[
                pltpu.VMEM((length, width), BF16), pltpu.VMEM((parts, groups) + columns.shape[2:], BF16),
                pltpu.SemaphoreType.DMA((len(pieces),)), pltpu.SemaphoreType.DMA((groups,)),
            ],
        ),
        out_shape=jax.ShapeDtypeStruct((length, chans), BF16),
        compiler_params=pltpu.CompilerParams(vmem_limit_bytes=LIMIT),
        name="gate",
    )(meta, *pieces, columns, low_in, up)


def back_gate_kernel(meta, *refs, parts):
    pieces, refs = refs[: parts + 1], refs[parts + 1 :]
    out_proj_ref, out_down_ref, out_up_ref, back_low_ref, cols_ref, grad_ref, rows_s, sems = refs
    step = pl.program_id(0)

    @pl.when(step == 0)
    def _():
        run_all(ring_copies(rows_s, pieces, meta[1], sems))

    block, span = cols_ref.shape
    at = pl.ds(pl.multiple_of(step * block, block), block)
    share_of = max(span * parts // rows_s.shape[1], 1)
    cols_ref[...] = rows_s[at, pl.ds(pl.multiple_of(lax.div(meta[1], share_of) * span, span), span)]
    rows = rows_s[at, :]
    back_low = nt(rows, out_up_ref[0]).astype(BF16)
    back_low_ref[...] = back_low
    grad_ref[...] = (nt(rows, out_proj_ref[...]) + nn(back_low, out_down_ref[0])).astype(BF16)


def back_gate(meta, pieces, out_proj, out_down, out_up, parts):
    tokens, width = pieces[0].shape
    chans, rank, block, length = out_proj.shape[0], out_up.shape[1], AT_ONCE * tokens, tokens * parts
    span = max(width // parts, 128)
    seq = lambda size: pl.BlockSpec((block, size), lambda i, meta: (i, 0))
    return pl.pallas_call(
        functools.partial(back_gate_kernel, parts=parts),
        grid_spec=pltpu.PrefetchScalarGridSpec(
            num_scalar_prefetch=1,
            grid=(length // block,),
            in_specs=[pl.BlockSpec(memory_space=pl.ANY)] * len(pieces)
            + [once(out_proj), chosen(out_down, 0, chans), chosen(out_up)],
            out_specs=[seq(rank), seq(span), seq(chans)],
            scratch_shapes=[pltpu.VMEM((length, width), BF16), pltpu.SemaphoreType.DMA((len(pieces),))],
        ),
        out_shape=[jax.ShapeDtypeStruct((length, size), BF16) for size in (rank, span, chans)],
        compiler_params=pltpu.CompilerParams(vmem_limit_bytes=LIMIT),
        name="back_gate",
    )(meta, *pieces, out_proj, out_down, out_up)


def project(meta, pieces, columns, in_down, up, weight, bias, proj, down, parts, groups):
    tokens, width = pieces[0].shape
    length, chans, rank = tokens * parts, columns[0].shape[-1], in_down.shape[1]
    cols = proj.shape[0] + rank
    once_rows = AT_ONCE // 2
    seq = lambda size: pl.BlockSpec((once_rows * tokens, size), lambda i, meta: (i, 0))
    rows = columns[0].shape[1]
    whole_shape = (parts, groups, rows, chans)
    return pl.pallas_call(
        functools.partial(project_kernel, parts=parts, groups=groups),
        grid_spec=pltpu.PrefetchScalarGridSpec(
            num_scalar_prefetch=1,
            grid=(parts // once_rows,),
            in_specs=[pl.BlockSpec(memory_space=pl.ANY)] * (len(pieces) + groups)
            + [chosen(in_down), chosen(up, 0, chans), once(weight), once(bias), once(proj), chosen(down)],
            out_specs=[
                seq(rank), seq(chans), seq(chans), pl.BlockSpec((once_rows, cols, tokens), lambda i, meta: (i, 0, 0))
            ],
            scratch_shapes=[
                pltpu.VMEM((8, chans), F32), pltpu.VMEM((length, width), BF16), pltpu.VMEM(whole_shape, BF16),
                pltpu.SemaphoreType.DMA((len(pieces),)), pltpu.SemaphoreType.DMA((groups,)),
            ],
        ),
        out_shape=[jax.ShapeDtypeStruct((length, size), BF16) for size in (rank, chans, chans)]
        + [jax.ShapeDtypeStruct((parts, cols, tokens), BF16)],
        compiler_params=pltpu.CompilerParams(vmem_limit_bytes=LIMIT),
        name="project",
    )(meta, *pieces, *columns, in_down, up, weight, bias, proj, down)


def share_kernel(meta, got_ref, state_up_ref, step_down_ref, out_ref, *, ranks, states):
    sums = got_ref[0].astype(F32)
    for i in range(1, got_ref.shape[0]):
        sums = sums + got_ref[i].astype(F32)
    sums = sums.T
    cut = ranks + 2 * states
    low_state = sums[:, cut:].astype(BF16)
    mixed = sums[:, :cut] + nn(low_state, state_up_ref[0])
    step_low = mixed[:, :ranks].astype(BF16)
    step_mid = nt(step_low, step_down_ref[0]).astype(BF16)
    out_ref[...] = jnp.concatenate([step_low, step_mid, mixed[:, ranks:].astype(BF16), low_state], 1)


def share(meta, got, state_up, step_down, ranks, states):
    tokens, rank = got.shape[2], step_down.shape[1]
    cols = ranks + 2 * rank + 2 * states
    return pl.pallas_call(
        functools.partial(share_kernel, ranks=ranks, states=states),
        grid_spec=pltpu.PrefetchScalarGridSpec(
            num_scalar_prefetch=1,
            grid=(1,),
            in_specs=[once(got), chosen(state_up), chosen(step_down)],
            out_specs=pl.BlockSpec((tokens, cols), lambda i, meta: (0, 0)),
        ),
        out_shape=jax.ShapeDtypeStruct((tokens, cols), BF16),
        name="share",
    )(meta, got, state_up, step_down)


def share_back_kernel(meta, got_ref, step_down_ref, out_ref, *, ranks, states):
    sums = got_ref[0].astype(F32)
    for i in range(1, got_ref.shape[0]):
        sums = sums + got_ref[i].astype(F32)
    sums = sums.T
    rank = step_down_ref.shape[1]
    mid, end = ranks + rank, ranks + rank + 2 * states
    back_mid = sums[:, ranks:mid]
    down = step_down_ref[0].astype(F32)
    back_step = sums[:, :ranks] + jnp.dot(back_mid, down, precision=lax.Precision.HIGHEST, preferred_element_type=F32)
    out_ref[...] = jnp.concatenate([back_step, sums[:, mid:end], back_mid, sums[:, end:]], 1).astype(BF16)


def share_back(meta, got, step_down, ranks, states):
    cols, tokens = got.shape[1:]
    return pl.pallas_call(
        functools.partial(share_back_kernel, ranks=ranks, states=states),
        grid_spec=pltpu.PrefetchScalarGridSpec(
            num_scalar_prefetch=1,
            grid=(1,),
            in_specs=[once(got), chosen(step_down)],
            out_specs=pl.BlockSpec((tokens, cols), lambda i, meta: (0, 0)),
        ),
        out_shape=jax.ShapeDtypeStruct((tokens, cols), BF16),
        name="share_back",
    )(meta, got, step_down)


def columns_of_groups(values, ref, sub):
    turned = values.astype(F32).T
    for k in range(ref.shape[0]):
        ref[k] = turned[:, k * sub : (k + 1) * sub]


def scan_kernel(
    meta, shared_ref, u_ref, z_ref, bg_ref, step_proj_ref, step_up_ref, bias_ref, rate_ref, decay_ref, skip_ref, down_ref,
    gated_ref, pre_ref, conv_ref, bz_ref, mixed_ref,
    carry, states_s, pre_s, delta_s, du_s, scanned_s, bs_s, wide_s, w_s, bd_s, bb_s, bc_s, turned_s, held_a, held_b,
    q_a, q_b, *, sub, ranks,
):
    rows, chans = u_ref.shape
    parts, tokens = shared_ref.shape[:2]
    per = rows // tokens
    states, rank = rate_ref.shape[0], step_up_ref.shape[1]
    step = pl.program_id(0)
    blocks = pl.num_programs(0) // 2
    block = jnp.where(step < blocks, step, 2 * blocks - 1 - step)
    origin = pl.multiple_of(block * rows, rows)
    here = pl.ds(origin, rows)
    shared = jnp.concatenate(
        [shared_ref[place_of_block(block * per + j, meta[1], parts)] for j in range(per)], 0
    )
    b_rows = shared[:, ranks + rank : ranks + rank + states]
    c_rows = shared[:, ranks + rank + states : ranks + rank + 2 * states]
    rate = rate_ref[...]
    pairs = rows // (2 * sub)

    @pl.when(step < blocks)
    def _():
        @pl.when(step == 0)
        def _():
            carry[...] = jnp.zeros_like(carry)
            held_b[...] = jnp.zeros_like(held_b)
            states_s[:states, :] = jnp.zeros((states, chans), BF16)
            wide_s[:sub, :] = jnp.zeros((sub, sub * states), BF16)

        pre = nn(shared[:, :ranks], step_proj_ref[...]) + nn(shared[:, ranks : ranks + rank], step_up_ref[0]) + bias_ref[...]
        delta = softplus(pre)
        pre_s[here, :] = pre
        delta_s[here, :] = delta
        du_s[here, :] = delta * u_ref[...].astype(F32)
        columns_of_groups(b_rows, turned_s, sub)
        spread = nn(c_rows, spread_matrix(states, sub)) * own_step_mask(rows, states, sub)
        wide_s[sub:, :] = spread.astype(BF16)

        def pair(k, s):
            for turn, (mine, other) in enumerate(((held_a, held_b), (held_b, held_a))):
                base = pl.multiple_of(k * (2 * sub) + turn * sub, sub)
                w_s[pl.ds(base, sub), :] = nn(wide_s[pl.ds(base, sub), :], other[...])
                bt = turned_s[k * 2 + turn]
                for t in range(sub):
                    dl = delta_s[pl.ds(origin + base + t, 1), :]
                    du = du_s[pl.ds(origin + base + t, 1), :]
                    s = jnp.exp2(dl * rate) * s + du * bt[:, t : t + 1]
                    low = s.astype(BF16)
                    mine[t * states : (t + 1) * states, :] = low
                    states_s[pl.ds(pl.multiple_of((origin + base + t + 1) * states, states), states), :] = low
            return s

        carry[...] = lax.fori_loop(0, pairs, pair, carry[...])
        w_s[rows:, :] = nn(wide_s[rows:, :], held_b[...])
        scanned = w_s[sub:, :] + skip_ref[...] * u_ref[...].astype(F32)
        scanned_s[here, :] = scanned
        gated_ref[...] = (scanned * jax.nn.silu(z_ref[...].astype(F32))).astype(BF16)

    @pl.when(step >= blocks)
    def _():
        @pl.when(step == blocks)
        def _():
            carry[...] = jnp.zeros_like(carry)
            for ref in (held_a, q_a):
                ref[...] = jnp.zeros_like(ref)
            wide_s[rows:, :] = jnp.zeros((sub, sub * states), BF16)
            du_s[pl.ds(blocks * rows, sub), :] = jnp.zeros((sub, chans), F32)

        z = z_ref[...].astype(F32)
        bg = bg_ref[...].astype(F32)
        sigma = jax.nn.sigmoid(z)
        bs_s[...] = bg * (z * sigma)
        bz_ref[...] = (bg * scanned_s[here, :] * (sigma * (1.0 + z * (1.0 - sigma)))).astype(BF16)
        columns_of_groups(c_rows, turned_s, sub)
        spread = nn(b_rows, spread_matrix(states, sub)) * own_step_mask(rows, states, sub)
        wide_s[:rows, :] = spread.astype(BF16)
        ones = own_step_mask(sub, states, sub).astype(BF16)
        col = lax.broadcasted_iota(jnp.int32, (states, sub), 1)
        decay = decay_ref[...]

        def diagonal(wide):
            out = wide[:states]
            for t in range(1, sub):
                out = jnp.where(col == t, wide[t * states : (t + 1) * states], out)
            return out

        def sums(at, k, g_ref, q_ref):
            w_s[pl.ds(at, sub), :] = nn(wide_s[pl.ds(at, sub), :], g_ref[...])
            bd_s[pl.ds(at, sub), :] = nn(ones, q_ref[...])
            bb_s[k] = diagonal(nt(g_ref[...], du_s[pl.ds(pl.multiple_of(origin + at, sub), sub), :].astype(BF16)))

        def pair(i, h):
            for turn, (g_mine, q_mine, g_other, q_other) in enumerate(
                ((held_b, q_b, held_a, q_a), (held_a, q_a, held_b, q_b))
            ):
                k = (pairs - 1 - i) * 2 + 1 - turn
                base = pl.multiple_of(k * sub, sub)
                sums(pl.multiple_of(base + sub, sub), k + 1, g_other, q_other)
                kept = states_s[pl.ds(pl.multiple_of((origin + base + 1) * states, states), sub * states), :]
                bc_s[k] = diagonal(nt(kept, bs_s[pl.ds(base, sub), :].astype(BF16)))
                ct = turned_s[k]
                for t in range(sub - 1, -1, -1):
                    dl = delta_s[pl.ds(origin + base + t, 1), :]
                    bs = bs_s[pl.ds(base + t, 1), :]
                    g = bs * ct[:, t : t + 1] + h
                    h = g * jnp.exp2(dl * rate)
                    before = states_s[pl.ds(pl.multiple_of((origin + base + t) * states, states), states), :]
                    g_mine[t * states : (t + 1) * states, :] = g.astype(BF16)
                    q_mine[t * states : (t + 1) * states, :] = h.astype(BF16) * (decay * before)
            return h

        carry[...] = lax.fori_loop(0, pairs, pair, carry[...])
        sums(0, 0, held_a, q_a)
        w = w_s[:rows, :]
        conv_ref[...] = w * delta_s[here, :] + skip_ref[...] * bs_s[...]
        back_delta = bd_s[:rows, :] + w * u_ref[...].astype(F32)
        back_pre = (back_delta * jax.nn.sigmoid(pre_s[here, :])).astype(BF16)
        pre_ref[...] = back_pre
        gated_low = nt(down_ref[0], gated_block(scanned_s[here, :], z))
        mixed = [nt(step_proj_ref[...], back_pre), nt(step_up_ref[0], back_pre)]
        mixed += [jnp.concatenate([ref[k] for k in range(rows // sub)], 1) for ref in (bb_s, bc_s)]
        mixed = jnp.concatenate(mixed + [gated_low], 0).astype(BF16)
        for j in range(per):
            mixed_ref[j] = mixed[:, j * tokens : (j + 1) * tokens]


def gated_block(scanned, z):
    return (scanned * jax.nn.silu(z)).astype(BF16)


def scan(meta, shared, u, z, bg, step_proj, step_up, bias, rate, decay, skip, out_down, parts, sub):
    length, chans = u.shape
    tokens = length // parts
    block = 2 * tokens
    blocks = length // block
    states, rank, ranks = rate.shape[0], step_up.shape[1], step_proj.shape[0]
    cols = ranks + 2 * rank + 2 * states
    mirrored = lambda i: jnp.where(i < blocks, i, 2 * blocks - 1 - i)
    back = lambda i: jnp.where(i < blocks, blocks - 1, 2 * blocks - 1 - i)
    both = pl.BlockSpec((block, chans), lambda i, meta: (mirrored(i), 0))
    first = pl.BlockSpec((block, chans), lambda i, meta: (jnp.minimum(i, blocks - 1), 0))
    second = pl.BlockSpec((block, chans), lambda i, meta: (back(i), 0))
    return pl.pallas_call(
        functools.partial(scan_kernel, sub=sub, ranks=ranks),
        grid_spec=pltpu.PrefetchScalarGridSpec(
            num_scalar_prefetch=1,
            grid=(2 * blocks,),
            in_specs=[
                once(shared), both, both, second, once(step_proj), chosen(step_up), once(bias), once(rate), once(decay),
                once(skip), chosen(out_down, 0, chans),
            ],
            out_specs=[
                first, second, second, second,
                pl.BlockSpec((2, cols, tokens), lambda i, meta: (back(i), 0, 0)),
            ],
            scratch_shapes=[
                pltpu.VMEM((states, chans), F32),
                pltpu.VMEM(((length + 1) * states, chans), BF16),
                pltpu.VMEM((length, chans), F32),
                pltpu.VMEM((length, chans), F32),
                pltpu.VMEM((length + sub, chans), F32),
                pltpu.VMEM((length, chans), F32),
                pltpu.VMEM((block, chans), F32),
                pltpu.VMEM((block + sub, sub * states), BF16),
                pltpu.VMEM((block + sub, chans), F32),
                pltpu.VMEM((block + sub, chans), F32),
                pltpu.VMEM((block // sub + 1, states, sub), F32),
                pltpu.VMEM((block // sub, states, sub), F32),
                pltpu.VMEM((block // sub, states, sub), F32),
                pltpu.VMEM((sub * states, chans), BF16),
                pltpu.VMEM((sub * states, chans), BF16),
                pltpu.VMEM((sub * states, chans), BF16),
                pltpu.VMEM((sub * states, chans), BF16),
            ],
        ),
        out_shape=[
            jax.ShapeDtypeStruct((length, chans), BF16),
            jax.ShapeDtypeStruct((length, chans), BF16),
            jax.ShapeDtypeStruct((length, chans), F32),
            jax.ShapeDtypeStruct((length, chans), BF16),
            jax.ShapeDtypeStruct((parts, cols, tokens), BF16),
        ],
        compiler_params=pltpu.CompilerParams(vmem_limit_bytes=LIMIT),
        name="scan",
    )(meta, shared, u, z, bg, step_proj, step_up, bias, rate, decay, skip, out_down)


def finish_kernel(
    meta, *refs, ranks, states, parts, groups,
):
    pieces, refs = refs[: parts + 1], refs[parts + 1 :]
    columns_x, columns_z, refs = refs[:groups], refs[groups], refs[groups + 1 :]
    (back_ref, shared_ref, conv_grad_ref, back_z_ref, back_pre_ref, x_ref, x_before_ref, u_ref, low_in_ref,
     gated_ref, back_low_ref, cols_ref, up_x_ref, up_z_ref, proj_ref, down_ref,
     state_up_ref, in_down_ref, weight_ref, bias_ref,
     parts_ref, wide_ref, local_ref,
     after, sums_s, down_s, local_s, rows_s, whole_x, whole_z, piece_sems, x_sems, z_sems) = refs
    copies = (
        ring_copies(rows_s, pieces, meta[1], piece_sems)
        + row_copies(whole_x, columns_x, meta[2], x_sems)
        + row_copies(whole_z, columns_z, None, z_sems)
    )
    step = pl.program_id(0)
    steps = pl.num_programs(0)
    rows, chans = u_ref.shape
    rank = state_up_ref.shape[1]
    taps = weight_ref.shape[0]
    mixes = ranks + 2 * states

    @pl.when(step == 0)
    def _():
        for copy in copies:
            copy.start()
        after[...] = jnp.zeros_like(after)
        sums_s[...] = jnp.zeros_like(sums_s)
        down_s[...] = jnp.zeros_like(down_s)
        local_s[...] = jnp.zeros_like(local_s)

    per = rows // back_ref.shape[1]
    places = [place_of_block((steps - 1 - step) * per + j, meta[1], parts) for j in range(per)]
    back = jnp.concatenate([back_ref[place] for place in places], 0)
    shared = jnp.concatenate([shared_ref[place] for place in places], 0)
    u = u_ref[...]
    mixed = back[:, :mixes]
    back_low_state = nt(mixed, state_up_ref[0]).astype(BF16)
    grad = conv_grad_ref[...] + nn(mixed, proj_ref[...]) + nn(back_low_state, down_ref[0])
    keep = jnp.where(step == steps - 1, 0.0, 1.0)
    conv_pre = conv_before(x_ref[...].astype(F32), x_before_ref[...].astype(F32) * keep, weight_ref, bias_ref)
    grad = grad * silu_grad(conv_pre)
    padded = jnp.concatenate([grad, after[...]], 0)
    back_x = weight_ref[taps - 1 : taps, :] * grad
    for tap in range(taps - 1):
        at = taps - 1 - tap
        back_x = back_x + weight_ref[tap : tap + 1, :] * padded[at : at + rows]
    after[...] = grad[:8]
    back_x, back_z = back_x.astype(BF16), back_z_ref[...]

    @pl.when(step == 0)
    def _():
        for copy in copies:
            copy.wait()

    normed = rows_s[pl.ds(pl.multiple_of((steps - 1 - step) * rows, rows), rows), :]
    back_low_in = (nt(back_x, up_x_ref[0]) + nt(back_z, up_z_ref[0])).astype(BF16)
    parts_ref[...] = (
        nt(back_x, flat(whole_x)) + nt(back_z, flat(whole_z)) + nn(back_low_in, in_down_ref[0])
    ).astype(BF16)
    down_s[...] += tn(back_low_in, normed)
    low_in = low_in_ref[...]
    sums_s[:, :chans] += tn(low_in, back_x)
    sums_s[:, chans : 2 * chans] += tn(low_in, back_z)
    sums_s[:, 2 * chans : 3 * chans] += tn(back_low_ref[...], gated_ref[...])
    sums_s[:, 3 * chans :] += tn(back[:, mixes + rank :], cols_ref[...])
    local_s[:, :chans] += tn(back_low_state, u)
    local_s[:, chans : 2 * chans] += tn(shared[:, ranks : ranks + rank], back_pre_ref[...])
    local_s[:, 2 * chans : 2 * chans + ranks] += tn(back[:, mixes : mixes + rank], shared[:, :ranks])
    at = 2 * chans + ranks
    local_s[:, at : at + mixes] += tn(shared[:, ranks + rank + 2 * states :], mixed)

    @pl.when(step == steps - 1)
    def _():
        for values, ref, first in (
            (sums_s, wide_ref, 0), (down_s, wide_ref, sums_s.shape[1] // 128), (local_s, local_ref, 0)
        ):
            for j in range(values.shape[1] // 128):
                ref[first + j] = values[:, j * 128 : (j + 1) * 128].astype(BF16)
        lane = lax.broadcasted_iota(jnp.int32, (rank, 128), 1)
        local_ref[local_ref.shape[0] - 1] = (lane == meta[0]).astype(BF16)


def finish(
    meta, pieces, columns_x, columns_z, back, shared, conv_grad, back_z, back_pre, x, u, low_in, gated, back_low, cols, up,
    proj, down, state_up, in_down, weight, bias, parts, groups, states,
):
    length, chans = u.shape
    block, rank, span = AT_ONCE * length // parts, low_in.shape[1], cols.shape[1]
    mixes = proj.shape[0]
    ranks = mixes - 2 * states
    width = pieces[0].shape[1]
    whole_shape = (parts, groups) + columns_x[0].shape[1:]
    end = length // block - 1
    seq = lambda size: pl.BlockSpec((block, size), lambda i, meta: (end - i, 0))
    wide = 3 * chans + span
    local = 2 * chans + ranks + 2 * 128
    chunks = ((wide + width) // 128, local // 128 + 1)
    fixed = lambda count: pl.BlockSpec((count, rank, 128), lambda i, meta: (0, 0, 0))
    return pl.pallas_call(
        functools.partial(finish_kernel, ranks=ranks, states=states, parts=parts, groups=groups),
        grid_spec=pltpu.PrefetchScalarGridSpec(
            num_scalar_prefetch=1,
            grid=(length // block,),
            in_specs=[pl.BlockSpec(memory_space=pl.ANY)] * (len(pieces) + groups + 1)
            + [
                once(back), once(shared), seq(chans), seq(chans), seq(chans), seq(chans),
                pl.BlockSpec((16, chans), lambda i, meta: (jnp.maximum((end - i) * (block // 16) - 1, 0), 0)),
                seq(chans), seq(rank), seq(chans), seq(rank), seq(span),
                chosen(up, 0, chans), chosen(up, parts, chans), once(proj), chosen(down), chosen(state_up),
                chosen(in_down), once(weight), once(bias),
            ],
            out_specs=[seq(width)] + [fixed(count) for count in chunks],
            scratch_shapes=[
                pltpu.VMEM((8, chans), F32), pltpu.VMEM((rank, wide), F32), pltpu.VMEM((rank, width), F32),
                pltpu.VMEM((rank, local), F32), pltpu.VMEM((length, width), BF16),
                pltpu.VMEM(whole_shape, BF16), pltpu.VMEM(whole_shape, BF16),
                pltpu.SemaphoreType.DMA((len(pieces),)), pltpu.SemaphoreType.DMA((groups,)),
                pltpu.SemaphoreType.DMA((groups,)),
            ],
        ),
        out_shape=[
            jax.ShapeDtypeStruct((length, width), BF16),
        ]
        + [jax.ShapeDtypeStruct((count, rank, 128), BF16) for count in chunks],
        compiler_params=pltpu.CompilerParams(vmem_limit_bytes=LIMIT),
        name="finish",
    )(
        meta, *pieces, *columns_x, columns_z, back, shared, conv_grad, back_z, back_pre, x, x, u, low_in, gated, back_low,
        cols, up, up, proj, down, state_up, in_down, weight, bias,
    )


def place_kernel(meta, *refs, groups, parts, chans, span, every, wide):
    values, outs = refs[:groups], refs[groups:]
    in_up_ref, out_down_ref, out_up_ref, in_down_ref, state_down_ref, step_up_ref, step_down_ref, state_up_ref = outs
    per = in_up_ref.shape[0]
    first = pl.program_id(0) * per

    def put(ref, column, at, size=128):
        terms = [value[at].astype(F32) for value in values]
        for i in range(per):
            total = None
            for g, term in enumerate(terms):
                term = jnp.where(meta[3 + g] == first + i, term, 0.0)
                total = term if total is None else total + term
            ref[i, :, column : column + size] = total[:, :size]

    inner = parts * chans
    for p in range(parts):
        at = place_of_block(p, meta[1], parts) * wide
        for j in range(chans // 128):
            put(in_up_ref, p * chans + j * 128, at + j)
            put(in_up_ref, inner + p * chans + j * 128, at + chans // 128 + j)
            put(out_down_ref, p * chans + j * 128, at + 2 * (chans // 128) + j)
        if p % every == 0:
            for j in range(span // 128):
                put(out_up_ref, p // every * span + j * 128, at + 3 * (chans // 128) + j)
    at = parts * wide
    for ref in (in_down_ref, state_down_ref, step_up_ref, step_down_ref, state_up_ref):
        for j in range(pl.cdiv(ref.shape[2], 128)):
            put(ref, j * 128, at, min(128, ref.shape[2] - j * 128))
            at += 1


def place(meta, values, adapters, parts, chans, span, width, wide, ranks, mixes):
    groups, rank = len(values), values[0].shape[1]
    every = max(span * parts // width, 1)
    sizes = (2 * parts * chans, parts * chans, width, width, chans, chans, ranks, mixes)
    return pl.pallas_call(
        functools.partial(place_kernel, groups=groups, parts=parts, chans=chans, span=span, every=every, wide=wide),
        grid_spec=pltpu.PrefetchScalarGridSpec(
            num_scalar_prefetch=1,
            grid=(adapters // 2,),
            in_specs=[once(value) for value in values],
            out_specs=[pl.BlockSpec((2, rank, size), lambda i, meta: (i, 0, 0)) for size in sizes],
        ),
        out_shape=[jax.ShapeDtypeStruct((adapters, rank, size), F32) for size in sizes],
        compiler_params=pltpu.CompilerParams(vmem_limit_bytes=32 << 20),
        name="place",
    )(meta, *values)


def split_kernel(values_ref, out_ref):
    chans = out_ref.shape[2]
    for i in range(out_ref.shape[0]):
        out_ref[i] = values_ref[:, i * chans : (i + 1) * chans]


def split_columns(values, parts):
    rows, cols = values.shape
    return pl.pallas_call(
        split_kernel, out_shape=jax.ShapeDtypeStruct((parts, rows, cols // parts), values.dtype), name="split_columns"
    )(values)


EPS = 1e-05


def ring_send(value, size, hop, axis):
    order = list(range(0, size, 2)) + list(range(1, size, 2))[::-1]
    pairs = [(order[i], order[(i + hop) % size]) for i in range(size)]
    return lax.ppermute(value, axis, pairs)


class RingGather:
    def __init__(self, own, size, axis):
        self.size, self.axis, self.rows, self.done = size, axis, own.shape[0], 0
        self.pieces = [own]
        self.ends = (own, own)

    def advance(self, hops):
        far, half = self.size // 2, self.rows // 2
        for _ in range(min(hops, far - self.done)):
            self.done += 1
            ahead, back = self.ends
            if self.done == far:
                ahead, back = ahead[:half], back[half:]
            self.ends = (ring_send(ahead, self.size, 1, self.axis), ring_send(back, self.size, -1, self.axis))
            self.pieces += list(self.ends)

    def all_pieces(self):
        self.advance(self.size)
        return self.pieces


class RingScatter:
    def __init__(self, partial, size, axis):
        self.partial, self.size, self.axis, self.done = partial, size, axis, 0
        self.rows = partial.shape[0] // size
        self.position = ring_position(lax.axis_index(axis), size)
        self.ends = None

    def block(self, offset, start=0, rows=None):
        at = ring_place(self.position + offset, self.size) * self.rows + start
        return lax.dynamic_slice_in_dim(self.partial, at, rows or self.rows, 0)

    def advance(self, hops):
        far, half = self.size // 2, self.rows // 2
        for _ in range(min(hops, far - self.done)):
            left = far - self.done
            if left == far:
                mine, other = self.block(far, 0, half), self.block(far, half, half)
            else:
                mine, other = self.block(left).astype(F32), self.block(-left).astype(F32)
                ahead, back = (end.astype(F32) for end in self.ends)
                if left == far - 1:
                    blank = jnp.zeros_like(ahead)
                    ahead, back = jnp.concatenate([ahead, blank], 0), jnp.concatenate([blank, back], 0)
                mine, other = (mine + ahead).astype(BF16), (other + back).astype(BF16)
            self.ends = (
                ring_send(mine, self.size, 1, self.axis),
                ring_send(other, self.size, -1, self.axis),
            )
            self.done += 1

    def total(self):
        self.advance(self.size)
        return self.block(0).astype(F32) + self.ends[0].astype(F32) + self.ends[1].astype(F32)


def together(*values):
    return lax.optimization_barrier(values)


def swap(value, size, bit, axis):
    return lax.ppermute(value, axis, [(i, i ^ bit) for i in range(size)])


def bits_of(size):
    bit = size // 2
    while bit:
        yield bit
        bit //= 2


def swap_gather(own, size, axis):
    held = [own]
    for bit in bits_of(size):
        held += [swap(block, size, bit, axis) for block in held]
    return held


def small_gather(own, size, axis):
    held = own[None]
    for bit in bits_of(size):
        held = jnp.concatenate([held, swap(held, size, bit, axis)], 0)
    return held


def exchange(values, axis):
    return lax.all_to_all(values, axis, split_axis=0, concat_axis=0, tiled=True)


def body(
    hidden, lengths, adapter_ids, norm_gain, in_proj_x, in_proj_z, conv_weight, conv_bias, state_proj,
    step_proj, step_bias, decay_log, skip_gain, out_proj, in_down, in_up, state_down, state_up, step_down,
    step_up, out_down, out_up, cotangent,
):
    parts, groups = lax.axis_size("seq"), lax.axis_size("fsdp")
    part, group = lax.axis_index("seq"), lax.axis_index("fsdp")
    tokens, width = hidden.shape[1:]
    chans = conv_weight.shape[1]
    ranks = step_proj.shape[0]
    states = decay_log.shape[0]
    rank = in_down.shape[2]
    adapters = in_down.shape[0]
    ident = adapter_ids[0]
    sub = 16
    meta = jnp.stack([ident, part, group]).astype(jnp.int32)
    in_down, state_down, step_down, out_down = (
        table.transpose(0, 2, 1) for table in (in_down, state_down, step_down, out_down)
    )
    state_proj = state_proj.T

    hidden_f = hidden[0].astype(F32)
    gain_f = norm_gain.astype(F32)
    inverse = lax.rsqrt(jnp.mean(hidden_f * hidden_f, axis=-1, keepdims=True) + EPS)
    normed = (hidden_f * inverse * gain_f).astype(BF16)
    positions = part * tokens + lax.broadcasted_iota(jnp.int32, (tokens, 1), 0)
    valid = (positions < lengths[0]).astype(F32)
    cot_f = cotangent[0].astype(F32)
    back_out = (valid * cot_f).astype(BF16)
    conv_weight, conv_bias = conv_weight.astype(F32), conv_bias.astype(F32)[None]
    bias, skip = step_bias.astype(F32)[None], skip_gain.astype(F32)[None]
    decay = -jnp.exp(decay_log.astype(F32))
    rate, decay = decay * LOG2E, decay.astype(BF16)
    rows = in_proj_x.shape[0]

    def own_columns_of(weight):
        return lax.all_to_all(weight, "seq", split_axis=0, concat_axis=0, tiled=True)

    hops = max(parts // 8, 1)
    whole_out = lax.all_gather(out_proj, "fsdp", axis=0, tiled=True)
    ring = RingGather(normed, parts, "seq")
    ring.advance(hops)
    mine_x = own_columns_of(split_columns(in_proj_x, parts))
    small = (conv_weight, conv_bias, bias, skip, rate, decay, meta, split_columns(in_proj_z, parts))
    ring.ends, small = together(ring.ends, small)
    conv_weight, conv_bias, bias, skip, rate, decay, meta, in_proj_z = small
    pieces = ring.all_pieces()
    columns = swap_gather(mine_x, groups, "fsdp")

    pieces, columns, back_out, in_proj_z = together(pieces, columns, back_out, in_proj_z)
    cot_ring = RingGather(back_out, parts, "seq")
    cot_ring.advance(hops)
    mine_z = own_columns_of(in_proj_z)
    low_in, x, conv_out, sums = project(
        meta, pieces, columns, in_down, in_up, conv_weight, conv_bias, state_proj, state_down, parts, groups
    )
    sums, mine_z = together(sums, mine_z)
    cot_ring.advance(hops)
    columns_z = lax.all_gather(mine_z, "fsdp")
    sums = exchange(sums, "seq")
    sums, cot_ring.ends = together(sums, cot_ring.ends)
    cot_ring.advance(hops)
    shared = share(meta, sums, state_up, step_down, ranks, states)[None]
    shared, columns_z = together(shared, columns_z)
    z = gate(meta, pieces, columns_z, low_in, in_up, parts, groups)
    for i, bit in enumerate(bits_of(parts)):
        shared = jnp.concatenate([shared, swap(shared, parts, bit, "seq")], 0)
        if i == 0:
            shared, cot_ring.ends, z = together(shared, cot_ring.ends, z)
            cot_ring.advance(parts)
    back = back_gate(meta, cot_ring.pieces, whole_out, out_down, out_up, parts)
    back_low, cols, back_gated = back
    gated, back_pre, conv_grad, back_z, mixed = scan(
        meta, shared, conv_out, z, back_gated, step_proj, step_up, bias, rate, decay, skip, out_down, parts, sub
    )
    out_ring = RingScatter(nn(gated, whole_out).astype(BF16), parts, "seq")
    out_ring.advance(hops)
    back_own = share_back(meta, exchange(mixed, "seq"), step_down, ranks, states)
    back = back_own[None]
    for i, bit in enumerate(bits_of(parts)):
        back = jnp.concatenate([back, swap(back, parts, bit, "seq")], 0)
        if i % 2 == 0:
            back, out_ring.ends = together(back, out_ring.ends)
            out_ring.advance(hops)
    in_parts, wide, local = finish(
        meta, pieces, columns, columns_z, back, shared, conv_grad, back_z, back_pre, x, conv_out, low_in, gated, back_low,
        cols, in_up, state_proj, state_down, state_up, in_down, conv_weight, conv_bias, parts, groups, states,
    )
    in_parts, wide, local, out_ring.ends = together(in_parts, wide, local, out_ring.ends)
    out_ring.advance(parts)
    in_ring = RingScatter(in_parts, parts, "seq")
    span = cols.shape[1]
    own = (3 * chans + span) // 128
    held, down_grad = wide[:own], wide[own:]
    for bit in bits_of(parts):
        in_ring.advance(hops)
        got = swap(jnp.concatenate([held, down_grad], 0), parts, bit, "seq")
        count = held.shape[0]
        held = jnp.concatenate([held, got[:count]], 0)
        down_grad = (down_grad.astype(F32) + got[count:].astype(F32)).astype(BF16)
        held, down_grad, in_ring.ends = together(held, down_grad, in_ring.ends)
    in_ring.advance(parts)
    chunks = [jnp.concatenate([held, down_grad, local], 0)]
    first, *others = bits_of(groups)
    chunks += [swap(chunks[0], groups, first, "fsdp")]
    branch = out_ring.total()
    chunks, in_ring.ends, branch = together(chunks, in_ring.ends, branch)
    for bit in others:
        chunks += [swap(block, groups, bit, "fsdp") for block in chunks]
    out_up_sel = lax.dynamic_index_in_dim(out_up, ident, 0, keepdims=False)
    block_out = (hidden_f + valid * (branch + nn(back_own[:, -rank:], out_up_sel))).astype(BF16)
    gained = in_ring.total() * gain_f
    input_grad = (
        cot_f
        + inverse * gained
        - hidden_f * inverse * inverse * inverse * jnp.mean(hidden_f * gained, axis=-1, keepdims=True)
    )

    lane = lax.broadcasted_iota(jnp.int32, (groups, adapters), 1)
    picks = jnp.stack([block[-1, 0, :adapters] for block in chunks]).astype(F32)
    idents = jnp.sum(picks * lane.astype(F32), axis=1).astype(jnp.int32)
    (in_up_grad, out_down_grad, out_up_grad, in_down_grad, state_down_grad, step_up_grad, step_down_grad,
     state_up_grad) = place(
        jnp.concatenate([meta, idents]), chunks, adapters, parts, chans, span, width, own, ranks, ranks + 2 * states
    )
    return (
        block_out[None], input_grad[None], in_down_grad.transpose(0, 2, 1), in_up_grad,
        state_down_grad.transpose(0, 2, 1), state_up_grad, step_down_grad.transpose(0, 2, 1), step_up_grad,
        out_down_grad.transpose(0, 2, 1), out_up_grad,
    )


def solution(mesh):
    seq, rows = P("fsdp", "seq", None), P(("seq", "fsdp"), None)
    in_specs = (
        seq, P("fsdp"), P("fsdp"), P(), rows, rows, P(None, "seq"), P("seq"), P("seq", None), P(None, "seq"),
        P("seq"), P(None, "seq"), P("seq"), rows, P(), P(), P(None, "seq", None), P(), P(), P(None, None, "seq"),
        P(), P(), seq,
    )
    out_specs = (seq, seq, P(), P(), P(None, "seq", None), P(), P(), P(None, None, "seq"), P(), P())
    return jax.shard_map(body, mesh=mesh, in_specs=in_specs, out_specs=out_specs, check_vma=False)
```

```python
import functools
import jax
import jax.numpy as jnp
from jax import lax
from jax.experimental import pallas as pl
from jax.experimental.pallas import tpu as pltpu
from jax.sharding import PartitionSpec as P

F32 = jnp.float32
BF16 = jnp.bfloat16
LOG2E = 1.4426950408889634


def silu_grad(values):
    sigma = jax.nn.sigmoid(values)
    return sigma * (1.0 + values * (1.0 - sigma))


def softplus(v):
    return jnp.maximum(v, 0.0) + jnp.log1p(jnp.exp(-jnp.abs(v)))


def nt(left, right):
    return lax.dot_general(left, right, (((1,), (1,)), ((), ())), preferred_element_type=F32)


def nn(left, right):
    return jnp.dot(left, right, preferred_element_type=F32)


def tn(left, right):
    return lax.dot_general(left, right, (((0,), (0,)), ((), ())), preferred_element_type=F32)


def spread_matrix(states, sub):
    row = lax.broadcasted_iota(jnp.int32, (states, sub * states), 0)
    col = lax.broadcasted_iota(jnp.int32, (states, sub * states), 1)
    return (lax.rem(col, states) == row).astype(BF16)


def own_step_mask(rows, width, sub):
    row = lax.broadcasted_iota(jnp.int32, (rows, sub * width), 0)
    col = lax.broadcasted_iota(jnp.int32, (rows, sub * width), 1)
    return (lax.rem(row, sub) == lax.div(col, width)).astype(F32)


def ring_place(position, size):
    position = lax.rem(position + size, size)
    return jnp.where(position < size // 2, 2 * position, 2 * (size - 1 - position) + 1)


def ring_position(place, size):
    return jnp.where(lax.rem(place, 2) == 0, lax.div(place, 2), size - 1 - lax.div(place, 2))


def ring_copies(out_ref, pieces, part, sems):
    size, rows = len(pieces) - 1, pieces[0].shape[0]
    far, half, here = size // 2, rows // 2, ring_position(part, size)
    copies = []
    for i, piece in enumerate(pieces):
        hop = (i + 1) // 2
        place = ring_place(here - hop if i % 2 else here + hop, size)
        at = place * rows
        if i == size:
            at = ring_place(here + far, size) * rows + half
        at = pl.multiple_of(at, half)
        copies.append(pltpu.make_async_copy(piece, out_ref.at[pl.ds(at, piece.shape[0]), :], sems.at[i]))
    return copies


def swap_order(size):
    order, bit = [0], size // 2
    while bit:
        order += [at ^ bit for at in order]
        bit //= 2
    return order


def place_of_block(block, part, size):
    apart, out, bit = jnp.bitwise_xor(block, part), 0, size // 2
    weight = 1
    while bit:
        out = out + weight * jnp.bitwise_and(lax.div(apart, bit), 1)
        weight, bit = weight * 2, bit // 2
    return out


def row_copies(out_ref, pieces, group, sems):
    copies = []
    for i, apart in enumerate(swap_order(out_ref.shape[1])):
        at = i if group is None else jnp.bitwise_xor(group, apart)
        piece = pieces.at[i] if group is None else pieces[i]
        copies.append(pltpu.make_async_copy(piece, out_ref.at[:, at], sems.at[i]))
    return copies


def run_all(copies):
    for copy in copies:
        copy.start()
    for copy in copies:
        copy.wait()


def flat(ref):
    return ref[...].reshape(-1, ref.shape[-1])


def conv_before(x, before, weight_ref, bias_ref):
    taps = weight_ref.shape[0]
    padded = jnp.concatenate([before, x], 0)
    out = bias_ref[...]
    for tap in range(taps):
        at = before.shape[0] - (taps - 1 - tap)
        out = out + weight_ref[tap : tap + 1, :] * padded[at : at + x.shape[0]]
    return out


def normalise_kernel(rows_ref, gain_ref, out_ref, inverse_ref):
    rows = rows_ref[0].astype(F32)
    inverse = lax.rsqrt(jnp.mean(rows * rows, axis=-1, keepdims=True) + EPS)
    out_ref[...] = (rows * inverse * gain_ref[...].astype(F32)).astype(BF16)
    inverse_ref[...] = jnp.broadcast_to(inverse, inverse_ref.shape)


def normalise(rows, gain):
    _, tokens, width = rows.shape
    return pl.pallas_call(
        normalise_kernel,
        out_shape=[jax.ShapeDtypeStruct((tokens, width), BF16), jax.ShapeDtypeStruct((tokens, 128), F32)],
        name="normalise",
    )(rows, gain)


def project_kernel(meta, *refs, parts, groups):
    pieces, refs = refs[: parts + 1], refs[parts + 1 :]
    columns, refs = refs[:groups], refs[groups:]
    (in_down_ref, up_ref, weight_ref, bias_ref, proj_ref, down_ref,
     low_in_ref, x_ref, conv_ref, sums_ref, before, rows_s, whole_s, piece_sems, column_sems) = refs
    step = pl.program_id(0)
    rows = x_ref.shape[0]

    @pl.when(step == 0)
    def _():
        run_all(ring_copies(rows_s, pieces, meta[1], piece_sems) + row_copies(whole_s, columns, meta[2], column_sems))
        before[...] = jnp.zeros_like(before)

    normed = rows_s[pl.ds(pl.multiple_of(step * rows, rows), rows), :]
    low_in = nt(normed, in_down_ref[0]).astype(BF16)
    low_in_ref[...] = low_in
    x = (nn(normed, flat(whole_s)) + nn(low_in, up_ref[0])).astype(BF16)
    x_ref[...] = x
    x_f = x.astype(F32)
    conv_out = jax.nn.silu(conv_before(x_f, before[...], weight_ref, bias_ref)).astype(BF16)
    before[...] = x_f[-8:]
    conv_ref[...] = conv_out
    sums = jnp.concatenate([nt(proj_ref[...], conv_out), nt(down_ref[0], conv_out)], 0).astype(BF16)
    tokens = sums_ref.shape[2]
    for j in range(sums_ref.shape[0]):
        sums_ref[j] = sums[:, j * tokens : (j + 1) * tokens]


def once(array):
    return pl.BlockSpec(array.shape, lambda i, *_: (0,) * array.ndim, pipeline_mode=pl.Buffered(1))


def chosen(table, which=0, width=None):
    if width is None:
        return pl.BlockSpec((1,) + table.shape[1:], lambda i, meta: (meta[0], 0, 0))
    return pl.BlockSpec((1, table.shape[1], width), lambda i, meta: (meta[0], 0, meta[1] + which))


LIMIT = 58 << 20
AT_ONCE = 4


def gate_kernel(meta, *refs, parts):
    pieces, refs = refs[: parts + 1], refs[parts + 1 :]
    columns, low_in_ref, up_ref, z_ref, rows_s, whole_s, piece_sems, column_sems = refs
    step = pl.program_id(0)

    @pl.when(step == 0)
    def _():
        run_all(ring_copies(rows_s, pieces, meta[1], piece_sems) + row_copies(whole_s, columns, None, column_sems))

    rows = z_ref.shape[0]
    normed = rows_s[pl.ds(pl.multiple_of(step * rows, rows), rows), :]
    z_ref[...] = (nn(normed, flat(whole_s)) + nn(low_in_ref[...], up_ref[0])).astype(BF16)


def gate(meta, pieces, columns, low_in, up, parts, groups):
    tokens, width = pieces[0].shape
    length, chans = tokens * parts, columns.shape[-1]
    block = AT_ONCE * tokens
    seq = lambda size: pl.BlockSpec((block, size), lambda i, meta: (i, 0))
    return pl.pallas_call(
        functools.partial(gate_kernel, parts=parts),
        grid_spec=pltpu.PrefetchScalarGridSpec(
            num_scalar_prefetch=1,
            grid=(length // block,),
            in_specs=[pl.BlockSpec(memory_space=pl.ANY)] * (len(pieces) + 1)
            + [seq(low_in.shape[1]), chosen(up, parts, chans)],
            out_specs=seq(chans),
            scratch_shapes=[
                pltpu.VMEM((length, width), BF16), pltpu.VMEM((parts, groups) + columns.shape[2:], BF16),
                pltpu.SemaphoreType.DMA((len(pieces),)), pltpu.SemaphoreType.DMA((groups,)),
            ],
        ),
        out_shape=jax.ShapeDtypeStruct((length, chans), BF16),
        compiler_params=pltpu.CompilerParams(vmem_limit_bytes=LIMIT),
        name="gate",
    )(meta, *pieces, columns, low_in, up)


def back_gate_kernel(meta, *refs, parts):
    pieces, refs = refs[: parts + 1], refs[parts + 1 :]
    out_proj_ref, out_down_ref, out_up_ref, back_low_ref, cols_ref, grad_ref, rows_s, sems = refs
    step = pl.program_id(0)

    @pl.when(step == 0)
    def _():
        run_all(ring_copies(rows_s, pieces, meta[1], sems))

    block, span = cols_ref.shape
    at = pl.ds(pl.multiple_of(step * block, block), block)
    share_of = max(span * parts // rows_s.shape[1], 1)
    cols_ref[...] = rows_s[at, pl.ds(pl.multiple_of(lax.div(meta[1], share_of) * span, span), span)]
    rows = rows_s[at, :]
    back_low = nt(rows, out_up_ref[0]).astype(BF16)
    back_low_ref[...] = back_low
    grad_ref[...] = (nt(rows, out_proj_ref[...]) + nn(back_low, out_down_ref[0])).astype(BF16)


def back_gate(meta, pieces, out_proj, out_down, out_up, parts):
    tokens, width = pieces[0].shape
    chans, rank, block, length = out_proj.shape[0], out_up.shape[1], AT_ONCE * tokens, tokens * parts
    span = max(width // parts, 128)
    seq = lambda size: pl.BlockSpec((block, size), lambda i, meta: (i, 0))
    return pl.pallas_call(
        functools.partial(back_gate_kernel, parts=parts),
        grid_spec=pltpu.PrefetchScalarGridSpec(
            num_scalar_prefetch=1,
            grid=(length // block,),
            in_specs=[pl.BlockSpec(memory_space=pl.ANY)] * len(pieces)
            + [once(out_proj), chosen(out_down, 0, chans), chosen(out_up)],
            out_specs=[seq(rank), seq(span), seq(chans)],
            scratch_shapes=[pltpu.VMEM((length, width), BF16), pltpu.SemaphoreType.DMA((len(pieces),))],
        ),
        out_shape=[jax.ShapeDtypeStruct((length, size), BF16) for size in (rank, span, chans)],
        compiler_params=pltpu.CompilerParams(vmem_limit_bytes=LIMIT),
        name="back_gate",
    )(meta, *pieces, out_proj, out_down, out_up)


def project(meta, pieces, columns, in_down, up, weight, bias, proj, down, parts, groups):
    tokens, width = pieces[0].shape
    length, chans, rank = tokens * parts, columns[0].shape[-1], in_down.shape[1]
    cols = proj.shape[0] + rank
    once_rows = AT_ONCE // 2
    seq = lambda size: pl.BlockSpec((once_rows * tokens, size), lambda i, meta: (i, 0))
    rows = columns[0].shape[1]
    whole_shape = (parts, groups, rows, chans)
    return pl.pallas_call(
        functools.partial(project_kernel, parts=parts, groups=groups),
        grid_spec=pltpu.PrefetchScalarGridSpec(
            num_scalar_prefetch=1,
            grid=(parts // once_rows,),
            in_specs=[pl.BlockSpec(memory_space=pl.ANY)] * (len(pieces) + groups)
            + [chosen(in_down), chosen(up, 0, chans), once(weight), once(bias), once(proj), chosen(down)],
            out_specs=[
                seq(rank), seq(chans), seq(chans), pl.BlockSpec((once_rows, cols, tokens), lambda i, meta: (i, 0, 0))
            ],
            scratch_shapes=[
                pltpu.VMEM((8, chans), F32), pltpu.VMEM((length, width), BF16), pltpu.VMEM(whole_shape, BF16),
                pltpu.SemaphoreType.DMA((len(pieces),)), pltpu.SemaphoreType.DMA((groups,)),
            ],
        ),
        out_shape=[jax.ShapeDtypeStruct((length, size), BF16) for size in (rank, chans, chans)]
        + [jax.ShapeDtypeStruct((parts, cols, tokens), BF16)],
        compiler_params=pltpu.CompilerParams(vmem_limit_bytes=LIMIT),
        name="project",
    )(meta, *pieces, *columns, in_down, up, weight, bias, proj, down)


def share_kernel(meta, got_ref, state_up_ref, step_down_ref, out_ref, *, ranks, states):
    sums = got_ref[0].astype(F32)
    for i in range(1, got_ref.shape[0]):
        sums = sums + got_ref[i].astype(F32)
    sums = sums.T
    cut = ranks + 2 * states
    low_state = sums[:, cut:].astype(BF16)
    mixed = sums[:, :cut] + nn(low_state, state_up_ref[0])
    step_low = mixed[:, :ranks].astype(BF16)
    step_mid = nt(step_low, step_down_ref[0]).astype(BF16)
    out_ref[...] = jnp.concatenate([step_low, step_mid, mixed[:, ranks:].astype(BF16), low_state], 1)


def share(meta, got, state_up, step_down, ranks, states):
    tokens, rank = got.shape[2], step_down.shape[1]
    cols = ranks + 2 * rank + 2 * states
    return pl.pallas_call(
        functools.partial(share_kernel, ranks=ranks, states=states),
        grid_spec=pltpu.PrefetchScalarGridSpec(
            num_scalar_prefetch=1,
            grid=(1,),
            in_specs=[once(got), chosen(state_up), chosen(step_down)],
            out_specs=pl.BlockSpec((tokens, cols), lambda i, meta: (0, 0)),
        ),
        out_shape=jax.ShapeDtypeStruct((tokens, cols), BF16),
        name="share",
    )(meta, got, state_up, step_down)


def share_back_kernel(meta, got_ref, step_down_ref, out_ref, *, ranks, states):
    sums = got_ref[0].astype(F32)
    for i in range(1, got_ref.shape[0]):
        sums = sums + got_ref[i].astype(F32)
    sums = sums.T
    rank = step_down_ref.shape[1]
    mid, end = ranks + rank, ranks + rank + 2 * states
    back_mid = sums[:, ranks:mid]
    down = step_down_ref[0].astype(F32)
    back_step = sums[:, :ranks] + jnp.dot(back_mid, down, precision=lax.Precision.HIGHEST, preferred_element_type=F32)
    out_ref[...] = jnp.concatenate([back_step, sums[:, mid:end], back_mid, sums[:, end:]], 1).astype(BF16)


def share_back(meta, got, step_down, ranks, states):
    cols, tokens = got.shape[1:]
    return pl.pallas_call(
        functools.partial(share_back_kernel, ranks=ranks, states=states),
        grid_spec=pltpu.PrefetchScalarGridSpec(
            num_scalar_prefetch=1,
            grid=(1,),
            in_specs=[once(got), chosen(step_down)],
            out_specs=pl.BlockSpec((tokens, cols), lambda i, meta: (0, 0)),
        ),
        out_shape=jax.ShapeDtypeStruct((tokens, cols), BF16),
        name="share_back",
    )(meta, got, step_down)


def columns_of_groups(values, ref, sub):
    turned = values.astype(F32).T
    for k in range(ref.shape[0]):
        ref[k] = turned[:, k * sub : (k + 1) * sub]


def scan_kernel(
    meta, shared_ref, u_ref, z_ref, bg_ref, step_proj_ref, step_up_ref, bias_ref, rate_ref, decay_ref, skip_ref, down_ref,
    gated_ref, pre_ref, conv_ref, bz_ref, mixed_ref,
    carry, states_s, pre_s, delta_s, du_s, scanned_s, bs_s, wide_s, w_s, bd_s, bb_s, bc_s, turned_s, held_a, held_b,
    q_a, q_b, *, sub, ranks,
):
    rows, chans = u_ref.shape
    parts, tokens = shared_ref.shape[:2]
    per = rows // tokens
    states, rank = rate_ref.shape[0], step_up_ref.shape[1]
    step = pl.program_id(0)
    blocks = pl.num_programs(0) // 2
    block = jnp.where(step < blocks, step, 2 * blocks - 1 - step)
    origin = pl.multiple_of(block * rows, rows)
    here = pl.ds(origin, rows)
    shared = jnp.concatenate(
        [shared_ref[place_of_block(block * per + j, meta[1], parts)] for j in range(per)], 0
    )
    b_rows = shared[:, ranks + rank : ranks + rank + states]
    c_rows = shared[:, ranks + rank + states : ranks + rank + 2 * states]
    rate = rate_ref[...]
    pairs = rows // (2 * sub)

    @pl.when(step < blocks)
    def _():
        @pl.when(step == 0)
        def _():
            carry[...] = jnp.zeros_like(carry)
            held_b[...] = jnp.zeros_like(held_b)
            states_s[:states, :] = jnp.zeros((states, chans), BF16)
            wide_s[:sub, :] = jnp.zeros((sub, sub * states), BF16)

        pre = nn(shared[:, :ranks], step_proj_ref[...]) + nn(shared[:, ranks : ranks + rank], step_up_ref[0]) + bias_ref[...]
        delta = softplus(pre)
        pre_s[here, :] = pre
        delta_s[here, :] = delta
        du_s[here, :] = delta * u_ref[...].astype(F32)
        columns_of_groups(b_rows, turned_s, sub)
        spread = nn(c_rows, spread_matrix(states, sub)) * own_step_mask(rows, states, sub)
        wide_s[sub:, :] = spread.astype(BF16)

        def pair(k, s):
            for turn, (mine, other) in enumerate(((held_a, held_b), (held_b, held_a))):
                base = pl.multiple_of(k * (2 * sub) + turn * sub, sub)
                w_s[pl.ds(base, sub), :] = nn(wide_s[pl.ds(base, sub), :], other[...])
                bt = turned_s[k * 2 + turn]
                for t in range(sub):
                    dl = delta_s[pl.ds(origin + base + t, 1), :]
                    du = du_s[pl.ds(origin + base + t, 1), :]
                    s = jnp.exp2(dl * rate) * s + du * bt[:, t : t + 1]
                    low = s.astype(BF16)
                    mine[t * states : (t + 1) * states, :] = low
                    states_s[pl.ds(pl.multiple_of((origin + base + t + 1) * states, states), states), :] = low
            return s

        carry[...] = lax.fori_loop(0, pairs, pair, carry[...])
        w_s[rows:, :] = nn(wide_s[rows:, :], held_b[...])
        scanned = w_s[sub:, :] + skip_ref[...] * u_ref[...].astype(F32)
        scanned_s[here, :] = scanned
        gated_ref[...] = (scanned * jax.nn.silu(z_ref[...].astype(F32))).astype(BF16)

    @pl.when(step >= blocks)
    def _():
        @pl.when(step == blocks)
        def _():
            carry[...] = jnp.zeros_like(carry)
            for ref in (held_a, q_a):
                ref[...] = jnp.zeros_like(ref)
            wide_s[rows:, :] = jnp.zeros((sub, sub * states), BF16)
            du_s[pl.ds(blocks * rows, sub), :] = jnp.zeros((sub, chans), F32)

        z = z_ref[...].astype(F32)
        bg = bg_ref[...].astype(F32)
        sigma = jax.nn.sigmoid(z)
        bs_s[...] = bg * (z * sigma)
        bz_ref[...] = (bg * scanned_s[here, :] * (sigma * (1.0 + z * (1.0 - sigma)))).astype(BF16)
        columns_of_groups(c_rows, turned_s, sub)
        spread = nn(b_rows, spread_matrix(states, sub)) * own_step_mask(rows, states, sub)
        wide_s[:rows, :] = spread.astype(BF16)
        ones = own_step_mask(sub, states, sub).astype(BF16)
        col = lax.broadcasted_iota(jnp.int32, (states, sub), 1)
        decay = decay_ref[...]

        def diagonal(wide):
            out = wide[:states]
            for t in range(1, sub):
                out = jnp.where(col == t, wide[t * states : (t + 1) * states], out)
            return out

        def sums(at, k, g_ref, q_ref):
            w_s[pl.ds(at, sub), :] = nn(wide_s[pl.ds(at, sub), :], g_ref[...])
            bd_s[pl.ds(at, sub), :] = nn(ones, q_ref[...])
            bb_s[k] = diagonal(nt(g_ref[...], du_s[pl.ds(pl.multiple_of(origin + at, sub), sub), :].astype(BF16)))

        def pair(i, h):
            for turn, (g_mine, q_mine, g_other, q_other) in enumerate(
                ((held_b, q_b, held_a, q_a), (held_a, q_a, held_b, q_b))
            ):
                k = (pairs - 1 - i) * 2 + 1 - turn
                base = pl.multiple_of(k * sub, sub)
                sums(pl.multiple_of(base + sub, sub), k + 1, g_other, q_other)
                kept = states_s[pl.ds(pl.multiple_of((origin + base + 1) * states, states), sub * states), :]
                bc_s[k] = diagonal(nt(kept, bs_s[pl.ds(base, sub), :].astype(BF16)))
                ct = turned_s[k]
                for t in range(sub - 1, -1, -1):
                    dl = delta_s[pl.ds(origin + base + t, 1), :]
                    bs = bs_s[pl.ds(base + t, 1), :]
                    g = bs * ct[:, t : t + 1] + h
                    h = g * jnp.exp2(dl * rate)
                    before = states_s[pl.ds(pl.multiple_of((origin + base + t) * states, states), states), :]
                    g_mine[t * states : (t + 1) * states, :] = g.astype(BF16)
                    q_mine[t * states : (t + 1) * states, :] = h.astype(BF16) * (decay * before)
            return h

        carry[...] = lax.fori_loop(0, pairs, pair, carry[...])
        sums(0, 0, held_a, q_a)
        w = w_s[:rows, :]
        conv_ref[...] = w * delta_s[here, :] + skip_ref[...] * bs_s[...]
        back_delta = bd_s[:rows, :] + w * u_ref[...].astype(F32)
        back_pre = (back_delta * jax.nn.sigmoid(pre_s[here, :])).astype(BF16)
        pre_ref[...] = back_pre
        gated_low = nt(down_ref[0], gated_block(scanned_s[here, :], z))
        mixed = [nt(step_proj_ref[...], back_pre), nt(step_up_ref[0], back_pre)]
        mixed += [jnp.concatenate([ref[k] for k in range(rows // sub)], 1) for ref in (bb_s, bc_s)]
        mixed = jnp.concatenate(mixed + [gated_low], 0).astype(BF16)
        for j in range(per):
            mixed_ref[j] = mixed[:, j * tokens : (j + 1) * tokens]


def gated_block(scanned, z):
    return (scanned * jax.nn.silu(z)).astype(BF16)


def scan(meta, shared, u, z, bg, step_proj, step_up, bias, rate, decay, skip, out_down, parts, sub):
    length, chans = u.shape
    tokens = length // parts
    block = 2 * tokens
    blocks = length // block
    states, rank, ranks = rate.shape[0], step_up.shape[1], step_proj.shape[0]
    cols = ranks + 2 * rank + 2 * states
    mirrored = lambda i: jnp.where(i < blocks, i, 2 * blocks - 1 - i)
    back = lambda i: jnp.where(i < blocks, blocks - 1, 2 * blocks - 1 - i)
    both = pl.BlockSpec((block, chans), lambda i, meta: (mirrored(i), 0))
    first = pl.BlockSpec((block, chans), lambda i, meta: (jnp.minimum(i, blocks - 1), 0))
    second = pl.BlockSpec((block, chans), lambda i, meta: (back(i), 0))
    return pl.pallas_call(
        functools.partial(scan_kernel, sub=sub, ranks=ranks),
        grid_spec=pltpu.PrefetchScalarGridSpec(
            num_scalar_prefetch=1,
            grid=(2 * blocks,),
            in_specs=[
                once(shared), both, both, second, once(step_proj), chosen(step_up), once(bias), once(rate), once(decay),
                once(skip), chosen(out_down, 0, chans),
            ],
            out_specs=[
                first, second, second, second,
                pl.BlockSpec((2, cols, tokens), lambda i, meta: (back(i), 0, 0)),
            ],
            scratch_shapes=[
                pltpu.VMEM((states, chans), F32),
                pltpu.VMEM(((length + 1) * states, chans), BF16),
                pltpu.VMEM((length, chans), F32),
                pltpu.VMEM((length, chans), F32),
                pltpu.VMEM((length + sub, chans), F32),
                pltpu.VMEM((length, chans), F32),
                pltpu.VMEM((block, chans), F32),
                pltpu.VMEM((block + sub, sub * states), BF16),
                pltpu.VMEM((block + sub, chans), F32),
                pltpu.VMEM((block + sub, chans), F32),
                pltpu.VMEM((block // sub + 1, states, sub), F32),
                pltpu.VMEM((block // sub, states, sub), F32),
                pltpu.VMEM((block // sub, states, sub), F32),
                pltpu.VMEM((sub * states, chans), BF16),
                pltpu.VMEM((sub * states, chans), BF16),
                pltpu.VMEM((sub * states, chans), BF16),
                pltpu.VMEM((sub * states, chans), BF16),
            ],
        ),
        out_shape=[
            jax.ShapeDtypeStruct((length, chans), BF16),
            jax.ShapeDtypeStruct((length, chans), BF16),
            jax.ShapeDtypeStruct((length, chans), F32),
            jax.ShapeDtypeStruct((length, chans), BF16),
            jax.ShapeDtypeStruct((parts, cols, tokens), BF16),
        ],
        compiler_params=pltpu.CompilerParams(vmem_limit_bytes=LIMIT),
        name="scan",
    )(meta, shared, u, z, bg, step_proj, step_up, bias, rate, decay, skip, out_down)


def finish_kernel(
    meta, *refs, ranks, states, parts, groups,
):
    pieces, refs = refs[: parts + 1], refs[parts + 1 :]
    columns_x, columns_z, refs = refs[:groups], refs[groups], refs[groups + 1 :]
    (back_ref, shared_ref, conv_grad_ref, back_z_ref, back_pre_ref, x_ref, x_before_ref, u_ref, low_in_ref,
     gated_ref, back_low_ref, cols_ref, up_x_ref, up_z_ref, proj_ref, down_ref,
     state_up_ref, in_down_ref, weight_ref, bias_ref,
     parts_ref, wide_ref, local_ref,
     after, sums_s, down_s, local_s, rows_s, whole_x, whole_z, piece_sems, x_sems, z_sems) = refs
    copies = (
        ring_copies(rows_s, pieces, meta[1], piece_sems)
        + row_copies(whole_x, columns_x, meta[2], x_sems)
        + row_copies(whole_z, columns_z, None, z_sems)
    )
    step = pl.program_id(0)
    steps = pl.num_programs(0)
    rows, chans = u_ref.shape
    rank = state_up_ref.shape[1]
    taps = weight_ref.shape[0]
    mixes = ranks + 2 * states

    @pl.when(step == 0)
    def _():
        for copy in copies:
            copy.start()
        after[...] = jnp.zeros_like(after)
        sums_s[...] = jnp.zeros_like(sums_s)
        down_s[...] = jnp.zeros_like(down_s)
        local_s[...] = jnp.zeros_like(local_s)

    per = rows // back_ref.shape[1]
    places = [place_of_block((steps - 1 - step) * per + j, meta[1], parts) for j in range(per)]
    back = jnp.concatenate([back_ref[place] for place in places], 0)
    shared = jnp.concatenate([shared_ref[place] for place in places], 0)
    u = u_ref[...]
    mixed = back[:, :mixes]
    back_low_state = nt(mixed, state_up_ref[0]).astype(BF16)
    grad = conv_grad_ref[...] + nn(mixed, proj_ref[...]) + nn(back_low_state, down_ref[0])
    keep = jnp.where(step == steps - 1, 0.0, 1.0)
    conv_pre = conv_before(x_ref[...].astype(F32), x_before_ref[...].astype(F32) * keep, weight_ref, bias_ref)
    grad = grad * silu_grad(conv_pre)
    padded = jnp.concatenate([grad, after[...]], 0)
    back_x = weight_ref[taps - 1 : taps, :] * grad
    for tap in range(taps - 1):
        at = taps - 1 - tap
        back_x = back_x + weight_ref[tap : tap + 1, :] * padded[at : at + rows]
    after[...] = grad[:8]
    back_x, back_z = back_x.astype(BF16), back_z_ref[...]

    @pl.when(step == 0)
    def _():
        for copy in copies:
            copy.wait()

    normed = rows_s[pl.ds(pl.multiple_of((steps - 1 - step) * rows, rows), rows), :]
    back_low_in = (nt(back_x, up_x_ref[0]) + nt(back_z, up_z_ref[0])).astype(BF16)
    parts_ref[...] = (
        nt(back_x, flat(whole_x)) + nt(back_z, flat(whole_z)) + nn(back_low_in, in_down_ref[0])
    ).astype(BF16)
    down_s[...] += tn(back_low_in, normed)
    low_in = low_in_ref[...]
    sums_s[:, :chans] += tn(low_in, back_x)
    sums_s[:, chans : 2 * chans] += tn(low_in, back_z)
    sums_s[:, 2 * chans : 3 * chans] += tn(back_low_ref[...], gated_ref[...])
    sums_s[:, 3 * chans :] += tn(back[:, mixes + rank :], cols_ref[...])
    local_s[:, :chans] += tn(back_low_state, u)
    local_s[:, chans : 2 * chans] += tn(shared[:, ranks : ranks + rank], back_pre_ref[...])
    local_s[:, 2 * chans : 2 * chans + ranks] += tn(back[:, mixes : mixes + rank], shared[:, :ranks])
    at = 2 * chans + ranks
    local_s[:, at : at + mixes] += tn(shared[:, ranks + rank + 2 * states :], mixed)

    @pl.when(step == steps - 1)
    def _():
        for values, ref, first in (
            (sums_s, wide_ref, 0), (down_s, wide_ref, sums_s.shape[1] // 128), (local_s, local_ref, 0)
        ):
            for j in range(values.shape[1] // 128):
                ref[first + j] = values[:, j * 128 : (j + 1) * 128].astype(BF16)
        lane = lax.broadcasted_iota(jnp.int32, (rank, 128), 1)
        local_ref[local_ref.shape[0] - 1] = (lane == meta[0]).astype(BF16)


def finish(
    meta, pieces, columns_x, columns_z, back, shared, conv_grad, back_z, back_pre, x, u, low_in, gated, back_low, cols, up,
    proj, down, state_up, in_down, weight, bias, parts, groups, states,
):
    length, chans = u.shape
    block, rank, span = AT_ONCE * length // parts, low_in.shape[1], cols.shape[1]
    mixes = proj.shape[0]
    ranks = mixes - 2 * states
    width = pieces[0].shape[1]
    whole_shape = (parts, groups) + columns_x[0].shape[1:]
    end = length // block - 1
    seq = lambda size: pl.BlockSpec((block, size), lambda i, meta: (end - i, 0))
    wide = 3 * chans + span
    local = 2 * chans + ranks + 2 * 128
    chunks = ((wide + width) // 128, local // 128 + 1)
    fixed = lambda count: pl.BlockSpec((count, rank, 128), lambda i, meta: (0, 0, 0))
    return pl.pallas_call(
        functools.partial(finish_kernel, ranks=ranks, states=states, parts=parts, groups=groups),
        grid_spec=pltpu.PrefetchScalarGridSpec(
            num_scalar_prefetch=1,
            grid=(length // block,),
            in_specs=[pl.BlockSpec(memory_space=pl.ANY)] * (len(pieces) + groups + 1)
            + [
                once(back), once(shared), seq(chans), seq(chans), seq(chans), seq(chans),
                pl.BlockSpec((16, chans), lambda i, meta: (jnp.maximum((end - i) * (block // 16) - 1, 0), 0)),
                seq(chans), seq(rank), seq(chans), seq(rank), seq(span),
                chosen(up, 0, chans), chosen(up, parts, chans), once(proj), chosen(down), chosen(state_up),
                chosen(in_down), once(weight), once(bias),
            ],
            out_specs=[seq(width)] + [fixed(count) for count in chunks],
            scratch_shapes=[
                pltpu.VMEM((8, chans), F32), pltpu.VMEM((rank, wide), F32), pltpu.VMEM((rank, width), F32),
                pltpu.VMEM((rank, local), F32), pltpu.VMEM((length, width), BF16),
                pltpu.VMEM(whole_shape, BF16), pltpu.VMEM(whole_shape, BF16),
                pltpu.SemaphoreType.DMA((len(pieces),)), pltpu.SemaphoreType.DMA((groups,)),
                pltpu.SemaphoreType.DMA((groups,)),
            ],
        ),
        out_shape=[
            jax.ShapeDtypeStruct((length, width), BF16),
        ]
        + [jax.ShapeDtypeStruct((count, rank, 128), BF16) for count in chunks],
        compiler_params=pltpu.CompilerParams(vmem_limit_bytes=LIMIT),
        name="finish",
    )(
        meta, *pieces, *columns_x, columns_z, back, shared, conv_grad, back_z, back_pre, x, x, u, low_in, gated, back_low,
        cols, up, up, proj, down, state_up, in_down, weight, bias,
    )


def place_kernel(meta, *refs, groups, parts, chans, span, every, wide):
    values, outs = refs[:groups], refs[groups:]
    in_up_ref, out_down_ref, out_up_ref, in_down_ref, state_down_ref, step_up_ref, step_down_ref, state_up_ref = outs
    per = in_up_ref.shape[0]
    first = pl.program_id(0) * per

    def put(ref, column, at, size=128):
        terms = [value[at].astype(F32) for value in values]
        for i in range(per):
            total = None
            for g, term in enumerate(terms):
                term = jnp.where(meta[3 + g] == first + i, term, 0.0)
                total = term if total is None else total + term
            ref[i, :, column : column + size] = total[:, :size]

    inner = parts * chans
    for p in range(parts):
        at = place_of_block(p, meta[1], parts) * wide
        for j in range(chans // 128):
            put(in_up_ref, p * chans + j * 128, at + j)
            put(in_up_ref, inner + p * chans + j * 128, at + chans // 128 + j)
            put(out_down_ref, p * chans + j * 128, at + 2 * (chans // 128) + j)
        if p % every == 0:
            for j in range(span // 128):
                put(out_up_ref, p // every * span + j * 128, at + 3 * (chans // 128) + j)
    at = parts * wide
    for ref in (in_down_ref, state_down_ref, step_up_ref, step_down_ref, state_up_ref):
        for j in range(pl.cdiv(ref.shape[2], 128)):
            put(ref, j * 128, at, min(128, ref.shape[2] - j * 128))
            at += 1


def place(meta, values, adapters, parts, chans, span, width, wide, ranks, mixes):
    groups, rank = len(values), values[0].shape[1]
    every = max(span * parts // width, 1)
    sizes = (2 * parts * chans, parts * chans, width, width, chans, chans, ranks, mixes)
    return pl.pallas_call(
        functools.partial(place_kernel, groups=groups, parts=parts, chans=chans, span=span, every=every, wide=wide),
        grid_spec=pltpu.PrefetchScalarGridSpec(
            num_scalar_prefetch=1,
            grid=(adapters // 4,),
            in_specs=[once(value) for value in values],
            out_specs=[pl.BlockSpec((4, rank, size), lambda i, meta: (i, 0, 0)) for size in sizes],
        ),
        out_shape=[jax.ShapeDtypeStruct((adapters, rank, size), F32) for size in sizes],
        compiler_params=pltpu.CompilerParams(vmem_limit_bytes=32 << 20),
        name="place",
    )(meta, *values)


def split_kernel(values_ref, out_ref):
    chans = out_ref.shape[2]
    for i in range(out_ref.shape[0]):
        out_ref[i] = values_ref[:, i * chans : (i + 1) * chans]


def split_columns(values, parts):
    rows, cols = values.shape
    return pl.pallas_call(
        split_kernel, out_shape=jax.ShapeDtypeStruct((parts, rows, cols // parts), values.dtype), name="split_columns"
    )(values)


EPS = 1e-05


def ring_send(value, size, hop, axis):
    order = list(range(0, size, 2)) + list(range(1, size, 2))[::-1]
    pairs = [(order[i], order[(i + hop) % size]) for i in range(size)]
    return lax.ppermute(value, axis, pairs)


class RingGather:
    def __init__(self, own, size, axis):
        self.size, self.axis, self.rows, self.done = size, axis, own.shape[0], 0
        self.pieces = [own]
        self.ends = (own, own)

    def advance(self, hops):
        far, half = self.size // 2, self.rows // 2
        for _ in range(min(hops, far - self.done)):
            self.done += 1
            ahead, back = self.ends
            if self.done == far:
                ahead, back = ahead[:half], back[half:]
            self.ends = (ring_send(ahead, self.size, 1, self.axis), ring_send(back, self.size, -1, self.axis))
            self.pieces += list(self.ends)

    def all_pieces(self):
        self.advance(self.size)
        return self.pieces


class RingScatter:
    def __init__(self, partial, size, axis):
        self.partial, self.size, self.axis, self.done = partial, size, axis, 0
        self.rows = partial.shape[0] // size
        self.position = ring_position(lax.axis_index(axis), size)
        self.ends = None

    def block(self, offset, start=0, rows=None):
        at = ring_place(self.position + offset, self.size) * self.rows + start
        return lax.dynamic_slice_in_dim(self.partial, at, rows or self.rows, 0)

    def advance(self, hops):
        far, half = self.size // 2, self.rows // 2
        for _ in range(min(hops, far - self.done)):
            left = far - self.done
            if left == far:
                mine, other = self.block(far, 0, half), self.block(far, half, half)
            else:
                mine, other = self.block(left).astype(F32), self.block(-left).astype(F32)
                ahead, back = (end.astype(F32) for end in self.ends)
                if left == far - 1:
                    blank = jnp.zeros_like(ahead)
                    ahead, back = jnp.concatenate([ahead, blank], 0), jnp.concatenate([blank, back], 0)
                mine, other = (mine + ahead).astype(BF16), (other + back).astype(BF16)
            self.ends = (
                ring_send(mine, self.size, 1, self.axis),
                ring_send(other, self.size, -1, self.axis),
            )
            self.done += 1

    def total(self):
        self.advance(self.size)
        return self.block(0).astype(F32) + self.ends[0].astype(F32) + self.ends[1].astype(F32)


def together(*values):
    return lax.optimization_barrier(values)


def swap(value, size, bit, axis):
    return lax.ppermute(value, axis, [(i, i ^ bit) for i in range(size)])


def bits_of(size):
    bit = size // 2
    while bit:
        yield bit
        bit //= 2


def swap_gather(own, size, axis):
    held = [own]
    for bit in bits_of(size):
        held += [swap(block, size, bit, axis) for block in held]
    return held


def small_gather(own, size, axis):
    held = own[None]
    for bit in bits_of(size):
        held = jnp.concatenate([held, swap(held, size, bit, axis)], 0)
    return held


def exchange(values, axis):
    return lax.all_to_all(values, axis, split_axis=0, concat_axis=0, tiled=True)


def body(
    hidden, lengths, adapter_ids, norm_gain, in_proj_x, in_proj_z, conv_weight, conv_bias, state_proj,
    step_proj, step_bias, decay_log, skip_gain, out_proj, in_down, in_up, state_down, state_up, step_down,
    step_up, out_down, out_up, cotangent,
):
    parts, groups = lax.axis_size("seq"), lax.axis_size("fsdp")
    part, group = lax.axis_index("seq"), lax.axis_index("fsdp")
    tokens, width = hidden.shape[1:]
    chans = conv_weight.shape[1]
    ranks = step_proj.shape[0]
    states = decay_log.shape[0]
    rank = in_down.shape[2]
    adapters = in_down.shape[0]
    ident = adapter_ids[0]
    sub = 16
    meta = jnp.stack([ident, part, group]).astype(jnp.int32)
    in_down, state_down, step_down, out_down = (
        table.transpose(0, 2, 1) for table in (in_down, state_down, step_down, out_down)
    )
    state_proj = state_proj.T

    hidden_f = hidden[0].astype(F32)
    gain_f = norm_gain.astype(F32)
    normed, inverse = normalise(hidden, norm_gain[None])
    inverse = inverse[:, :1]
    positions = part * tokens + lax.broadcasted_iota(jnp.int32, (tokens, 1), 0)
    valid = (positions < lengths[0]).astype(F32)
    cot_f = cotangent[0].astype(F32)
    back_out = (valid * cot_f).astype(BF16)
    conv_weight, conv_bias = conv_weight.astype(F32), conv_bias.astype(F32)[None]
    bias, skip = step_bias.astype(F32)[None], skip_gain.astype(F32)[None]
    decay = -jnp.exp(decay_log.astype(F32))
    rate, decay = decay * LOG2E, decay.astype(BF16)
    rows = in_proj_x.shape[0]

    def own_columns_of(weight):
        return lax.all_to_all(weight, "seq", split_axis=0, concat_axis=0, tiled=True)

    hops = max(parts // 8, 1)
    whole_out = lax.all_gather(out_proj, "fsdp", axis=0, tiled=True)
    ring = RingGather(normed, parts, "seq")
    ring.advance(hops)
    mine_x = own_columns_of(split_columns(in_proj_x, parts))
    small = (conv_weight, conv_bias, bias, skip, rate, decay, meta, split_columns(in_proj_z, parts))
    ring.ends, small = together(ring.ends, small)
    conv_weight, conv_bias, bias, skip, rate, decay, meta, in_proj_z = small
    pieces = ring.all_pieces()
    columns = swap_gather(mine_x, groups, "fsdp")

    pieces, columns, back_out, in_proj_z = together(pieces, columns, back_out, in_proj_z)
    cot_ring = RingGather(back_out, parts, "seq")
    cot_ring.advance(hops)
    mine_z = own_columns_of(in_proj_z)
    low_in, x, conv_out, sums = project(
        meta, pieces, columns, in_down, in_up, conv_weight, conv_bias, state_proj, state_down, parts, groups
    )
    sums, mine_z = together(sums, mine_z)
    cot_ring.advance(hops)
    columns_z = lax.all_gather(mine_z, "fsdp")
    sums = exchange(sums, "seq")
    sums, cot_ring.ends = together(sums, cot_ring.ends)
    cot_ring.advance(hops)
    shared = share(meta, sums, state_up, step_down, ranks, states)[None]
    shared, columns_z = together(shared, columns_z)
    z = gate(meta, pieces, columns_z, low_in, in_up, parts, groups)
    for i, bit in enumerate(bits_of(parts)):
        shared = jnp.concatenate([shared, swap(shared, parts, bit, "seq")], 0)
        if i == 0:
            shared, cot_ring.ends, z = together(shared, cot_ring.ends, z)
            cot_ring.advance(parts)
    back = back_gate(meta, cot_ring.pieces, whole_out, out_down, out_up, parts)
    back_low, cols, back_gated = back
    gated, back_pre, conv_grad, back_z, mixed = scan(
        meta, shared, conv_out, z, back_gated, step_proj, step_up, bias, rate, decay, skip, out_down, parts, sub
    )
    out_ring = RingScatter(nn(gated, whole_out).astype(BF16), parts, "seq")
    out_ring.advance(hops)
    back_own = share_back(meta, exchange(mixed, "seq"), step_down, ranks, states)
    back = back_own[None]
    for i, bit in enumerate(bits_of(parts)):
        back = jnp.concatenate([back, swap(back, parts, bit, "seq")], 0)
        if i % 2 == 0:
            back, out_ring.ends = together(back, out_ring.ends)
            out_ring.advance(hops)
    in_parts, wide, local = finish(
        meta, pieces, columns, columns_z, back, shared, conv_grad, back_z, back_pre, x, conv_out, low_in, gated, back_low,
        cols, in_up, state_proj, state_down, state_up, in_down, conv_weight, conv_bias, parts, groups, states,
    )
    in_parts, wide, local, out_ring.ends = together(in_parts, wide, local, out_ring.ends)
    out_ring.advance(parts)
    in_ring = RingScatter(in_parts, parts, "seq")
    span = cols.shape[1]
    own = (3 * chans + span) // 128
    held, down_grad = wide[:own], wide[own:]
    for bit in bits_of(parts):
        in_ring.advance(hops)
        got = swap(jnp.concatenate([held, down_grad], 0), parts, bit, "seq")
        count = held.shape[0]
        held = jnp.concatenate([held, got[:count]], 0)
        down_grad = (down_grad.astype(F32) + got[count:].astype(F32)).astype(BF16)
        held, down_grad, in_ring.ends = together(held, down_grad, in_ring.ends)
    in_ring.advance(parts)
    chunks = [jnp.concatenate([held, down_grad, local], 0)]
    first, *others = bits_of(groups)
    chunks += [swap(chunks[0], groups, first, "fsdp")]
    branch = out_ring.total()
    chunks, in_ring.ends, branch = together(chunks, in_ring.ends, branch)
    for bit in others:
        chunks += [swap(block, groups, bit, "fsdp") for block in chunks]
    out_up_sel = lax.dynamic_index_in_dim(out_up, ident, 0, keepdims=False)
    block_out = (hidden_f + valid * (branch + nn(back_own[:, -rank:], out_up_sel))).astype(BF16)
    gained = in_ring.total() * gain_f
    input_grad = (
        cot_f
        + inverse * gained
        - hidden_f * inverse * inverse * inverse * jnp.mean(hidden_f * gained, axis=-1, keepdims=True)
    )

    lane = lax.broadcasted_iota(jnp.int32, (groups, adapters), 1)
    picks = jnp.stack([block[-1, 0, :adapters] for block in chunks]).astype(F32)
    idents = jnp.sum(picks * lane.astype(F32), axis=1).astype(jnp.int32)
    (in_up_grad, out_down_grad, out_up_grad, in_down_grad, state_down_grad, step_up_grad, step_down_grad,
     state_up_grad) = place(
        jnp.concatenate([meta, idents]), chunks, adapters, parts, chans, span, width, own, ranks, ranks + 2 * states
    )
    return (
        block_out[None], input_grad[None], in_down_grad.transpose(0, 2, 1), in_up_grad,
        state_down_grad.transpose(0, 2, 1), state_up_grad, step_down_grad.transpose(0, 2, 1), step_up_grad,
        out_down_grad.transpose(0, 2, 1), out_up_grad,
    )


def solution(mesh):
    seq, rows = P("fsdp", "seq", None), P(("seq", "fsdp"), None)
    in_specs = (
        seq, P("fsdp"), P("fsdp"), P(), rows, rows, P(None, "seq"), P("seq"), P("seq", None), P(None, "seq"),
        P("seq"), P(None, "seq"), P("seq"), rows, P(), P(), P(None, "seq", None), P(), P(), P(None, None, "seq"),
        P(), P(), seq,
    )
    out_specs = (seq, seq, P(), P(), P(None, "seq", None), P(), P(), P(None, None, "seq"), P(), P())
    return jax.shard_map(body, mesh=mesh, in_specs=in_specs, out_specs=out_specs, check_vma=False)
```
